32 devices in a mesh: replica: 8 (over z, x), group: 4 (over y, core).
Axes of the slice: x: 2, y: 2, z: 4, core: 2. Of those that a mesh axis runs over, the one named last changes fastest.
Arguments:
- images: bfloat16 [160, 197, 768], P(('replica', 'group')), may hold values from -6 to 6
- counts: int32 [32], P(('replica', 'group')), may hold values from 1 to 5, as said below
- ln1_gain: bfloat16 [768], P('group'), may hold values from 0.099609375 to 1.8984375
- ln1_shift: bfloat16 [768], P('group'), may hold values from -1.75 to 1.75
- w_qkv: bfloat16 [768, 2304], P('group'), may hold values from -0.21875 to 0.21875
- b_query: bfloat16 [768], P('group'), may hold values from -3 to 3
- b_value: bfloat16 [768], P('group'), may hold values from -3 to 3
- w_out: bfloat16 [768, 768], P('group'), may hold values from -1.75 to 1.75
- b_out: bfloat16 [768], P('group'), may hold values from -3 to 3
- ln2_gain: bfloat16 [768], P('group'), may hold values from 0.099609375 to 1.8984375
- ln2_shift: bfloat16 [768], P('group'), may hold values from -1.75 to 1.75
- w_up: bfloat16 [768, 3072], P('group'), may hold values from -0.21875 to 0.21875
- b_up: bfloat16 [3072], P('group'), may hold values from -3 to 3
- w_down: bfloat16 [3072, 768], P('group'), may hold values from -0.109375 to 0.109375
- b_down: bfloat16 [768], P('group'), may hold values from -3 to 3
- cotangent: bfloat16 [160, 197, 768], P(('replica', 'group')), may hold values from -6 to 6
Outputs:
- activations: bfloat16 [160, 197, 768], P(('replica', 'group'))
- input_grad: float32 [160, 197, 768], P(('replica', 'group'))
- grad_ln1_gain: float32 [768], P('group')
- grad_ln1_shift: float32 [768], P('group')
- grad_w_qkv: float32 [768, 2304], P('group')
- grad_b_query: float32 [768], P('group')
- grad_b_value: float32 [768], P('group')
- grad_w_out: float32 [768, 768], P('group')
- grad_b_out: float32 [768], P('group')
- grad_ln2_gain: float32 [768], P('group')
- grad_ln2_shift: float32 [768], P('group')
- grad_w_up: float32 [768, 3072], P('group')
- grad_b_up: float32 [3072], P('group')
- grad_w_down: float32 [3072, 768], P('group')
- grad_b_down: float32 [768], P('group')
The draws below stay inside these ranges and needn't reach their ends.
Inputs may be any that keep to these rules, and one draw needn't show every extreme that they name: counts[d] is the number of live image slots of device d, slots 0 to counts[d] - 1; some device has all 5 live in every draw.
All inputs are finite; a program needn't handle non-finite values.
Results may differ from the reference program's by a relative error of at most 0.015.
Values may be sent and summed in bfloat16 or wider, within the bound.
No kernel may reach another device: no remote copies, remote signals or barrier semaphores. Data moves between devices by JAX's collectives and lax.ppermute only.
A program may use at most 192 MiB of HBM per device.

```python
import jax
import jax.numpy as jnp
from jax import lax

D = 768
HEADS = 12
HEAD_DIM = 64
FF = 3072
SEQ = 197
SLOTS = 5
IMAGES = 160


def draw_counts(key, part):
    key = jax.random.fold_in(key, 7)
    first, second = jax.random.split(key)
    device_count = IMAGES // SLOTS
    drawn = jax.random.randint(first, (device_count,), 1, SLOTS + 1)
    where_full = jax.random.randint(second, (), 0, device_count)
    return jnp.where(jnp.arange(device_count) == where_full, SLOTS, drawn).astype(jnp.int32)


def steps_of(rng, dims, cuts, smallest, largest):
    loudness, own = 1.0, jax.random.fold_in(rng, 6)
    for axis_at, shards_of in cuts:
        steps = jnp.exp(jax.random.uniform(jax.random.fold_in(own, axis_at), (shards_of,), jnp.float32, smallest / len(cuts), largest / len(cuts)))
        loudness = loudness * jnp.repeat(steps, dims[axis_at] // shards_of).reshape([-1 if axis == axis_at else 1 for axis in range(len(dims))])
    return loudness


def noise(own_key, shape, deviation, limit, shards=(), kind=jnp.bfloat16):
    loudness = steps_of(own_key, shape, shards, -0.22, 0.18) if shards else 1.0
    values = jax.random.normal(own_key, shape, jnp.float32) * deviation * loudness
    return jnp.minimum(jnp.maximum(values, -limit), limit).astype(kind)


def setup_inputs(seed: int = 0) -> dict:
    key_of = jax.random.split(jax.random.key(seed), 17)
    return {
        "images": noise(key_of[0], (IMAGES, SEQ, D), 1.0, 6.0, ((0, 32),)),
        "counts": draw_counts(jax.random.fold_in(key_of[16], 71), 0),
        "ln1_gain": jnp.clip(1.0 + 0.18 * jax.random.normal(key_of[2], (D,), jnp.float32), 0.099609375, 1.8984375).astype(jnp.bfloat16),
        "ln1_shift": noise(key_of[3], (D,), 0.3, 1.75, ((0, 4),)),
        "w_qkv": noise(key_of[4], (D, 3 * D), D ** -0.5, 0.21875, ((0, 4),)),
        "b_query": noise(key_of[5], (D,), 0.5, 3.0, ((0, 4),)),
        "b_value": noise(key_of[6], (D,), 0.5, 3.0, ((0, 4),)),
        "w_out": noise(key_of[7], (D, D), (D // 64) ** -0.5, 1.75, ((0, 4),)),
        "b_out": noise(key_of[8], (D,), 0.5, 3.0, ((0, 4),)),
        "ln2_gain": jnp.clip(1.0 + 0.18 * jax.random.normal(key_of[9], (D,), jnp.float32), 0.099609375, 1.8984375).astype(jnp.bfloat16),
        "ln2_shift": noise(key_of[10], (D,), 0.3, 1.75, ((0, 4),)),
        "w_up": noise(key_of[11], (D, FF), D ** -0.5, 0.21875, ((0, 4),)),
        "b_up": noise(key_of[12], (FF,), 0.5, 3.0, ((0, 4),)),
        "w_down": noise(key_of[13], (FF, D), FF ** -0.5, 0.109375, ((0, 4),)),
        "b_down": noise(key_of[14], (D,), 0.5, 3.0, ((0, 4),)),
        "cotangent": noise(key_of[15], (IMAGES, SEQ, D), 1.0, 6.0, ((0, 32),)),
    }


@jax.custom_vjp
def low(v):
    return lax.optimization_barrier(v.astype(jnp.bfloat16)).astype(jnp.float32)

@jax.custom_vjp
def low_back(v):
    return v

def low_keep(v):
    return (low(v), None)

def low_pass(kept, grad):
    return (grad,)

def back_keep(v):
    return (v, None)

def back_low(kept, grad):
    return (low(grad),)
low.defvjp(low_keep, low_pass)
low_back.defvjp(back_keep, back_low)

def layer_norm(field, gain, shift):
    centred = field - lax.optimization_barrier(jnp.mean(field, -1, keepdims=True))
    spread = lax.optimization_barrier(jnp.mean(centred * centred, -1, keepdims=True))
    return centred * lax.rsqrt(spread + 1e-06) * gain + shift

def matmul(form, left, right):
    return jnp.einsum(form, left, right, precision=lax.Precision.HIGHEST)

def block(field, live, params):
    gain_one, shift_one, proj_qkv, bias_query, bias_value, proj_out, bias_out, gain_two, shift_two, proj_up, bias_up, proj_down, bias_down = params
    slot_count = field.shape[0]
    low_one = low(layer_norm(field, gain_one, shift_one))
    bias_cat = jnp.concatenate([bias_query, jnp.zeros_like(bias_query), bias_value])
    packed = low(low_back(matmul('bsd,de->bse', low_one, proj_qkv) + bias_cat))
    query = packed[..., :D].reshape(slot_count, SEQ, HEADS, HEAD_DIM)
    keys_all = packed[..., D:2 * D].reshape(slot_count, SEQ, HEADS, HEAD_DIM)
    values_all = packed[..., 2 * D:].reshape(slot_count, SEQ, HEADS, HEAD_DIM)
    scores = low_back(matmul('bqhe,bkhe->bhqk', query, keys_all)) * HEAD_DIM ** (-0.5)
    probs = low(jax.nn.softmax(scores, axis=-1))
    attended = matmul('bhqk,bkhe->bqhe', probs, values_all).reshape(slot_count, SEQ, D)
    attended = low(low_back(attended))
    middle = field + low_back(matmul('bsd,de->bse', attended, proj_out) + bias_out)
    low_two = low(layer_norm(middle, gain_two, shift_two))
    hidden_pre = low_back(matmul('bsd,df->bsf', low_two, proj_up) + bias_up)
    hidden_low = low(jax.nn.gelu(hidden_pre, approximate=True))
    branch_two = low_back(matmul('bsf,fd->bsd', hidden_low, proj_down) + bias_down)
    return (middle + branch_two) * live[:, None, None]

def reference(images, counts, ln1_gain, ln1_shift, w_qkv, b_query, b_value, w_out, b_out, ln2_gain, ln2_shift, w_up, b_up, w_down, b_down, cotangent):
    device_count = IMAGES // SLOTS
    params = tuple((p.astype(jnp.float32) for p in (ln1_gain, ln1_shift, w_qkv, b_query, b_value, w_out, b_out, ln2_gain, ln2_shift, w_up, b_up, w_down, b_down)))
    live = (jnp.arange(SLOTS, dtype=jnp.int32)[None, :] < counts[:, None]).astype(jnp.float32)
    field = images.astype(jnp.float32).reshape(device_count, SLOTS, SEQ, D)
    checked = jax.checkpoint(block)

    def forward(inputs, weights):
        return lax.map(lambda pair: checked(pair[0], pair[1], weights), (inputs, live))
    result, pull = jax.vjp(forward, field, params)
    input_grad, grads = pull(cotangent.astype(jnp.float32).reshape(device_count, SLOTS, SEQ, D))
    return (result.reshape(IMAGES, SEQ, D).astype(jnp.bfloat16), input_grad.reshape(IMAGES, SEQ, D), grads[0], grads[1], grads[2], grads[3], grads[4], grads[5], grads[6], grads[7], grads[8], grads[9], grads[10], grads[11], grads[12])
```

```python
import functools

import jax
import jax.numpy as jnp
from jax import lax
from jax.sharding import PartitionSpec as P

HEADS = 12


def layer_norm(field, gain, shift):
    centred = field - jnp.mean(field, -1, keepdims=True)
    spread = jnp.mean(centred * centred, -1, keepdims=True)
    return centred * lax.rsqrt(spread + 1e-06) * gain + shift


def smooth(field):
    return jax.nn.gelu(field, approximate=True)


def swap(field, axis, size, bit):
    return lax.ppermute(field, axis, [(at, at ^ bit) for at in range(size)])


def is_power(size):
    return size & (size - 1) == 0


def pick(field, at, axis):
    return lax.dynamic_index_in_dim(field, at, axis, keepdims=False)


def gather_shards(shard, sizes):
    groups, replicas = sizes
    rows = shard.shape[0]
    if groups != 4 or replicas % 2 or rows % 32:
        return lax.all_gather(shard, "group", axis=0, tiled=True)
    me = lax.axis_index("group")
    half = lax.axis_index("replica") & 1
    near = swap(shard, "group", 4, 1)
    first = swap(pick(shard.reshape(2, rows // 2, -1), half, 0), "group", 4, 2)
    second = swap(first, "replica", replicas, 1)
    far_first = swap(first, "group", 4, 1)
    far_second = swap(second, "group", 4, 1)
    whole = jnp.zeros((4 * rows, shard.shape[1]), shard.dtype)

    def put(whole, part, owner, at):
        return lax.dynamic_update_slice(whole, part, (owner * rows + at * (rows // 2), 0))

    whole = put(whole, shard, me, 0)
    whole = put(whole, near, me ^ 1, 0)
    whole = put(whole, first, me ^ 2, half)
    whole = put(whole, second, me ^ 2, 1 - half)
    whole = put(whole, far_first, me ^ 3, half)
    return put(whole, far_second, me ^ 3, 1 - half)


def add_low(left, right, kind):
    return (left.astype(jnp.float32) + right.astype(jnp.float32)).astype(kind)


def reduce_shards(grad, sizes, halvings):
    groups, replicas = sizes
    rows = grad.shape[0] // groups
    kind = grad.dtype
    if not (is_power(groups) and is_power(replicas)):
        shard = lax.psum_scatter(grad, "group", scatter_dimension=0, tiled=True)
        return lax.psum(shard.astype(jnp.float32), "replica")
    me = lax.axis_index("group")
    other = lax.axis_index("replica")
    tail = grad.shape[1:]
    field = grad.reshape((groups, rows) + tail)
    bit = 1
    while bit < groups:
        side = (me // bit) & 1
        pairs = field.reshape((field.shape[0] // 2, 2, rows) + tail)
        came = swap(pick(pairs, 1 - side, 1), "group", groups, bit)
        field = add_low(pick(pairs, side, 1), came, kind)
        bit *= 2
    field = field[0]
    done = []
    bit = 1
    while bit < replicas:
        side = (other // bit) & 1
        if len(done) < halvings:
            pairs = field.reshape((2, field.shape[0] // 2) + tail)
            came = swap(pick(pairs, 1 - side, 0), "replica", replicas, bit)
            field = add_low(pick(pairs, side, 0), came, kind)
            done.append((bit, side))
        else:
            field = add_low(field, swap(field, "replica", replicas, bit), kind)
        bit *= 2
    for bit, side in reversed(done):
        came = swap(field, "replica", replicas, bit)
        field = jnp.where(
            side == 0, jnp.concatenate([field, came]), jnp.concatenate([came, field])
        )
    return field.astype(jnp.float32)


def on_device(
    sizes,
    images,
    counts,
    ln1_gain,
    ln1_shift,
    w_qkv,
    b_query,
    b_value,
    w_out,
    b_out,
    ln2_gain,
    ln2_shift,
    w_up,
    b_up,
    w_down,
    b_down,
    cotangent,
):
    f32 = jnp.float32
    bf16 = jnp.bfloat16
    vectors = (ln1_gain, ln1_shift, b_query, b_value, b_out, ln2_gain, ln2_shift, b_down, b_up)
    row = jnp.concatenate(vectors)
    rows = lax.all_gather(row, "group", axis=0, tiled=False)
    ends = [0]
    for vector in vectors:
        ends.append(ends[-1] + vector.shape[0])
    small = [rows[:, at:end].reshape(-1) for at, end in zip(ends, ends[1:])]
    w_qkv = gather_shards(w_qkv, sizes)
    w_out = gather_shards(w_out, sizes)
    w_up = gather_shards(w_up, sizes)
    w_down = gather_shards(w_down, sizes)
    weights = (
        small[0],
        small[1],
        w_qkv,
        small[2],
        small[3],
        w_out,
        small[4],
        small[5],
        small[6],
        w_up,
        small[8],
        w_down,
        small[7],
    )
    slot_count, length, width = images.shape
    head_count = HEADS
    head_size = width // head_count
    factor = head_size ** (-0.5)
    live = (jnp.arange(slot_count, dtype=jnp.int32) < counts[0]).astype(f32)[:, None, None]
    inputs = images.astype(f32)
    gain_one = weights[0].astype(f32)
    shift_one = weights[1].astype(f32)
    gain_two = weights[7].astype(f32)
    shift_two = weights[8].astype(f32)
    normed_one, pull_one = jax.vjp(layer_norm, inputs, gain_one, shift_one)
    low_one = normed_one.astype(bf16)
    bias_cat = jnp.concatenate([weights[3], jnp.zeros_like(weights[3]), weights[4]]).astype(f32)
    packed = (
        jnp.einsum("bsd,de->bse", low_one, weights[2], preferred_element_type=f32) + bias_cat
    ).astype(bf16)
    query = packed[..., :width].reshape(slot_count, length, head_count, head_size)
    keys_low = packed[..., width : 2 * width].reshape(slot_count, length, head_count, head_size)
    values_low = packed[..., 2 * width :].reshape(slot_count, length, head_count, head_size)
    scores = jnp.einsum("bqhe,bkhe->bhqk", query, keys_low, preferred_element_type=f32) * factor
    top = jnp.max(scores, -1, keepdims=True)
    expo = jnp.exp(scores - top)
    total = jnp.sum(expo, -1, keepdims=True)
    log_total = top + jnp.log(total)
    probs_low = (expo / total).astype(bf16)
    attended = jnp.einsum("bhqk,bkhe->bqhe", probs_low, values_low, preferred_element_type=f32)
    attended = attended.reshape(slot_count, length, width).astype(bf16)
    middle = (
        inputs
        + jnp.einsum("bsd,de->bse", attended, weights[5], preferred_element_type=f32)
        + weights[6].astype(f32)
    )
    normed_two, pull_two = jax.vjp(layer_norm, middle, gain_two, shift_two)
    low_two = normed_two.astype(bf16)
    hidden_pre = jnp.einsum(
        "bsd,df->bsf", low_two, weights[9], preferred_element_type=f32
    ) + weights[10].astype(f32)
    hidden_act, pull_act = jax.vjp(smooth, hidden_pre)
    hidden_low = hidden_act.astype(bf16)
    branch_two = jnp.einsum(
        "bsf,fd->bsd", hidden_low, weights[11], preferred_element_type=f32
    ) + weights[12].astype(f32)
    outputs = ((middle + branch_two) * live).astype(bf16)
    proj_qkv, proj_out, proj_up, proj_down = (w_qkv, w_out, w_up, w_down)
    grad_out = cotangent.astype(f32) * live
    grad_low = grad_out.astype(bf16)
    grad_down = jnp.einsum("bsf,bsd->fd", hidden_low, grad_low, preferred_element_type=f32)
    grad_bdown = jnp.sum(grad_low.astype(f32), (0, 1))
    grad_hidden = jnp.einsum("bsd,fd->bsf", grad_low, proj_down, preferred_element_type=f32)
    grad_pre = pull_act(grad_hidden)[0].astype(bf16)
    grad_up = jnp.einsum("bsd,bsf->df", low_two, grad_pre, preferred_element_type=f32)
    grad_bup = jnp.sum(grad_pre.astype(f32), (0, 1))
    grad_normed = jnp.einsum("bsf,df->bsd", grad_pre, proj_up, preferred_element_type=f32)
    grad_mid_norm, grad_gain_two, grad_shift_two = pull_two(grad_normed)
    grad_middle = grad_out + grad_mid_norm
    grad_branch = grad_middle.astype(bf16)
    grad_proj_out = jnp.einsum("bsd,bse->de", attended, grad_branch, preferred_element_type=f32)
    grad_bout = jnp.sum(grad_branch.astype(f32), (0, 1))
    grad_att = jnp.einsum("bse,de->bsd", grad_branch, proj_out, preferred_element_type=f32).astype(
        bf16
    )
    grad_att = grad_att.reshape(slot_count, length, head_count, head_size)
    again_scores = (
        jnp.einsum("bqhe,bkhe->bhqk", query, keys_low, preferred_element_type=f32) * factor
    )
    again_probs = jnp.exp(again_scores - log_total)
    grad_value = jnp.einsum(
        "bhqk,bqhe->bkhe", again_probs.astype(bf16), grad_att, preferred_element_type=f32
    )
    grad_probs = jnp.einsum("bqhe,bkhe->bhqk", grad_att, values_low, preferred_element_type=f32)
    inner = jnp.sum(again_probs * grad_probs, -1, keepdims=True)
    grad_scores = (again_probs * (grad_probs - inner) * factor).astype(bf16)
    grad_query = jnp.einsum("bhqk,bkhe->bqhe", grad_scores, keys_low, preferred_element_type=f32)
    grad_key = jnp.einsum("bhqk,bqhe->bkhe", grad_scores, query, preferred_element_type=f32)
    grad_packed = jnp.concatenate(
        [
            grad_query.reshape(slot_count, length, width),
            grad_key.reshape(slot_count, length, width),
            grad_value.reshape(slot_count, length, width),
        ],
        -1,
    ).astype(bf16)
    grad_qkv = jnp.einsum("bsd,bse->de", low_one, grad_packed, preferred_element_type=f32)
    packed_sums = jnp.sum(grad_packed.astype(f32), (0, 1))
    grad_bquery = packed_sums[:width]
    grad_bvalue = packed_sums[2 * width :]
    grad_norm_one = jnp.einsum("bse,de->bsd", grad_packed, proj_qkv, preferred_element_type=f32)
    grad_in_norm, grad_gain_one, grad_shift_one = pull_one(grad_norm_one)
    input_grad = grad_middle + grad_in_norm
    big = [
        reduce_shards(grad.astype(bf16), sizes, 2)
        for grad in (grad_down, grad_up, grad_proj_out, grad_qkv)
    ]
    parts = (
        grad_gain_one,
        grad_shift_one,
        grad_bquery,
        grad_bvalue,
        grad_bout,
        grad_gain_two,
        grad_shift_two,
        grad_bdown,
        grad_bup,
    )
    joined = jnp.concatenate([part.reshape(sizes[0], -1) for part in parts], 1)
    little = reduce_shards(joined.reshape(sizes[0], -1, 128), sizes, 0).reshape(-1)
    sums = [little[at:end] for at, end in zip(ends, ends[1:])]
    summed = (
        sums[0],
        sums[1],
        big[3],
        sums[2],
        sums[3],
        big[2],
        sums[4],
        sums[5],
        sums[6],
        big[1],
        sums[8],
        big[0],
        sums[7],
    )
    return (
        outputs,
        input_grad,
        summed[0],
        summed[1],
        summed[2],
        summed[3],
        summed[4],
        summed[5],
        summed[6],
        summed[7],
        summed[8],
        summed[9],
        summed[10],
        summed[11],
        summed[12],
    )


def solution(mesh):
    sizes = (mesh.shape["group"], mesh.shape["replica"])
    return jax.shard_map(
        functools.partial(on_device, sizes),
        mesh=mesh,
        in_specs=(
            P(("replica", "group"), None, None),
            P(("replica", "group")),
            P("group"),
            P("group"),
            P("group", None),
            P("group"),
            P("group"),
            P("group", None),
            P("group"),
            P("group"),
            P("group"),
            P("group", None),
            P("group"),
            P("group", None),
            P("group"),
            P(("replica", "group"), None, None),
        ),
        out_specs=(
            P(("replica", "group"), None, None),
            P(("replica", "group"), None, None),
            P("group"),
            P("group"),
            P("group", None),
            P("group"),
            P("group"),
            P("group", None),
            P("group"),
            P("group"),
            P("group"),
            P("group", None),
            P("group"),
            P("group", None),
            P("group"),
        ),
        check_vma=False,
    )
```

```python
import functools

import jax
import jax.numpy as jnp
from jax import lax
from jax.experimental import pallas as pl
from jax.experimental.pallas import tpu as pltpu
from jax.sharding import PartitionSpec as P

HEADS = 12
F32 = jnp.float32
BF16 = jnp.bfloat16
GELU_A = 0.7978845608028654
GELU_B = 0.044715


def swap(field, axis, size, bit):
    return lax.ppermute(field, axis, [(at, at ^ bit) for at in range(size)])


def is_power(size):
    return size & (size - 1) == 0


def pick(field, at, axis):
    return lax.dynamic_index_in_dim(field, at, axis, keepdims=False)


def gather_pieces(shard, sizes):
    groups, replicas = sizes
    rows = shard.shape[0]
    if groups != 4 or replicas % 2 or rows % 32:
        return (lax.all_gather(shard, "group", axis=0, tiled=True),)
    half = lax.axis_index("replica") & 1
    first = swap(pick(shard.reshape(2, rows // 2, -1), half, 0), "group", 4, 2)
    near = swap(shard, "group", 4, 1)
    second = swap(first, "replica", replicas, 1)
    far_first = swap(first, "group", 4, 1)
    far_second = swap(second, "group", 4, 1)
    return (shard, near, first, second, far_first, far_second)


def place_pieces(rows, pieces, me, half):
    if pieces == 1:
        return [0]
    part = rows // 2
    return [
        me * rows,
        (me ^ 1) * rows,
        (me ^ 2) * rows + half * part,
        (me ^ 2) * rows + (1 - half) * part,
        (me ^ 3) * rows + half * part,
        (me ^ 3) * rows + (1 - half) * part,
    ]


def add_low(left, right, kind):
    return (left.astype(F32) + right.astype(F32)).astype(kind)


def reduce_shards(grad, sizes, halvings):
    groups, replicas = sizes
    rows = grad.shape[0] // groups
    kind = grad.dtype
    if not (is_power(groups) and is_power(replicas)):
        shard = lax.psum_scatter(grad, "group", scatter_dimension=0, tiled=True)
        return lax.psum(shard.astype(F32), "replica")
    me = lax.axis_index("group")
    other = lax.axis_index("replica")
    tail = grad.shape[1:]
    field = grad.reshape((groups, rows) + tail)
    bit = 1
    while bit < groups:
        side = (me // bit) & 1
        pairs = field.reshape((field.shape[0] // 2, 2, rows) + tail)
        came = swap(pick(pairs, 1 - side, 1), "group", groups, bit)
        field = add_low(pick(pairs, side, 1), came, kind)
        bit *= 2
    field = field[0]
    done = []
    bit = 1
    while bit < replicas:
        side = (other // bit) & 1
        if len(done) < halvings:
            pairs = field.reshape((2, field.shape[0] // 2) + tail)
            came = swap(pick(pairs, 1 - side, 0), "replica", replicas, bit)
            field = add_low(pick(pairs, side, 0), came, kind)
            done.append((bit, side))
        else:
            field = add_low(field, swap(field, "replica", replicas, bit), kind)
        bit *= 2
    for bit, side in reversed(done):
        came = swap(field, "replica", replicas, bit)
        field = jnp.where(
            side == 0, jnp.concatenate([field, came]), jnp.concatenate([came, field])
        )
    return field.astype(F32)


def dot(left, right):
    return lax.dot_general(left, right, (((1,), (0,)), ((), ())), preferred_element_type=F32)


def dot_nt(left, right):
    return lax.dot_general(left, right, (((1,), (1,)), ((), ())), preferred_element_type=F32)


def dot_tn(left, right):
    return lax.dot_general(left, right, (((0,), (0,)), ((), ())), preferred_element_type=F32)


def per_image(body, place, blocked, whole, weights, outs, sums, flops, after=()):
    slots = blocked[0].shape[0]
    counts = [len(pieces) for pieces in weights]
    rows_of = [pieces[0].shape[0] for pieces in weights]
    total = [rows * (4 if len(pieces) > 1 else 1) for rows, pieces in zip(rows_of, weights)]

    def kernel(*refs):
        refs = list(refs)

        def take(count):
            taken = refs[:count]
            del refs[:count]
            return taken

        (where,) = take(1)
        blocked_refs = take(len(blocked))
        whole_refs = take(len(whole))
        piece_refs = [take(count) for count in counts]
        take(len(after))
        out_refs = take(len(outs))
        sum_refs = take(len(sums))
        weight_refs = take(len(weights))
        at = pl.program_id(0)

        @pl.when(at == 0)
        def _():
            copies = []
            for index, pieces in enumerate(piece_refs):
                starts = place_pieces(rows_of[index], len(pieces), where[0], where[1])
                for spot, (piece, start) in enumerate(zip(pieces, starts)):
                    target = weight_refs[index].at[pl.ds(pl.multiple_of(start, 16), piece.shape[0])]
                    copies.append(pltpu.make_async_copy(piece, target, refs[0].at[index, spot]))
            for copy in copies:
                copy.start()
            for ref in sum_refs:
                ref[...] = jnp.zeros_like(ref)
            for copy in copies:
                copy.wait()

        body(at, where, blocked_refs, whole_refs, weight_refs, out_refs, sum_refs)

    in_specs = [pl.BlockSpec(memory_space=pltpu.SMEM)]
    for array in blocked:
        in_specs.append(pl.BlockSpec((1,) + array.shape[1:], lambda i: (i, 0, 0)))
    for array in whole:
        in_specs.append(pl.BlockSpec(array.shape, lambda i: (0, 0)))
    pieces = [piece for parts in weights for piece in parts]
    in_specs += [pl.BlockSpec(memory_space=pl.ANY)] * (len(pieces) + len(after))
    out_specs = [pl.BlockSpec((1, rows, columns), lambda i: (i, 0, 0)) for rows, columns, _ in outs]
    out_specs += [pl.BlockSpec((1, columns), lambda i: (0, 0)) for columns in sums]
    shapes = [jax.ShapeDtypeStruct((slots, rows, columns), kind) for rows, columns, kind in outs]
    shapes += [jax.ShapeDtypeStruct((1, columns), F32) for columns in sums]
    scratch = [
        pltpu.VMEM((rows, parts[0].shape[1]), BF16) for rows, parts in zip(total, weights)
    ]
    if weights:
        scratch.append(pltpu.SemaphoreType.DMA((len(weights), 6)))
    moved = sum(array.size * array.dtype.itemsize for array in list(blocked) + pieces)
    moved += sum(shape.size * shape.dtype.itemsize for shape in shapes)
    return pl.pallas_call(
        kernel,
        grid=(slots,),
        in_specs=in_specs,
        out_specs=out_specs,
        out_shape=shapes,
        scratch_shapes=scratch,
        compiler_params=pltpu.CompilerParams(
            dimension_semantics=("arbitrary",), vmem_limit_bytes=56 * 2**20
        ),
        cost_estimate=pl.CostEstimate(flops=flops, bytes_accessed=moved, transcendentals=0),
    )(place, *blocked, *whole, *pieces, *after)


def normed(field):
    centred = field - jnp.mean(field, -1, keepdims=True)
    scale = lax.rsqrt(jnp.mean(centred * centred, -1, keepdims=True) + 1e-06)
    return centred * scale, scale


def norm_back(grad, gain, hat, scale):
    inner = grad * gain
    mean = jnp.mean(inner, -1, keepdims=True)
    along = jnp.mean(inner * hat, -1, keepdims=True)
    return scale * (inner - mean - hat * along)


def column_sum(field):
    return jnp.sum(field.astype(F32), 0, keepdims=True)


def query_body(at, where, blocked, whole, weights, outs, sums):
    gain, shift, bias = whole
    hat, _ = normed(blocked[0][0].astype(F32))
    low = (hat * gain[...] + shift[...]).astype(BF16)
    outs[0][0] = low
    width = low.shape[1]
    for part in range(3):
        cut = slice(part * width, (part + 1) * width)
        outs[1][0, :, cut] = (dot(low, weights[0][:, cut]) + bias[:, cut]).astype(BF16)


def attend_body(length, at, where, blocked, whole, weights, outs, sums):
    packed, images = blocked
    bias, gain, shift = whole
    rows, width = images.shape[1:]
    lanes = 2 * width // HEADS
    factor = (width // HEADS) ** (-0.5)
    low_lane = lax.broadcasted_iota(jnp.int32, (rows, lanes), 1) < lanes // 2
    key_there = lax.broadcasted_iota(jnp.int32, (rows, rows), 1) < length
    for pair in range(HEADS // 2):
        start = pair * lanes
        query = packed[0, :, start : start + lanes] * jnp.asarray(factor, BF16)
        keys = packed[0, :, width + start : width + start + lanes]
        values = packed[0, :, 2 * width + start : 2 * width + start + lanes]
        both = []
        for side in range(2):
            mine = low_lane if side == 0 else jnp.logical_not(low_lane)
            scores = dot_nt(jnp.where(mine, query, jnp.zeros_like(query)), keys)
            scores = jnp.where(key_there, scores, -1e30)
            expo = jnp.exp(scores - jnp.max(scores, -1, keepdims=True))
            probs = expo * (1.0 / jnp.sum(expo, -1, keepdims=True))
            both.append(dot(probs.astype(BF16), values))
        outs[0][0, :, start : start + lanes] = jnp.where(low_lane, both[0], both[1]).astype(BF16)
    middle = images[0].astype(F32) + dot(outs[0][0], weights[0][...]) + bias[...]
    outs[1][0] = middle
    hat, _ = normed(middle)
    outs[2][0] = (hat * gain[...] + shift[...]).astype(BF16)


def up_body(at, where, blocked, whole, weights, outs, sums):
    low = blocked[0][0]
    inner = weights[0].shape[1]
    width = low.shape[1]
    for start in range(0, inner, width):
        cut = slice(start, start + width)
        pre = dot(low, weights[0][:, cut]) + whole[0][:, cut]
        square = pre * pre
        bend = jnp.tanh(pre * (GELU_A + (GELU_A * GELU_B) * square))
        half = 0.5 + 0.5 * bend
        outs[0][0, :, cut] = (pre * half).astype(BF16)
        slope = GELU_A + (3.0 * GELU_A * GELU_B) * square
        outs[1][0, :, cut] = (half + (0.5 * pre) * ((1.0 - bend * bend) * slope)).astype(BF16)


def back_body(at, where, blocked, whole, weights, outs, sums):
    cotangent, slope, middle = blocked
    (gain,) = whole
    w_down, w_up, w_out = weights
    grad_low = cotangent[0]
    width = grad_low.shape[1]
    inner = slope.shape[2]
    grad_two = None
    for start in range(0, inner, width):
        cut = slice(start, start + width)
        grad_pre = dot_nt(grad_low, w_down[cut, :]) * slope[0, :, cut].astype(F32)
        low = grad_pre.astype(BF16)
        outs[0][0, :, cut] = low
        sums[0][:, cut] += column_sum(low)
        part = dot_nt(low, w_up[:, cut])
        grad_two = part if grad_two is None else grad_two + part
    hat, scale = normed(middle[0])
    sums[1][...] += column_sum(grad_two * hat)
    sums[2][...] += column_sum(grad_two)
    sums[3][...] += column_sum(grad_low)
    grad_middle = grad_low.astype(F32) + norm_back(grad_two, gain[...], hat, scale)
    outs[1][0] = grad_middle
    low = grad_middle.astype(BF16)
    outs[2][0] = low
    sums[4][...] += column_sum(low)
    outs[3][0] = dot_nt(low, w_out[...]).astype(BF16)


def attend_back_body(length, at, where, blocked, whole, weights, outs, sums):
    packed, grads = blocked
    rows, width = grads.shape[1:]
    lanes = 2 * width // HEADS
    factor = (width // HEADS) ** (-0.5)
    low_lane = lax.broadcasted_iota(jnp.int32, (rows, lanes), 1) < lanes // 2
    key_there = lax.broadcasted_iota(jnp.int32, (rows, rows), 0) < length
    for pair in range(HEADS // 2):
        start = pair * lanes
        cuts = [slice(at * width + start, at * width + start + lanes) for at in range(3)]
        query, keys, values = (packed[0, :, cut] for cut in cuts)
        grad = grads[0, :, start : start + lanes]
        scaled = query * jnp.asarray(factor, BF16)
        results = []
        for side in range(2):
            mine = low_lane if side == 0 else jnp.logical_not(low_lane)
            scores = dot_nt(jnp.where(mine, keys, jnp.zeros_like(keys)), scaled)
            scores = jnp.where(key_there, scores, -1e30)
            expo = jnp.exp(scores - jnp.max(scores, 0, keepdims=True))
            probs = expo * (1.0 / jnp.sum(expo, 0, keepdims=True))
            grad_probs = dot_nt(jnp.where(mine, values, jnp.zeros_like(values)), grad)
            inner = jnp.sum(probs * grad_probs, 0, keepdims=True)
            grad_scores = (probs * (grad_probs - inner) * factor).astype(BF16)
            results.append(
                (
                    dot_tn(grad_scores, keys),
                    dot(grad_scores, query),
                    dot(probs.astype(BF16), grad),
                )
            )
        for cut, left, right in zip(cuts, results[0], results[1]):
            low = jnp.where(low_lane, left, right).astype(BF16)
            outs[0][0, :, cut] = low
            sums[0][:, cut] += column_sum(low)


def input_body(length, at, where, blocked, whole, weights, outs, sums):
    packed, images, grad_middle = blocked
    grad_one = dot_nt(packed[0], weights[0][...])
    hat, scale = normed(images[0].astype(F32))
    sums[0][...] += column_sum(grad_one * hat)
    sums[1][...] += column_sum(grad_one)
    result = grad_middle[0] + norm_back(grad_one, whole[0][...], hat, scale)
    outs[0][0] = result[:length]


def down_body(length, at, where, blocked, whole, weights, outs, sums):
    hidden, middle = blocked
    result = middle[0] + dot(hidden[0], weights[0][...]) + whole[0][...]
    live = jnp.where(at < where[2], 1.0, 0.0).astype(F32)
    outs[0][0] = (result * live)[:length].astype(BF16)


def on_device(
    sizes,
    images,
    counts,
    ln1_gain,
    ln1_shift,
    w_qkv,
    b_query,
    b_value,
    w_out,
    b_out,
    ln2_gain,
    ln2_shift,
    w_up,
    b_up,
    w_down,
    b_down,
    cotangent,
):
    slots, length, width = images.shape
    inner = w_up.shape[1]
    rows = -(-length // 16) * 16
    vectors = (ln1_gain, ln1_shift, b_query, b_value, b_out, ln2_gain, ln2_shift, b_down, b_up)
    gathered = lax.all_gather(jnp.concatenate(vectors), "group", axis=0, tiled=False)
    ends = [0]
    for vector in vectors:
        ends.append(ends[-1] + vector.shape[0])
    small = [
        gathered[:, at:end].reshape(1, -1).astype(F32) for at, end in zip(ends, ends[1:])
    ]
    gain_one, shift_one, bias_query, bias_value, bias_out, gain_two, shift_two, bias_down, bias_up = small
    bias_cat = jnp.concatenate([bias_query, jnp.zeros_like(bias_query), bias_value], 1)
    w_qkv = gather_pieces(w_qkv, sizes)
    w_out = gather_pieces(w_out, sizes)
    w_up = gather_pieces(w_up, sizes)
    w_down = gather_pieces(w_down, sizes)
    place = jnp.stack(
        [lax.axis_index("group"), lax.axis_index("replica") & 1, counts[0], counts[0]]
    ).astype(jnp.int32)
    live = (jnp.arange(slots, dtype=jnp.int32) < counts[0]).astype(BF16)[:, None, None]
    fill = ((0, 0), (0, rows - length), (0, 0))
    images = jnp.pad(images, fill)
    cotangent = jnp.pad(cotangent * live, fill)
    tokens = slots * rows
    unit = 2 * tokens * width * width

    low_one, packed = per_image(
        query_body, place, [images], [gain_one, shift_one, bias_cat], [w_qkv],
        [(rows, width, BF16), (rows, 3 * width, BF16)], [], 3 * unit,
    )
    attended, middle, low_two = per_image(
        functools.partial(attend_body, length), place, [packed, images],
        [bias_out, gain_two, shift_two], [w_out],
        [(rows, width, BF16), (rows, width, F32), (rows, width, BF16)], [], 4 * unit,
    )
    hidden, slope = per_image(
        up_body, place, [low_two], [bias_up], [w_up],
        [(rows, inner, BF16), (rows, inner, BF16)], [], 6 * unit,
    )

    def outer(left, right):
        left = left.reshape(tokens, -1)
        right = right.reshape(tokens, -1)
        return dot_tn(left, right).astype(BF16)

    grad_down = outer(hidden, cotangent)
    grad_pre, grad_middle, grad_branch, grad_att, grad_bup, grad_gain_two, grad_shift_two, grad_bdown, grad_bout = per_image(
        back_body, place, [cotangent, slope, middle], [gain_two], [w_down, w_up, w_out],
        [(rows, inner, BF16), (rows, width, F32), (rows, width, BF16), (rows, width, BF16)],
        [inner, width, width, width, width], 10 * unit,
    )
    grad_up = outer(low_two, grad_pre)
    grad_proj_out = outer(attended, grad_branch)
    grad_packed, packed_sums = per_image(
        functools.partial(attend_back_body, length), place, [packed, grad_att], [], [],
        [(rows, 3 * width, BF16)], [3 * width], 8 * unit,
    )
    grad_qkv = outer(low_one, grad_packed)
    input_grad, grad_gain_one, grad_shift_one = per_image(
        functools.partial(input_body, length), place, [grad_packed, images, grad_middle],
        [gain_one], [w_qkv], [(length, width, F32)], [width, width], 4 * unit,
    )
    (outputs,) = per_image(
        functools.partial(down_body, length), place, [hidden, middle], [bias_down], [w_down],
        [(length, width, BF16)], [], 5 * unit,
    )
    big = [
        reduce_shards(grad, sizes, 2)
        for grad in (grad_down, grad_up, grad_proj_out, grad_qkv)
    ]
    parts = (
        grad_gain_one,
        grad_shift_one,
        packed_sums[:, :width],
        packed_sums[:, 2 * width :],
        grad_bout,
        grad_gain_two,
        grad_shift_two,
        grad_bdown,
        grad_bup,
    )
    joined = jnp.concatenate([part.reshape(sizes[0], -1) for part in parts], 1)
    little = reduce_shards(joined.reshape(sizes[0], -1, 128), sizes, 0).reshape(-1)
    sums = [little[at:end] for at, end in zip(ends, ends[1:])]
    return (
        outputs,
        input_grad,
        sums[0],
        sums[1],
        big[3],
        sums[2],
        sums[3],
        big[2],
        sums[4],
        sums[5],
        sums[6],
        big[1],
        sums[8],
        big[0],
        sums[7],
    )


def solution(mesh):
    sizes = (mesh.shape["group"], mesh.shape["replica"])
    line = P("group")
    grid = P("group", None)
    field = P(("replica", "group"), None, None)
    return jax.shard_map(
        functools.partial(on_device, sizes),
        mesh=mesh,
        in_specs=(
            field, P(("replica", "group")), line, line, grid, line, line, grid, line, line, line,
            grid, line, grid, line, field,
        ),
        out_specs=(
            field, field, line, line, grid, line, line, grid, line, line, line, grid, line, grid,
            line,
        ),
        check_vma=False,
    )
```

```python
import functools

import jax
import jax.numpy as jnp
from jax import lax
from jax.experimental import pallas as pl
from jax.experimental.pallas import tpu as pltpu
from jax.sharding import PartitionSpec as P

HEADS = 12
F32 = jnp.float32
BF16 = jnp.bfloat16
GELU_A = 0.7978845608028654
GELU_B = 0.044715


def swap(field, axis, size, bit):
    return lax.ppermute(field, axis, [(at, at ^ bit) for at in range(size)])


def is_power(size):
    return size & (size - 1) == 0


def pick(field, at, axis):
    return lax.dynamic_index_in_dim(field, at, axis, keepdims=False)


def fence(*groups):
    return lax.optimization_barrier(groups)


class Gather:
    def __init__(self, shard, sizes, partner):
        self.groups, self.replicas = sizes
        self.shard = shard
        self.rows = shard.shape[0]
        self.split = self.groups == 4 and self.replicas % (2 * partner) == 0 and self.rows % 32 == 0
        self.partner = partner
        self.half = (lax.axis_index("replica") // partner) & 1
        if not self.split:
            self.whole = lax.all_gather(shard, "group", axis=0, tiled=True)
            return
        self.out = pick(shard.reshape(2, self.rows // 2, -1), self.half, 0)

    def near(self):
        if self.split:
            self.beside = swap(self.shard, "group", 4, 1)

    def far(self):
        if self.split:
            self.first = swap(self.out, "group", 4, 2)

    def across(self):
        if self.split:
            self.second = swap(self.first, "replica", self.replicas, self.partner)
            self.far_first = swap(self.first, "group", 4, 1)

    def last(self):
        if self.split:
            self.far_second = swap(self.second, "group", 4, 1)

    def pieces(self):
        if not self.split:
            return (self.whole,)
        return (self.shard, self.beside, self.first, self.second, self.far_first, self.far_second)


def place_pieces(rows, pieces, me, half):
    if pieces == 1:
        return [0]
    part = rows // 2
    return [
        me * rows,
        (me ^ 1) * rows,
        (me ^ 2) * rows + half * part,
        (me ^ 2) * rows + (1 - half) * part,
        (me ^ 3) * rows + half * part,
        (me ^ 3) * rows + (1 - half) * part,
    ]


def add_low(left, right, kind):
    return (left.astype(F32) + right.astype(F32)).astype(kind)


class Reduce:
    def __init__(self, grad, sizes, halvings):
        self.sizes = sizes
        self.kind = grad.dtype
        groups, replicas = sizes
        self.rows = grad.shape[0] // groups
        self.hops = []
        self.flying = False
        if not (is_power(groups) and is_power(replicas)):
            shard = lax.psum_scatter(grad, "group", scatter_dimension=0, tiled=True)
            self.terms = [lax.psum(shard.astype(F32), "replica")]
            return
        self.terms = [grad.reshape((groups, self.rows) + grad.shape[1:])]
        bit = 1
        while bit < groups:
            self.hops.append(("group", bit, "split"))
            bit *= 2
        bit = 1
        while bit < replicas:
            self.hops.append(("replica", bit, "halve" if len(self.hops) < halvings + 2 else "whole"))
            bit *= 2
        back = [(axis, bit, "back") for axis, bit, kind in self.hops if kind == "halve"]
        self.hops += reversed(back)

    def total(self, parts=None, kind=None):
        parts = self.terms if parts is None else parts
        if len(parts) == 1:
            return parts[0].astype(kind or self.kind)
        return sum(part.astype(F32) for part in parts).astype(kind or self.kind)

    def outgoing(self):
        axis, bit, kind = self.hops[0]
        side = (lax.axis_index(axis) // bit) & 1
        if kind == "split":
            shape = self.terms[0].shape
            pairs = [term.reshape((shape[0] // 2, 2) + shape[1:]) for term in self.terms]
            self.keep = [pick(term, side, 1) for term in pairs]
            if shape[0] == 2:
                self.keep = [term[0] for term in self.keep]
            return self.total([pick(term, 1 - side, 1) for term in pairs])
        if kind == "halve":
            shape = self.terms[0].shape
            pairs = [term.reshape((2, shape[0] // 2) + shape[1:]) for term in self.terms]
            self.keep = [pick(term, side, 0) for term in pairs]
            return self.total([pick(term, 1 - side, 0) for term in pairs])
        return self.total()

    def launch(self, out):
        axis, bit, kind = self.hops.pop(0)
        size = self.sizes[0] if axis == "group" else self.sizes[1]
        self.came = swap(out, axis, size, bit)
        side = (lax.axis_index(axis) // bit) & 1
        if kind in ("split", "halve"):
            self.held = self.total(self.keep)
        else:
            self.held = out
        self.kind_of_hop, self.side = kind, side
        self.flying = True

    def land(self, came):
        self.flying = False
        if self.kind_of_hop == "back":
            held = self.held
            self.terms = [
                jnp.where(
                    self.side == 0,
                    jnp.concatenate([held, came]),
                    jnp.concatenate([came, held]),
                )
            ]
            return
        if self.kind_of_hop == "split" and self.held.ndim < came.ndim:
            came = came[0]
        self.terms = [self.held, came]

    def drain(self):
        while self.flying:
            self.land(self.came)
            if self.hops:
                self.launch(self.outgoing())

    def result(self):
        return self.total(kind=F32)


def turn(landing, launching, carry):
    landing = [chain for chain in landing if chain.flying]
    came, carry = fence([chain.came for chain in landing], carry)
    for chain, part in zip(landing, came):
        chain.land(part)
    launching = [chain for chain in launching if chain.hops]
    outs, carry = fence([chain.outgoing() for chain in launching], carry)
    for chain, out in zip(launching, outs):
        chain.launch(out)
    return carry


def dot(left, right):
    return lax.dot_general(left, right, (((1,), (0,)), ((), ())), preferred_element_type=F32)


def dot_nt(left, right):
    return lax.dot_general(left, right, (((1,), (1,)), ((), ())), preferred_element_type=F32)


def dot_tn(left, right):
    return lax.dot_general(left, right, (((0,), (0,)), ((), ())), preferred_element_type=F32)


def per_image(body, place, blocked, whole, weights, outs, sums, flops, after=()):
    slots = blocked[0].shape[0]
    halves = [1 + gather.partner for gather in weights]
    weights = [gather.pieces() for gather in weights]
    counts = [len(pieces) for pieces in weights]
    rows_of = [pieces[0].shape[0] for pieces in weights]
    total = [rows * (4 if len(pieces) > 1 else 1) for rows, pieces in zip(rows_of, weights)]

    def kernel(*refs):
        refs = list(refs)

        def take(count):
            taken = refs[:count]
            del refs[:count]
            return taken

        (where,) = take(1)
        blocked_refs = take(len(blocked))
        whole_refs = take(len(whole))
        piece_refs = [take(count) for count in counts]
        take(len(after))
        out_refs = take(len(outs))
        sum_refs = take(len(sums))
        weight_refs = take(len(weights))
        at = pl.program_id(0)

        @pl.when(at == 0)
        def _():
            copies = []
            for index, pieces in enumerate(piece_refs):
                starts = place_pieces(rows_of[index], len(pieces), where[0], where[halves[index]])
                for spot, (piece, start) in enumerate(zip(pieces, starts)):
                    target = weight_refs[index].at[pl.ds(pl.multiple_of(start, 16), piece.shape[0])]
                    copies.append(pltpu.make_async_copy(piece, target, refs[0].at[index, spot]))
            for copy in copies:
                copy.start()
            for ref in sum_refs:
                ref[...] = jnp.zeros_like(ref)
            for copy in copies:
                copy.wait()

        body(at, where, blocked_refs, whole_refs, weight_refs, out_refs, sum_refs)

    in_specs = [pl.BlockSpec(memory_space=pltpu.SMEM)]
    for array in blocked:
        in_specs.append(pl.BlockSpec((1,) + array.shape[1:], lambda i: (i, 0, 0)))
    for array in whole:
        in_specs.append(pl.BlockSpec(array.shape, lambda i: (0, 0)))
    pieces = [piece for parts in weights for piece in parts]
    in_specs += [pl.BlockSpec(memory_space=pl.ANY)] * (len(pieces) + len(after))
    out_specs = [pl.BlockSpec((1, rows, columns), lambda i: (i, 0, 0)) for rows, columns, _ in outs]
    out_specs += [pl.BlockSpec((1, columns), lambda i: (0, 0)) for columns in sums]
    shapes = [jax.ShapeDtypeStruct((slots, rows, columns), kind) for rows, columns, kind in outs]
    shapes += [jax.ShapeDtypeStruct((1, columns), F32) for columns in sums]
    scratch = [
        pltpu.VMEM((rows, parts[0].shape[1]), BF16) for rows, parts in zip(total, weights)
    ]
    if weights:
        scratch.append(pltpu.SemaphoreType.DMA((len(weights), 6)))
    moved = sum(array.size * array.dtype.itemsize for array in list(blocked) + pieces)
    moved += sum(shape.size * shape.dtype.itemsize for shape in shapes)
    return pl.pallas_call(
        kernel,
        grid=(slots,),
        in_specs=in_specs,
        out_specs=out_specs,
        out_shape=shapes,
        scratch_shapes=scratch,
        compiler_params=pltpu.CompilerParams(
            dimension_semantics=("arbitrary",), vmem_limit_bytes=56 * 2**20
        ),
        cost_estimate=pl.CostEstimate(flops=flops, bytes_accessed=moved, transcendentals=0),
    )(place, *blocked, *whole, *pieces, *after)


def normed(field):
    centred = field - jnp.mean(field, -1, keepdims=True)
    scale = lax.rsqrt(jnp.mean(centred * centred, -1, keepdims=True) + 1e-06)
    return centred * scale, scale


def norm_back(grad, gain, hat, scale):
    inner = grad * gain
    mean = jnp.mean(inner, -1, keepdims=True)
    along = jnp.mean(inner * hat, -1, keepdims=True)
    return scale * (inner - mean - hat * along)


def column_sum(field):
    return jnp.sum(field.astype(F32), 0, keepdims=True)


def query_body(at, where, blocked, whole, weights, outs, sums):
    gain, shift, bias = whole
    hat, _ = normed(blocked[0][0].astype(F32))
    low = (hat * gain[...] + shift[...]).astype(BF16)
    outs[0][0] = low
    width = low.shape[1]
    for part in range(3):
        cut = slice(part * width, (part + 1) * width)
        outs[1][0, :, cut] = (dot(low, weights[0][:, cut]) + bias[:, cut]).astype(BF16)


def attend_body(length, at, where, blocked, whole, weights, outs, sums):
    (packed,) = blocked
    rows = packed.shape[1]
    width = packed.shape[2] // 3
    lanes = 2 * width // HEADS
    factor = (width // HEADS) ** (-0.5)
    low_lane = lax.broadcasted_iota(jnp.int32, (rows, lanes), 1) < lanes // 2
    key_there = lax.broadcasted_iota(jnp.int32, (rows, rows), 1) < length
    for pair in range(HEADS // 2):
        start = pair * lanes
        query = packed[0, :, start : start + lanes] * jnp.asarray(factor, BF16)
        keys = packed[0, :, width + start : width + start + lanes]
        values = packed[0, :, 2 * width + start : 2 * width + start + lanes]
        both = []
        for side in range(2):
            mine = low_lane if side == 0 else jnp.logical_not(low_lane)
            scores = dot_nt(jnp.where(mine, query, jnp.zeros_like(query)), keys)
            scores = jnp.where(key_there, scores, -1e30)
            expo = jnp.exp(scores - jnp.max(scores, -1, keepdims=True))
            probs = expo * (1.0 / jnp.sum(expo, -1, keepdims=True))
            both.append(dot(probs.astype(BF16), values))
        outs[0][0, :, start : start + lanes] = jnp.where(low_lane, both[0], both[1]).astype(BF16)


def up_body(at, where, blocked, whole, weights, outs, sums):
    attended, images = blocked
    bias_out, gain, shift, bias_up = whole
    w_out, w_up = weights
    middle = images[0].astype(F32) + dot(attended[0], w_out[...]) + bias_out[...]
    outs[2][0] = middle
    hat, _ = normed(middle)
    low = (hat * gain[...] + shift[...]).astype(BF16)
    outs[3][0] = low
    inner = w_up.shape[1]
    width = low.shape[1]
    for start in range(0, inner, width):
        cut = slice(start, start + width)
        pre = dot(low, w_up[:, cut]) + bias_up[:, cut]
        square = pre * pre
        bend = jnp.tanh(pre * (GELU_A + (GELU_A * GELU_B) * square))
        half = 0.5 + 0.5 * bend
        outs[0][0, :, cut] = (pre * half).astype(BF16)
        slope = GELU_A + (3.0 * GELU_A * GELU_B) * square
        outs[1][0, :, cut] = (half + (0.5 * pre) * ((1.0 - bend * bend) * slope)).astype(BF16)


def pre_body(at, where, blocked, whole, weights, outs, sums):
    cotangent, slope = blocked
    grad_low = cotangent[0]
    width = grad_low.shape[1]
    for start in range(0, slope.shape[2], width):
        cut = slice(start, start + width)
        grad_pre = dot_nt(grad_low, weights[0][cut, :]) * slope[0, :, cut].astype(F32)
        low = grad_pre.astype(BF16)
        outs[0][0, :, cut] = low
        sums[0][:, cut] += column_sum(low)
    sums[1][...] += column_sum(grad_low)


def back_body(at, where, blocked, whole, weights, outs, sums):
    cotangent, grad_pre, middle = blocked
    (gain,) = whole
    w_up, w_out = weights
    grad_two = dot_nt(grad_pre[0], w_up[...])
    hat, scale = normed(middle[0])
    sums[0][...] += column_sum(grad_two * hat)
    sums[1][...] += column_sum(grad_two)
    grad_middle = cotangent[0].astype(F32) + norm_back(grad_two, gain[...], hat, scale)
    outs[0][0] = grad_middle
    low = grad_middle.astype(BF16)
    outs[1][0] = low
    sums[2][...] += column_sum(low)
    outs[2][0] = dot_nt(low, w_out[...]).astype(BF16)


def attend_back_body(length, pairs, at, where, blocked, whole, weights, outs, sums):
    packed, grads = blocked
    rows, width = grads.shape[1:]
    part = outs[0].shape[2] // 3
    lanes = 2 * width // HEADS
    factor = (width // HEADS) ** (-0.5)
    low_lane = lax.broadcasted_iota(jnp.int32, (rows, lanes), 1) < lanes // 2
    key_there = lax.broadcasted_iota(jnp.int32, (rows, rows), 0) < length
    for pair in pairs:
        start = pair * lanes
        first = (pair - pairs[0]) * lanes
        cuts = [slice(at * width + start, at * width + start + lanes) for at in range(3)]
        query, keys, values = (packed[0, :, cut] for cut in cuts)
        grad = grads[0, :, start : start + lanes]
        scaled = query * jnp.asarray(factor, BF16)
        results = []
        for side in range(2):
            mine = low_lane if side == 0 else jnp.logical_not(low_lane)
            scores = dot_nt(jnp.where(mine, keys, jnp.zeros_like(keys)), scaled)
            scores = jnp.where(key_there, scores, -1e30)
            expo = jnp.exp(scores - jnp.max(scores, 0, keepdims=True))
            probs = expo * (1.0 / jnp.sum(expo, 0, keepdims=True))
            grad_probs = dot_nt(jnp.where(mine, values, jnp.zeros_like(values)), grad)
            inner = jnp.sum(probs * grad_probs, 0, keepdims=True)
            grad_scores = (probs * (grad_probs - inner) * factor).astype(BF16)
            results.append(
                (
                    dot_tn(grad_scores, keys),
                    dot(grad_scores, query),
                    dot(probs.astype(BF16), grad),
                )
            )
        for kind in range(3):
            low = jnp.where(low_lane, results[0][kind], results[1][kind]).astype(BF16)
            cut = slice(kind * part + first, kind * part + first + lanes)
            outs[0][0, :, cut] = low
            sums[0][:, cut] += column_sum(low)


def input_body(length, at, where, blocked, whole, weights, outs, sums):
    *packed, images, grad_middle = blocked
    width = images.shape[2]
    grad_one = None
    start = 0
    for array in packed:
        part = array.shape[2] // 3
        for kind in range(3):
            weight = weights[0][:, kind * width + start : kind * width + start + part]
            term = dot_nt(array[0, :, kind * part : (kind + 1) * part], weight)
            grad_one = term if grad_one is None else grad_one + term
        start += part
    hat, scale = normed(images[0].astype(F32))
    sums[0][...] += column_sum(grad_one * hat)
    sums[1][...] += column_sum(grad_one)
    result = grad_middle[0] + norm_back(grad_one, whole[0][...], hat, scale)
    outs[0][0] = result[:length]


def down_body(length, at, where, blocked, whole, weights, outs, sums):
    hidden, middle = blocked
    result = middle[0] + dot(hidden[0], weights[0][...]) + whole[0][...]
    live = jnp.where(at < where[1], 1.0, 0.0).astype(F32)
    outs[0][0] = (result * live)[:length].astype(BF16)


def on_device(
    sizes,
    images,
    counts,
    ln1_gain,
    ln1_shift,
    w_qkv,
    b_query,
    b_value,
    w_out,
    b_out,
    ln2_gain,
    ln2_shift,
    w_up,
    b_up,
    w_down,
    b_down,
    cotangent,
):
    slots, length, width = images.shape
    inner = w_up.shape[1]
    rows = -(-length // 16) * 16
    vectors = (ln1_gain, ln1_shift, b_query, b_value, b_out, ln2_gain, ln2_shift, b_down, b_up)
    row = jnp.concatenate(vectors)
    g_qkv = Gather(w_qkv, sizes, 1)
    g_out = Gather(w_out, sizes, 1)
    g_up = Gather(w_up, sizes, 2)
    g_down = Gather(w_down, sizes, 1)
    if sizes[0] == 4:
        me = lax.axis_index("group")
        line = row.reshape(-1, 128)
        far_line = swap(line, "group", 4, 2)
        near_line = swap(line, "group", 4, 1)
        far_near = swap(far_line, "group", 4, 1)
    g_qkv.near()
    g_qkv.far()
    if sizes[0] == 4:
        lines = jnp.stack([line, near_line, far_line, far_near])
        gathered = jnp.stack([pick(lines, at ^ me, 0) for at in range(4)]).reshape(4, -1)
    else:
        gathered = lax.all_gather(row, "group", axis=0, tiled=False)
    ends = [0]
    for vector in vectors:
        ends.append(ends[-1] + vector.shape[0])
    small = [
        gathered[:, at:end].reshape(1, -1).astype(F32) for at, end in zip(ends, ends[1:])
    ]
    gain_one, shift_one, bias_query, bias_value, bias_out, gain_two, shift_two, bias_down, bias_up = small
    bias_cat = jnp.concatenate([bias_query, jnp.zeros_like(bias_query), bias_value], 1)
    place = jnp.stack(
        [lax.axis_index("group"), counts[0], lax.axis_index("replica") & 1, (lax.axis_index("replica") >> 1) & 1]
    ).astype(jnp.int32)
    live = (jnp.arange(slots, dtype=jnp.int32) < counts[0]).astype(BF16)[:, None, None]
    fill = ((0, 0), (0, rows - length), (0, 0))
    images = jnp.pad(images, fill)
    cotangent = jnp.pad(cotangent * live, fill)
    tokens = slots * rows
    unit = 2 * tokens * width * width


    def outer(left, right):
        left = left.reshape(tokens, -1)
        right = right.reshape(tokens, -1)
        return dot_tn(left, right).astype(BF16)

    def hand_over(gather, name, carry):
        if gather.split:
            part, carry = fence(getattr(gather, name), carry)
            setattr(gather, name, part)
        return carry

    if g_qkv.split:
        g_qkv.first, g_out.out, g_up.out = fence(g_qkv.first, g_out.out, g_up.out)
    g_qkv.across()
    g_out.far()
    g_up.far()
    g_up.near()
    g_out.near()
    g_qkv.last()
    low_one, packed = per_image(
        query_body, place, [images], [gain_one, shift_one, bias_cat], [g_qkv],
        [(rows, width, BF16), (rows, 3 * width, BF16)], [], 3 * unit,
    )
    packed = hand_over(g_out, "first", packed)
    packed = hand_over(g_up, "first", packed)
    if g_down.split:
        g_down.out, packed = fence(g_down.out, packed)
    g_out.across()
    g_up.across()
    g_down.far()
    g_down.near()
    (attended,) = per_image(
        functools.partial(attend_body, length), place, [packed], [], [],
        [(rows, width, BF16)], [], 3 * unit,
    )
    attended = hand_over(g_out, "second", attended)
    attended = hand_over(g_up, "second", attended)
    attended = hand_over(g_down, "first", attended)
    g_out.last()
    g_up.last()
    g_down.across()
    hidden, slope, middle, low_two = per_image(
        up_body, place, [attended, images], [bias_out, gain_two, shift_two, bias_up],
        [g_out, g_up],
        [(rows, inner, BF16), (rows, inner, BF16), (rows, width, F32), (rows, width, BF16)],
        [], 8 * unit,
    )
    hidden = hand_over(g_down, "second", hidden)
    g_down.last()
    down = Reduce(outer(hidden, cotangent), sizes, 2)
    slope = turn([], [down], slope)
    grad_pre, grad_bup, grad_bdown = per_image(
        pre_body, place, [cotangent, slope], [], [g_down],
        [(rows, inner, BF16)], [inner, width], 6 * unit,
    )
    grad_pre = turn([down], [down], grad_pre)
    up = Reduce(outer(low_two, grad_pre), sizes, 2)
    grad_pre = turn([], [up], grad_pre)
    grad_middle, grad_branch, grad_att, grad_gain_two, grad_shift_two, grad_bout = per_image(
        back_body, place, [cotangent, grad_pre, middle], [gain_two], [g_up, g_out],
        [(rows, width, F32), (rows, width, BF16), (rows, width, BF16)],
        [width, width, width], 7 * unit,
    )
    out = Reduce(outer(attended, grad_branch), sizes, 2)
    grad_att = turn([down, up], [down, up, out], grad_att)
    half = HEADS // 4
    grad_one, sums_one = per_image(
        functools.partial(attend_back_body, length, range(half)), place, [packed, grad_att],
        [], [], [(rows, 3 * width // 2, BF16)], [3 * width // 2], 4 * unit,
    )
    qkv_one = Reduce(outer(low_one, grad_one), sizes, 2)
    grad_att = turn([down, out], [down, out, qkv_one], grad_att)
    grad_two, sums_two = per_image(
        functools.partial(attend_back_body, length, range(half, 2 * half)), place,
        [packed, grad_att], [], [], [(rows, 3 * width // 2, BF16)], [3 * width // 2], 4 * unit,
    )
    qkv_two = Reduce(outer(low_one, grad_two), sizes, 2)
    grad_middle = turn(
        [down, up, out, qkv_one], [down, up, out, qkv_one, qkv_two], grad_middle
    )
    input_grad, grad_gain_one, grad_shift_one = per_image(
        functools.partial(input_body, length), place, [grad_one, grad_two, images, grad_middle],
        [gain_one], [g_qkv], [(length, width, F32)], [width, width], 4 * unit,
    )
    packed_sums = jnp.concatenate(
        [
            sums[:, kind * width // 2 : (kind + 1) * width // 2]
            for kind in range(3)
            for sums in (sums_one, sums_two)
        ],
        1,
    )
    parts = (
        grad_gain_one,
        grad_shift_one,
        packed_sums[:, :width],
        packed_sums[:, 2 * width :],
        grad_bout,
        grad_gain_two,
        grad_shift_two,
        grad_bdown,
        grad_bup,
    )
    joined = jnp.concatenate([part.reshape(sizes[0], -1) for part in parts], 1)
    little = Reduce(joined.reshape(sizes[0], -1, 128), sizes, 0)
    chains = [down, up, out, qkv_one, qkv_two]
    hidden = turn(chains, [little] + chains, hidden)
    (outputs,) = per_image(
        functools.partial(down_body, length), place, [hidden, middle], [bias_down], [g_down],
        [(length, width, BF16)], [], 5 * unit,
    )
    for chain in [little] + chains:
        chain.drain()
    little = little.result().reshape(-1)
    sums = [little[at:end] for at, end in zip(ends, ends[1:])]
    left, right = qkv_one.result(), qkv_two.result()
    grad_qkv = jnp.concatenate(
        [
            side[:, kind * width // 2 : (kind + 1) * width // 2]
            for kind in range(3)
            for side in (left, right)
        ],
        1,
    )
    big = [down.result(), up.result(), out.result(), grad_qkv]
    return (
        outputs,
        input_grad,
        sums[0],
        sums[1],
        big[3],
        sums[2],
        sums[3],
        big[2],
        sums[4],
        sums[5],
        sums[6],
        big[1],
        sums[8],
        big[0],
        sums[7],
    )


def solution(mesh):
    sizes = (mesh.shape["group"], mesh.shape["replica"])
    line = P("group")
    grid = P("group", None)
    field = P(("replica", "group"), None, None)
    return jax.shard_map(
        functools.partial(on_device, sizes),
        mesh=mesh,
        in_specs=(
            field, P(("replica", "group")), line, line, grid, line, line, grid, line, line, line,
            grid, line, grid, line, field,
        ),
        out_specs=(
            field, field, line, line, grid, line, line, grid, line, line, line, grid, line, grid,
            line,
        ),
        check_vma=False,
    )
```

```python
import functools

import jax
import jax.numpy as jnp
from jax import lax
from jax.experimental import pallas as pl
from jax.experimental.pallas import tpu as pltpu
from jax.sharding import PartitionSpec as P

HEADS = 12
F32 = jnp.float32
BF16 = jnp.bfloat16
GELU_A = 0.7978845608028654
GELU_B = 0.044715


def swap(field, axis, size, bit):
    return lax.ppermute(field, axis, [(at, at ^ bit) for at in range(size)])


def is_power(size):
    return size & (size - 1) == 0


def pick(field, at, axis):
    return lax.dynamic_index_in_dim(field, at, axis, keepdims=False)


def fence(*groups):
    return lax.optimization_barrier(groups)


class Gather:
    def __init__(self, shard, sizes, partner):
        self.groups, self.replicas = sizes
        self.shard = shard
        self.rows = shard.shape[0]
        self.split = self.groups == 4 and self.replicas % (2 * partner) == 0 and self.rows % 32 == 0
        self.partner = partner
        self.half = (lax.axis_index("replica") // partner) & 1
        if not self.split:
            self.whole = lax.all_gather(shard, "group", axis=0, tiled=True)
            return
        self.out = pick(shard.reshape(2, self.rows // 2, -1), self.half, 0)

    def near(self):
        if self.split:
            self.beside = swap(self.shard, "group", 4, 1)

    def far(self):
        if self.split:
            self.first = swap(self.out, "group", 4, 2)

    def across(self):
        if self.split:
            self.second = swap(self.first, "replica", self.replicas, self.partner)
            self.far_first = swap(self.first, "group", 4, 1)

    def last(self):
        if self.split:
            self.far_second = swap(self.second, "group", 4, 1)

    def pieces(self):
        if not self.split:
            return (self.whole,)
        return (self.shard, self.beside, self.first, self.second, self.far_first, self.far_second)


def place_pieces(rows, pieces, me, half):
    if pieces == 1:
        return [0]
    part = rows // 2
    return [
        me * rows,
        (me ^ 1) * rows,
        (me ^ 2) * rows + half * part,
        (me ^ 2) * rows + (1 - half) * part,
        (me ^ 3) * rows + half * part,
        (me ^ 3) * rows + (1 - half) * part,
    ]


def add_low(left, right, kind):
    return (left.astype(F32) + right.astype(F32)).astype(kind)


class Share:
    def __init__(self, field, sizes):
        self.field = field
        self.flying = False
        self.hops = []
        if not (is_power(sizes[0]) and is_power(sizes[1])):
            self.field = lax.psum(field, ("replica", "group"))
            return
        for axis, size in zip(("group", "replica"), sizes):
            bit = 1
            while bit < size:
                self.hops.append((axis, size, bit))
                bit *= 2

    def outgoing(self):
        return self.field

    def launch(self, out):
        self.field = out
        self.came = swap(out, *self.hops.pop(0))
        self.flying = True

    def land(self, came):
        self.field = self.field + came
        self.flying = False

    def drain(self):
        while self.flying:
            self.land(self.came)
            if self.hops:
                self.launch(self.outgoing())


class Reduce:
    def __init__(self, grad, sizes, halvings, scatter=False):
        self.sizes = sizes
        self.ready = None
        self.kind = BF16
        groups, replicas = sizes
        self.hops = []
        self.flying = False
        if not (is_power(groups) and is_power(replicas)):
            shard = lax.psum_scatter(grad, "group", scatter_dimension=0, tiled=True)
            self.terms = [lax.psum(shard.astype(F32), "replica")]
            return
        if scatter:
            self.terms = [lax.psum_scatter(grad, "group", scatter_dimension=0, tiled=True)]
        else:
            self.ready = grad
            bit = 1
            while bit < groups:
                self.hops.append(("group", bit, "split"))
                bit *= 2
        bit = 1
        back = []
        while bit < replicas:
            if len(back) < halvings:
                self.hops.append(("replica", bit, "halve"))
                back.append(("replica", bit, "back"))
            else:
                self.hops.append(("replica", bit, "whole"))
            bit *= 2
        self.hops += reversed(back)

    def total(self, parts=None, kind=None):
        parts = self.terms if parts is None else parts
        if len(parts) == 1:
            return parts[0].astype(kind or self.kind)
        return sum(part.astype(F32) for part in parts).astype(kind or self.kind)

    def outgoing(self):
        if self.ready:
            out, keep = self.ready
            self.ready, self.keep = None, [keep]
            return out
        axis, bit, kind = self.hops[0]
        side = (lax.axis_index(axis) // bit) & 1
        if kind == "split":
            shape = self.terms[0].shape
            pairs = [term.reshape((shape[0] // 2, 2) + shape[1:]) for term in self.terms]
            self.keep = [pick(term, side, 1) for term in pairs]
            if shape[0] == 2:
                self.keep = [term[0] for term in self.keep]
            return self.total([pick(term, 1 - side, 1) for term in pairs])
        if kind == "halve":
            shape = self.terms[0].shape
            pairs = [term.reshape((2, shape[0] // 2) + shape[1:]) for term in self.terms]
            self.keep = [pick(term, side, 0) for term in pairs]
            return self.total([pick(term, 1 - side, 0) for term in pairs])
        return self.total()

    def launch(self, out):
        axis, bit, kind = self.hops.pop(0)
        size = self.sizes[0] if axis == "group" else self.sizes[1]
        self.came = swap(out, axis, size, bit)
        side = (lax.axis_index(axis) // bit) & 1
        if kind in ("split", "halve"):
            self.held = self.total(self.keep)
            if kind == "split" and out.shape[0] == 1 and self.held.ndim == out.ndim:
                self.held = self.held[0]
        else:
            self.held = out
        self.kind_of_hop, self.side = kind, side
        self.flying = True

    def land(self, came):
        self.flying = False
        if self.kind_of_hop == "back":
            held = self.held
            self.terms = [
                jnp.where(
                    self.side == 0,
                    jnp.concatenate([held, came]),
                    jnp.concatenate([came, held]),
                )
            ]
            return
        if self.kind_of_hop == "split" and self.held.ndim < came.ndim:
            came = came[0]
        self.terms = [self.held, came]

    def drain(self):
        while self.flying:
            self.land(self.came)
            if self.hops:
                self.launch(self.outgoing())

    def result(self):
        return self.total(kind=F32)


def turn(landing, launching, carry):
    landing = [chain for chain in landing if chain.flying]
    came, carry = fence([chain.came for chain in landing], carry)
    for chain, part in zip(landing, came):
        chain.land(part)
    launching = [chain for chain in launching if chain.hops]
    outs, carry = fence([chain.outgoing() for chain in launching], carry)
    for chain, out in zip(launching, outs):
        chain.launch(out)
    return carry


def dot(left, right):
    return lax.dot_general(left, right, (((1,), (0,)), ((), ())), preferred_element_type=F32)


def dot_nt(left, right):
    return lax.dot_general(left, right, (((1,), (1,)), ((), ())), preferred_element_type=F32)


def dot_tn(left, right):
    return lax.dot_general(left, right, (((0,), (0,)), ((), ())), preferred_element_type=F32)


def per_image(body, place, blocked, whole, weights, outs, sums):
    slots = blocked[0].shape[0]
    halves = [1 + gather.partner for gather in weights]
    weights = [gather.pieces() for gather in weights]
    counts = [len(pieces) for pieces in weights]
    rows_of = [pieces[0].shape[0] for pieces in weights]
    total = [rows * (4 if len(pieces) > 1 else 1) for rows, pieces in zip(rows_of, weights)]

    def kernel(*refs):
        refs = list(refs)

        def take(count):
            taken = refs[:count]
            del refs[:count]
            return taken

        (where,) = take(1)
        blocked_refs = take(len(blocked))
        whole_refs = take(len(whole))
        piece_refs = [take(count) for count in counts]
        out_refs = take(len(outs))
        sum_refs = take(len(sums))
        weight_refs = take(len(weights))
        at = pl.program_id(0)

        @pl.when(at == 0)
        def _():
            copies = []
            for index, pieces in enumerate(piece_refs):
                starts = place_pieces(rows_of[index], len(pieces), where[0], where[halves[index]])
                for spot, (piece, start) in enumerate(zip(pieces, starts)):
                    target = weight_refs[index].at[pl.ds(pl.multiple_of(start, 16), piece.shape[0])]
                    copies.append(pltpu.make_async_copy(piece, target, refs[0].at[index, spot]))
            for copy in copies:
                copy.start()
            for ref in sum_refs:
                ref[...] = jnp.zeros_like(ref)
            for copy in copies:
                copy.wait()

        body(at, where, blocked_refs, whole_refs, weight_refs, out_refs, sum_refs)

    in_specs = [pl.BlockSpec(memory_space=pltpu.SMEM)]
    for array in blocked:
        in_specs.append(pl.BlockSpec((1,) + array.shape[1:], lambda i: (i, 0, 0)))
    for array in whole:
        in_specs.append(pl.BlockSpec(array.shape, lambda i: (0, 0)))
    pieces = [piece for parts in weights for piece in parts]
    in_specs += [pl.BlockSpec(memory_space=pl.ANY)] * len(pieces)
    out_specs = [pl.BlockSpec((1, rows, columns), lambda i: (i, 0, 0)) for rows, columns, _ in outs]
    out_specs += [pl.BlockSpec((1, columns), lambda i: (0, 0)) for columns in sums]
    shapes = [jax.ShapeDtypeStruct((slots, rows, columns), kind) for rows, columns, kind in outs]
    shapes += [jax.ShapeDtypeStruct((1, columns), F32) for columns in sums]
    scratch = [
        pltpu.VMEM((rows, parts[0].shape[1]), BF16) for rows, parts in zip(total, weights)
    ]
    if weights:
        scratch.append(pltpu.SemaphoreType.DMA((len(weights), 6)))
    return pl.pallas_call(
        kernel,
        grid=(slots,),
        in_specs=in_specs,
        out_specs=out_specs,
        out_shape=shapes,
        scratch_shapes=scratch,
        compiler_params=pltpu.CompilerParams(
            dimension_semantics=("arbitrary",), vmem_limit_bytes=56 * 2**20
        ),
        cost_estimate=pl.CostEstimate(flops=1, bytes_accessed=1, transcendentals=0),
    )(place, *blocked, *whole, *pieces)


def normed(field):
    centred = field - jnp.mean(field, -1, keepdims=True)
    scale = lax.rsqrt(jnp.mean(centred * centred, -1, keepdims=True) + 1e-06)
    return centred * scale, scale


def norm_back(grad, gain, hat, scale):
    inner = grad * gain
    mean = jnp.mean(inner, -1, keepdims=True)
    along = jnp.mean(inner * hat, -1, keepdims=True)
    return scale * (inner - mean - hat * along)


def column_sum(field):
    return jnp.sum(field.astype(F32), 0, keepdims=True)


def outer_halves(place, left, right, groups):
    slots, rows, width = left.shape
    columns = right.shape[2]
    tokens = slots * rows
    share = width // groups
    step = columns // 3

    def kernel(where, left_ref, right_ref, send_ref, keep_ref, flipped, total):
        @pl.when(pl.program_id(0) == 0)
        def _():
            flipped[...] = left_ref[...].T

        total[...] = dot(flipped[...], right_ref[...]).astype(BF16)
        side = where[0] & 1
        for spot in range(groups // 2):
            for ref, mine in ((send_ref, 1 - side), (keep_ref, side)):
                start = pl.multiple_of((2 * spot + mine) * share, 16)
                ref[spot] = total[pl.ds(start, share), :]

    shape = jax.ShapeDtypeStruct((groups // 2, share, columns), BF16)
    return pl.pallas_call(
        kernel,
        grid=(3,),
        in_specs=[
            pl.BlockSpec(memory_space=pltpu.SMEM),
            pl.BlockSpec((tokens, width), lambda i: (0, 0)),
            pl.BlockSpec((tokens, step), lambda i: (0, i)),
        ],
        out_specs=[pl.BlockSpec((groups // 2, share, step), lambda i: (0, 0, i))] * 2,
        out_shape=[shape, shape],
        scratch_shapes=[pltpu.VMEM((width, tokens), BF16), pltpu.VMEM((width, step), BF16)],
        compiler_params=pltpu.CompilerParams(
            dimension_semantics=("arbitrary",), vmem_limit_bytes=56 * 2**20
        ),
        cost_estimate=pl.CostEstimate(flops=1, bytes_accessed=1, transcendentals=0),
    )(place, left.reshape(tokens, width), right.reshape(tokens, columns))


def pack(parts):
    total = sum(part.shape[1] for part in parts) // 128

    def kernel(*refs):
        at = 0
        for ref in refs[:-1]:
            for start in range(0, ref.shape[1], 128):
                refs[-1][at : at + 1, :] = ref[:, start : start + 128]
                at += 1

    return pl.pallas_call(
        kernel,
        in_specs=[pl.BlockSpec(memory_space=pltpu.VMEM)] * len(parts),
        out_specs=pl.BlockSpec(memory_space=pltpu.VMEM),
        out_shape=jax.ShapeDtypeStruct((total, 128), F32),
        cost_estimate=pl.CostEstimate(flops=1, bytes_accessed=1, transcendentals=0),
    )(*parts)


def unpack(place, lines, widths):
    total = lines[0].shape[1]

    def kernel(where, *refs):
        parts = [ref[...].astype(F32) for ref in refs[:4]]
        for owner in range(4):
            mine = jnp.zeros((1, total), F32)
            for spot, part in enumerate(parts):
                mine = jnp.where((where[0] ^ spot) == owner, part, mine)
            start = 0
            for ref, width in zip(refs[4:], widths):
                ref[:, owner * width : (owner + 1) * width] = mine[:, start : start + width]
                start += width

    return pl.pallas_call(
        kernel,
        in_specs=[pl.BlockSpec(memory_space=pltpu.SMEM)]
        + [pl.BlockSpec(memory_space=pltpu.VMEM)] * 4,
        out_specs=[pl.BlockSpec(memory_space=pltpu.VMEM)] * len(widths),
        out_shape=[jax.ShapeDtypeStruct((1, 4 * width), F32) for width in widths],
        cost_estimate=pl.CostEstimate(flops=1, bytes_accessed=1, transcendentals=0),
    )(place, *lines)


def query_body(at, where, blocked, whole, weights, outs, sums):
    gain, shift, bias = whole
    hat, _ = normed(blocked[0][0].astype(F32))
    low = (hat * gain[...] + shift[...]).astype(BF16)
    outs[0][0] = low
    width = low.shape[1]
    for part in range(3):
        cut = slice(part * width, (part + 1) * width)
        outs[1][0, :, cut] = (dot(low, weights[0][:, cut]) + bias[:, cut]).astype(BF16)


def attend_body(length, at, where, blocked, whole, weights, outs, sums):
    (packed,) = blocked
    rows = packed.shape[1]
    width = packed.shape[2] // 3
    lanes = 2 * width // HEADS
    factor = (width // HEADS) ** (-0.5)
    low_lane = lax.broadcasted_iota(jnp.int32, (rows, lanes), 1) < lanes // 2
    key_there = lax.broadcasted_iota(jnp.int32, (rows, rows), 1) < length
    for pair in range(HEADS // 2):
        start = pair * lanes
        query = packed[0, :, start : start + lanes] * jnp.asarray(factor, BF16)
        keys = packed[0, :, width + start : width + start + lanes]
        values = packed[0, :, 2 * width + start : 2 * width + start + lanes]
        both = []
        for side in range(2):
            mine = low_lane if side == 0 else jnp.logical_not(low_lane)
            scores = dot_nt(jnp.where(mine, query, jnp.zeros_like(query)), keys)
            scores = jnp.where(key_there, scores, -1e30)
            expo = jnp.exp(scores - jnp.max(scores, -1, keepdims=True))
            probs = expo * (1.0 / jnp.sum(expo, -1, keepdims=True))
            both.append(dot(probs.astype(BF16), values))
        outs[0][0, :, start : start + lanes] = jnp.where(low_lane, both[0], both[1]).astype(BF16)


def up_body(at, where, blocked, whole, weights, outs, sums):
    attended, images = blocked
    bias_out, gain, shift, bias_up = whole
    w_out, w_up = weights
    middle = images[0].astype(F32) + dot(attended[0], w_out[...]) + bias_out[...]
    outs[2][0] = middle
    hat, _ = normed(middle)
    low = (hat * gain[...] + shift[...]).astype(BF16)
    outs[3][0] = low
    inner = w_up.shape[1]
    width = low.shape[1]
    for start in range(0, inner, width):
        cut = slice(start, start + width)
        pre = dot(low, w_up[:, cut]) + bias_up[:, cut]
        square = pre * pre
        bend = jnp.tanh(pre * (GELU_A + (GELU_A * GELU_B) * square))
        half = 0.5 + 0.5 * bend
        outs[0][0, :, cut] = (pre * half).astype(BF16)
        slope = GELU_A + (3.0 * GELU_A * GELU_B) * square
        outs[1][0, :, cut] = (half + (0.5 * pre) * ((1.0 - bend * bend) * slope)).astype(BF16)


def pre_body(at, where, blocked, whole, weights, outs, sums):
    cotangent, slope = blocked
    grad_low = cotangent[0]
    width = grad_low.shape[1]
    for start in range(0, slope.shape[2], width):
        cut = slice(start, start + width)
        grad_pre = dot_nt(grad_low, weights[0][cut, :]) * slope[0, :, cut].astype(F32)
        low = grad_pre.astype(BF16)
        outs[0][0, :, cut] = low
        sums[0][:, cut] += column_sum(low)
    sums[1][...] += column_sum(grad_low)


def back_body(at, where, blocked, whole, weights, outs, sums):
    cotangent, grad_pre, middle = blocked
    (gain,) = whole
    w_up, w_out = weights
    grad_two = dot_nt(grad_pre[0], w_up[...])
    hat, scale = normed(middle[0])
    sums[0][...] += column_sum(grad_two * hat)
    sums[1][...] += column_sum(grad_two)
    grad_middle = cotangent[0].astype(F32) + norm_back(grad_two, gain[...], hat, scale)
    outs[0][0] = grad_middle
    low = grad_middle.astype(BF16)
    outs[1][0] = low
    sums[2][...] += column_sum(low)
    outs[2][0] = dot_nt(low, w_out[...]).astype(BF16)


def attend_back_body(length, pairs, at, where, blocked, whole, weights, outs, sums):
    packed, grads = blocked
    rows, width = grads.shape[1:]
    part = outs[0].shape[2] // 3
    lanes = 2 * width // HEADS
    factor = (width // HEADS) ** (-0.5)
    low_lane = lax.broadcasted_iota(jnp.int32, (rows, lanes), 1) < lanes // 2
    key_there = lax.broadcasted_iota(jnp.int32, (rows, rows), 0) < length
    for pair in pairs:
        start = pair * lanes
        first = (pair - pairs[0]) * lanes
        cuts = [slice(at * width + start, at * width + start + lanes) for at in range(3)]
        query, keys, values = (packed[0, :, cut] for cut in cuts)
        grad = grads[0, :, start : start + lanes]
        scaled = query * jnp.asarray(factor, BF16)
        results = []
        for side in range(2):
            mine = low_lane if side == 0 else jnp.logical_not(low_lane)
            scores = dot_nt(jnp.where(mine, keys, jnp.zeros_like(keys)), scaled)
            scores = jnp.where(key_there, scores, -1e30)
            expo = jnp.exp(scores - jnp.max(scores, 0, keepdims=True))
            probs = expo * (1.0 / jnp.sum(expo, 0, keepdims=True))
            grad_probs = dot_nt(jnp.where(mine, values, jnp.zeros_like(values)), grad)
            inner = jnp.sum(probs * grad_probs, 0, keepdims=True)
            grad_scores = (probs * (grad_probs - inner) * factor).astype(BF16)
            results.append(
                (
                    dot_tn(grad_scores, keys),
                    dot(grad_scores, query),
                    dot(probs.astype(BF16), grad),
                )
            )
        for kind in range(3):
            low = jnp.where(low_lane, results[0][kind], results[1][kind]).astype(BF16)
            cut = slice(kind * part + first, kind * part + first + lanes)
            outs[0][0, :, cut] = low
            sums[0][:, cut] += column_sum(low)


def input_body(length, at, where, blocked, whole, weights, outs, sums):
    *packed, images, grad_middle = blocked
    width = images.shape[2]
    grad_one = None
    start = 0
    for array in packed:
        part = array.shape[2] // 3
        for kind in range(3):
            weight = weights[0][:, kind * width + start : kind * width + start + part]
            term = dot_nt(array[0, :, kind * part : (kind + 1) * part], weight)
            grad_one = term if grad_one is None else grad_one + term
        start += part
    hat, scale = normed(images[0].astype(F32))
    sums[0][...] += column_sum(grad_one * hat)
    sums[1][...] += column_sum(grad_one)
    result = grad_middle[0] + norm_back(grad_one, whole[0][...], hat, scale)
    outs[0][0] = result[:length]


def down_body(length, at, where, blocked, whole, weights, outs, sums):
    hidden, middle = blocked
    result = middle[0] + dot(hidden[0], weights[0][...]) + whole[0][...]
    live = jnp.where(at < where[1], 1.0, 0.0).astype(F32)
    outs[0][0] = (result * live)[:length].astype(BF16)


def on_device(
    sizes,
    images,
    counts,
    ln1_gain,
    ln1_shift,
    w_qkv,
    b_query,
    b_value,
    w_out,
    b_out,
    ln2_gain,
    ln2_shift,
    w_up,
    b_up,
    w_down,
    b_down,
    cotangent,
):
    slots, length, width = images.shape
    inner = w_up.shape[1]
    rows = -(-length // 16) * 16
    vectors = (ln1_gain, ln1_shift, b_query, b_value, b_out, ln2_gain, ln2_shift, b_down, b_up)
    g_qkv = Gather(w_qkv, sizes, 1)
    g_out = Gather(w_out, sizes, 1)
    g_up = Gather(w_up, sizes, 2)
    g_down = Gather(w_down, sizes, 1)
    if g_qkv.split:
        g_qkv.out, vectors = fence(g_qkv.out, vectors)
    g_qkv.far()
    g_qkv.near()
    place = jnp.stack(
        [
            lax.axis_index("group"),
            counts[0],
            lax.axis_index("replica") & 1,
            (lax.axis_index("replica") >> 1) & 1,
        ]
    ).astype(jnp.int32)
    line = jnp.concatenate(vectors).reshape(1, -1)
    widths = [vector.shape[0] for vector in vectors]
    if sizes[0] == 4:
        far_line = swap(line, "group", 4, 2)
        near_line = swap(line, "group", 4, 1)
        far_near = swap(far_line, "group", 4, 1)
        small = unpack(place, (line, near_line, far_line, far_near), widths)
    else:
        gathered = lax.all_gather(line[0], "group", axis=0, tiled=False)
        small = []
        start = 0
        for size in widths:
            small.append(gathered[:, start : start + size].reshape(1, -1).astype(F32))
            start += size
    gain_one, shift_one, bias_query, bias_value, bias_out, gain_two, shift_two, bias_down, bias_up = small
    bias_cat = jnp.concatenate([bias_query, jnp.zeros_like(bias_query), bias_value], 1)
    live = (jnp.arange(slots, dtype=jnp.int32) < counts[0]).astype(BF16)[:, None, None]
    fill = ((0, 0), (0, rows - length), (0, 0))
    images = jnp.pad(images, fill)
    cotangent = jnp.pad(cotangent * live, fill)
    tokens = slots * rows


    def outer(left, right):
        left = left.reshape(tokens, -1)
        right = right.reshape(tokens, -1)
        return dot_tn(left, right).astype(BF16)

    def chain(left, right, halvings):
        if sizes[0] > 1 and is_power(sizes[0]) and is_power(sizes[1]):
            return Reduce(outer_halves(place, left, right, sizes[0]), sizes, halvings)
        return Reduce(outer(left, right), sizes, halvings)

    def hand_over(gather, name, carry):
        if gather.split:
            part, carry = fence(getattr(gather, name), carry)
            setattr(gather, name, part)
        return carry

    if g_qkv.split:
        g_qkv.first, g_out.out, g_up.out = fence(g_qkv.first, g_out.out, g_up.out)
    g_qkv.across()
    g_out.far()
    g_up.far()
    g_up.near()
    g_out.near()
    g_qkv.last()
    low_one, packed = per_image(
        query_body, place, [images], [gain_one, shift_one, bias_cat], [g_qkv],
        [(rows, width, BF16), (rows, 3 * width, BF16)], [],
    )
    packed = hand_over(g_out, "first", packed)
    packed = hand_over(g_up, "first", packed)
    if g_down.split:
        g_down.out, packed = fence(g_down.out, packed)
    g_out.across()
    g_up.across()
    g_down.far()
    g_down.near()
    (attended,) = per_image(
        functools.partial(attend_body, length), place, [packed], [], [],
        [(rows, width, BF16)], [],
    )
    attended = hand_over(g_out, "second", attended)
    attended = hand_over(g_up, "second", attended)
    attended = hand_over(g_down, "first", attended)
    g_out.last()
    g_up.last()
    g_down.across()
    hidden, slope, middle, low_two = per_image(
        up_body, place, [attended, images], [bias_out, gain_two, shift_two, bias_up],
        [g_out, g_up],
        [(rows, inner, BF16), (rows, inner, BF16), (rows, width, F32), (rows, width, BF16)],
        [],
    )
    hidden = hand_over(g_down, "second", hidden)
    g_down.last()
    down = Reduce(outer(hidden, cotangent), sizes, 2, True)
    grad_pre, grad_bup, grad_bdown = per_image(
        pre_body, place, [cotangent, slope], [], [g_down],
        [(rows, inner, BF16)], [inner, width],
    )
    up = Reduce(outer(low_two, grad_pre), sizes, 2, True)
    grad_middle, grad_branch, grad_att, grad_gain_two, grad_shift_two, grad_bout = per_image(
        back_body, place, [cotangent, grad_pre, middle], [gain_two], [g_up, g_out],
        [(rows, width, F32), (rows, width, BF16), (rows, width, BF16)],
        [width, width, width],
    )
    out = chain(attended, grad_branch, 2)
    grad_att = turn([], [down, out], grad_att)
    half = HEADS // 4
    grad_one, sums_one = per_image(
        functools.partial(attend_back_body, length, range(half)), place, [packed, grad_att],
        [], [], [(rows, 3 * width // 2, BF16)], [3 * width // 2],
    )
    qkv_one = chain(low_one, grad_one, 1)
    grad_att = turn([down, out], [down, out, qkv_one], grad_att)
    grad_two, sums_two = per_image(
        functools.partial(attend_back_body, length, range(half, 2 * half)), place,
        [packed, grad_att], [], [], [(rows, 3 * width // 2, BF16)], [3 * width // 2],
    )
    qkv_two = chain(low_one, grad_two, 1)
    grad_middle = turn(
        [down, out, qkv_one], [down, up, out, qkv_one, qkv_two], grad_middle
    )
    input_grad, grad_gain_one, grad_shift_one = per_image(
        functools.partial(input_body, length), place, [grad_one, grad_two, images, grad_middle],
        [gain_one], [g_qkv], [(length, width, F32)], [width, width],
    )
    part = width // 2
    parts = (
        grad_gain_one,
        grad_shift_one,
        sums_one[:, :part],
        sums_two[:, :part],
        sums_one[:, 2 * part :],
        sums_two[:, 2 * part :],
        grad_bout,
        grad_gain_two,
        grad_shift_two,
        grad_bdown,
        grad_bup,
    )
    little = Share(pack(parts), sizes)
    chains = [down, up, out, qkv_one, qkv_two]
    hidden = turn(chains, [little] + chains, hidden)
    (outputs,) = per_image(
        functools.partial(down_body, length), place, [hidden, middle], [bias_down], [g_down],
        [(length, width, BF16)], [],
    )
    for chain in [little] + chains:
        chain.drain()
    little = little.field.reshape(-1)
    sums = []
    start = 0
    for size in widths:
        mine = lax.axis_index("group") * size
        sums.append(lax.dynamic_slice(little, (start + mine,), (size,)))
        start += size * sizes[0]
    left, right = qkv_one.result(), qkv_two.result()
    grad_qkv = jnp.concatenate(
        [
            side[:, kind * width // 2 : (kind + 1) * width // 2]
            for kind in range(3)
            for side in (left, right)
        ],
        1,
    )
    big = [down.result(), up.result(), out.result(), grad_qkv]
    return (
        outputs,
        input_grad,
        sums[0],
        sums[1],
        big[3],
        sums[2],
        sums[3],
        big[2],
        sums[4],
        sums[5],
        sums[6],
        big[1],
        sums[8],
        big[0],
        sums[7],
    )


def solution(mesh):
    sizes = (mesh.shape["group"], mesh.shape["replica"])
    line = P("group")
    grid = P("group", None)
    field = P(("replica", "group"), None, None)
    return jax.shard_map(
        functools.partial(on_device, sizes),
        mesh=mesh,
        in_specs=(
            field, P(("replica", "group")), line, line, grid, line, line, grid, line, line, line,
            grid, line, grid, line, field,
        ),
        out_specs=(
            field, field, line, line, grid, line, line, grid, line, line, line, grid, line, grid,
            line,
        ),
        check_vma=False,
    )
```

```python
import functools

import jax
import jax.numpy as jnp
from jax import lax
from jax.experimental import pallas as pl
from jax.experimental.pallas import tpu as pltpu
from jax.sharding import PartitionSpec as P

HEADS = 12
F32 = jnp.float32
BF16 = jnp.bfloat16
GELU_A = 0.7978845608028654
GELU_B = 0.044715


def swap(field, axis, size, bit):
    return lax.ppermute(field, axis, [(at, at ^ bit) for at in range(size)])


def is_power(size):
    return size & (size - 1) == 0


def pick(field, at, axis):
    return lax.dynamic_index_in_dim(field, at, axis, keepdims=False)


def fence(*groups):
    return lax.optimization_barrier(groups)


class Gather:
    def __init__(self, shard, sizes, partner):
        self.groups, self.replicas = sizes
        self.shard = shard
        self.rows = shard.shape[0]
        self.hops = self.groups == 4 and self.rows % 32 == 0
        self.split = self.hops and partner and self.replicas % (2 * partner) == 0
        self.partner = partner
        if not self.hops:
            self.whole = lax.all_gather(shard, "group", axis=0, tiled=True)
        self.out = shard
        if self.split:
            half = (lax.axis_index("replica") // partner) & 1
            self.out = pick(shard.reshape(2, self.rows // 2, -1), half, 0)

    def near(self):
        if self.hops:
            self.beside = swap(self.shard, "group", 4, 1)

    def far(self):
        if self.hops:
            self.first = swap(self.out, "group", 4, 2)

    def across(self):
        if self.split:
            self.second = swap(self.first, "replica", self.replicas, self.partner)
        if self.hops:
            self.far_first = swap(self.first, "group", 4, 1)

    def last(self):
        if self.split:
            self.far_second = swap(self.second, "group", 4, 1)

    def pieces(self):
        if not self.hops:
            return (self.whole,)
        if not self.split:
            return (self.shard, self.beside, self.first, self.far_first)
        return (self.shard, self.beside, self.first, self.second, self.far_first, self.far_second)


def place_pieces(rows, pieces, me, half):
    if pieces == 1:
        return [0]
    if pieces == 4:
        return [(me ^ spot) * rows for spot in range(4)]
    part = rows // 2
    return [
        me * rows,
        (me ^ 1) * rows,
        (me ^ 2) * rows + half * part,
        (me ^ 2) * rows + (1 - half) * part,
        (me ^ 3) * rows + half * part,
        (me ^ 3) * rows + (1 - half) * part,
    ]


def add_low(left, right, kind):
    return (left.astype(F32) + right.astype(F32)).astype(kind)


class Share:
    def __init__(self, field, sizes):
        self.field = field
        self.flying = False
        self.hops = []
        if not (is_power(sizes[0]) and is_power(sizes[1])):
            self.field = lax.psum(field, ("replica", "group"))
            return
        for axis, size in zip(("group", "replica"), sizes):
            bit = 1
            while bit < size:
                self.hops.append((axis, size, bit))
                bit *= 2

    def outgoing(self):
        return self.field

    def launch(self, out):
        self.field = out
        self.came = swap(out, *self.hops.pop(0))
        self.flying = True

    def land(self, came):
        self.field = self.field + came
        self.flying = False

    def drain(self):
        while self.flying:
            self.land(self.came)
            if self.hops:
                self.launch(self.outgoing())


class Reduce:
    def __init__(self, grad, sizes, halvings, scatter=False):
        self.sizes = sizes
        self.ready = None
        self.kind = BF16
        groups, replicas = sizes
        self.hops = []
        self.flying = False
        if not (is_power(groups) and is_power(replicas)):
            shard = lax.psum_scatter(grad, "group", scatter_dimension=0, tiled=True)
            self.terms = [lax.psum(shard.astype(F32), "replica")]
            return
        if scatter:
            self.terms = [lax.psum_scatter(grad, "group", scatter_dimension=0, tiled=True)]
        else:
            self.ready = grad
            bit = 1
            while bit < groups:
                self.hops.append(("group", bit, "split"))
                bit *= 2
        bit = 1
        back = []
        while bit < replicas:
            if len(back) < halvings:
                self.hops.append(("replica", bit, "halve"))
                back.append(("replica", bit, "back"))
            else:
                self.hops.append(("replica", bit, "whole"))
            bit *= 2
        self.hops += reversed(back)

    def total(self, parts=None, kind=None):
        parts = self.terms if parts is None else parts
        if len(parts) == 1:
            return parts[0].astype(kind or self.kind)
        return sum(part.astype(F32) for part in parts).astype(kind or self.kind)

    def outgoing(self):
        if self.ready:
            out, keep = self.ready
            self.ready, self.keep = None, [keep]
            return out
        axis, bit, kind = self.hops[0]
        side = (lax.axis_index(axis) // bit) & 1
        if kind == "split":
            shape = self.terms[0].shape
            pairs = [term.reshape((shape[0] // 2, 2) + shape[1:]) for term in self.terms]
            self.keep = [pick(term, side, 1) for term in pairs]
            if shape[0] == 2:
                self.keep = [term[0] for term in self.keep]
            return self.total([pick(term, 1 - side, 1) for term in pairs])
        if kind == "halve":
            shape = self.terms[0].shape
            pairs = [term.reshape((2, shape[0] // 2) + shape[1:]) for term in self.terms]
            self.keep = [pick(term, side, 0) for term in pairs]
            return self.total([pick(term, 1 - side, 0) for term in pairs])
        return self.total()

    def launch(self, out):
        axis, bit, kind = self.hops.pop(0)
        size = self.sizes[0] if axis == "group" else self.sizes[1]
        self.came = swap(out, axis, size, bit)
        side = (lax.axis_index(axis) // bit) & 1
        if kind in ("split", "halve"):
            self.held = self.total(self.keep)
            if kind == "split" and out.shape[0] == 1 and self.held.ndim == out.ndim:
                self.held = self.held[0]
        else:
            self.held = out
        self.kind_of_hop, self.side = kind, side
        self.flying = True

    def land(self, came):
        self.flying = False
        if self.kind_of_hop == "back":
            held = self.held
            self.terms = [
                jnp.where(
                    self.side == 0,
                    jnp.concatenate([held, came]),
                    jnp.concatenate([came, held]),
                )
            ]
            return
        if self.kind_of_hop == "split" and self.held.ndim < came.ndim:
            came = came[0]
        self.terms = [self.held, came]

    def drain(self):
        while self.flying:
            self.land(self.came)
            if self.hops:
                self.launch(self.outgoing())

    def result(self):
        return self.total(kind=F32)


def turn(landing, launching, carry, quick=()):
    landing = [chain for chain in landing if chain.flying]
    came, carry = fence([chain.came for chain in landing], carry)
    for chain, part in zip(landing, came):
        chain.land(part)
    for chain in quick:
        out, carry = fence(chain.outgoing(), carry)
        chain.launch(out)
    launching = [chain for chain in launching if chain.hops]
    outs, carry = fence([chain.outgoing() for chain in launching], carry)
    for chain, out in zip(launching, outs):
        chain.launch(out)
    for chain in quick:
        came, outs, carry = fence(chain.came, outs, carry)
        chain.land(came)
        out, carry = fence(chain.outgoing(), carry)
        chain.launch(out)
    return carry


def dot(left, right):
    return lax.dot_general(left, right, (((1,), (0,)), ((), ())), preferred_element_type=F32)


def dot_nt(left, right):
    return lax.dot_general(left, right, (((1,), (1,)), ((), ())), preferred_element_type=F32)


def dot_tn(left, right):
    return lax.dot_general(left, right, (((0,), (0,)), ((), ())), preferred_element_type=F32)


def per_image(body, place, blocked, whole, weights, outs, sums, span=None, into=None):
    slots = blocked[0].shape[0]
    first, last = span or (0, slots)
    halves = [1 + (gather.partner or 1) for gather in weights]
    weights = [gather.pieces() for gather in weights]
    counts = [len(pieces) for pieces in weights]
    rows_of = [pieces[0].shape[0] for pieces in weights]
    total = [rows * (4 if len(pieces) > 1 else 1) for rows, pieces in zip(rows_of, weights)]

    def kernel(*refs):
        refs = list(refs)

        def take(count):
            taken = refs[:count]
            del refs[:count]
            return taken

        (where,) = take(1)
        blocked_refs = take(len(blocked))
        whole_refs = take(len(whole))
        piece_refs = [take(count) for count in counts]
        take(0 if into is None else 1)
        out_refs = take(len(outs))
        sum_refs = take(len(sums))
        weight_refs = take(len(weights))
        at = pl.program_id(0)

        @pl.when(at == 0)
        def _():
            copies = []
            for index, pieces in enumerate(piece_refs):
                starts = place_pieces(rows_of[index], len(pieces), where[0], where[halves[index]])
                for spot, (piece, start) in enumerate(zip(pieces, starts)):
                    target = weight_refs[index].at[pl.ds(pl.multiple_of(start, 16), piece.shape[0])]
                    copies.append(pltpu.make_async_copy(piece, target, refs[0].at[index, spot]))
            for copy in copies:
                copy.start()
            for ref in sum_refs:
                ref[...] = jnp.zeros_like(ref)
            for copy in copies:
                copy.wait()

        body(at + first, where, blocked_refs, whole_refs, weight_refs, out_refs, sum_refs)

    in_specs = [pl.BlockSpec(memory_space=pltpu.SMEM)]
    for array in blocked:
        in_specs.append(pl.BlockSpec((1,) + array.shape[1:], lambda i: (i + first, 0, 0)))
    for array in whole:
        in_specs.append(pl.BlockSpec(array.shape, lambda i: (0, 0)))
    pieces = [piece for parts in weights for piece in parts]
    extra = [] if into is None else [into]
    in_specs += [pl.BlockSpec(memory_space=pltpu.HBM)] * (len(pieces) + len(extra))
    out_specs = [
        pl.BlockSpec((1, rows, columns), lambda i: (i + first, 0, 0)) for rows, columns, _ in outs
    ]
    out_specs += [pl.BlockSpec((1, columns), lambda i: (0, 0)) for columns in sums]
    shapes = [jax.ShapeDtypeStruct((slots, rows, columns), kind) for rows, columns, kind in outs]
    shapes += [jax.ShapeDtypeStruct((1, columns), F32) for columns in sums]
    scratch = [
        pltpu.VMEM((rows, parts[0].shape[1]), BF16) for rows, parts in zip(total, weights)
    ]
    if weights:
        scratch.append(pltpu.SemaphoreType.DMA((len(weights), 6)))
    return pl.pallas_call(
        kernel,
        grid=(last - first,),
        in_specs=in_specs,
        out_specs=out_specs,
        input_output_aliases={len(in_specs) - 1: 0} if extra else {},
        out_shape=shapes,
        scratch_shapes=scratch,
        compiler_params=pltpu.CompilerParams(
            dimension_semantics=("arbitrary",), vmem_limit_bytes=56 * 2**20
        ),
        cost_estimate=pl.CostEstimate(flops=1, bytes_accessed=1, transcendentals=0),
    )(place, *blocked, *whole, *pieces, *extra)


def normed(field):
    centred = field - jnp.mean(field, -1, keepdims=True)
    scale = lax.rsqrt(jnp.mean(centred * centred, -1, keepdims=True) + 1e-06)
    return centred * scale, scale


def norm_back(grad, gain, hat, scale):
    inner = grad * gain
    mean = jnp.mean(inner, -1, keepdims=True)
    along = jnp.mean(inner * hat, -1, keepdims=True)
    return scale * (inner - mean - hat * along)


def column_sum(field):
    return jnp.sum(field.astype(F32), 0, keepdims=True)


def outer_halves(place, pairs, groups, step):
    slots, rows, width = pairs[0][0].shape
    tokens = slots * rows
    share = width // groups
    columns = sum(right.shape[2] for _, right in pairs)
    bounds = [0]
    for _, right in pairs:
        bounds.append(bounds[-1] + right.shape[2] // step)

    def kernel(where, *refs):
        lefts, rights = refs[: len(pairs)], refs[len(pairs) : 2 * len(pairs)]
        send_ref, keep_ref, total = refs[2 * len(pairs) :]
        at = pl.program_id(0)
        for left, right, first, last in zip(lefts, rights, bounds, bounds[1:]):

            @pl.when((at >= first) & (at < last))
            def _(left=left, right=right):
                total[...] = dot_tn(left[...], right[...]).astype(BF16)

        side = where[0] & 1
        for spot in range(groups // 2):
            for ref, mine in ((send_ref, 1 - side), (keep_ref, side)):
                start = pl.multiple_of((2 * spot + mine) * share, 16)
                ref[spot] = total[pl.ds(start, share), :]

    def column_map(first, last):
        return lambda i: (0, jnp.clip(i - first, 0, last - first - 1))

    shape = jax.ShapeDtypeStruct((groups // 2, share, columns), BF16)
    return pl.pallas_call(
        kernel,
        grid=(bounds[-1],),
        in_specs=[pl.BlockSpec(memory_space=pltpu.SMEM)]
        + [pl.BlockSpec((tokens, width), lambda i: (0, 0))] * len(pairs)
        + [
            pl.BlockSpec((tokens, step), column_map(first, last))
            for first, last in zip(bounds, bounds[1:])
        ],
        out_specs=[pl.BlockSpec((groups // 2, share, step), lambda i: (0, 0, i))] * 2,
        out_shape=[shape, shape],
        scratch_shapes=[pltpu.VMEM((width, step), BF16)],
        compiler_params=pltpu.CompilerParams(
            dimension_semantics=("arbitrary",), vmem_limit_bytes=56 * 2**20
        ),
        cost_estimate=pl.CostEstimate(flops=1, bytes_accessed=1, transcendentals=0),
    )(
        place,
        *[left.reshape(tokens, width) for left, _ in pairs],
        *[right.reshape(tokens, -1) for _, right in pairs],
    )


def prepare(place, images, cotangent, rows):
    slots, length, width = images.shape

    def kernel(where, images_ref, cotangent_ref, images_out, cotangent_out):
        live = jnp.where(pl.program_id(0) < where[1], 1.0, 0.0).astype(BF16)
        empty = jnp.zeros((rows - length // 16 * 16, width), BF16)
        for ref, scale, out in (
            (images_ref, None, images_out),
            (cotangent_ref, live, cotangent_out),
        ):
            out[0, length // 16 * 16 :, :] = empty
            value = ref[0] if scale is None else ref[0] * scale
            out[0, :length, :] = value

    shape = jax.ShapeDtypeStruct((slots, rows, width), BF16)
    block = pl.BlockSpec((1, length, width), lambda i: (i, 0, 0))
    padded = pl.BlockSpec((1, rows, width), lambda i: (i, 0, 0))
    return pl.pallas_call(
        kernel,
        grid=(slots,),
        in_specs=[pl.BlockSpec(memory_space=pltpu.SMEM), block, block],
        out_specs=[padded, padded],
        out_shape=[shape, shape],
        compiler_params=pltpu.CompilerParams(dimension_semantics=("arbitrary",)),
        cost_estimate=pl.CostEstimate(flops=1, bytes_accessed=16 * 2**20, transcendentals=0),
    )(place, images, cotangent)


def pack(parts):
    total = sum(part.shape[1] for part in parts) // 128

    def kernel(*refs):
        at = 0
        for ref in refs[:-1]:
            for start in range(0, ref.shape[1], 128):
                refs[-1][at : at + 1, :] = ref[:, start : start + 128]
                at += 1

    return pl.pallas_call(
        kernel,
        in_specs=[pl.BlockSpec(memory_space=pltpu.VMEM)] * len(parts),
        out_specs=pl.BlockSpec(memory_space=pltpu.VMEM),
        out_shape=jax.ShapeDtypeStruct((total, 128), F32),
        cost_estimate=pl.CostEstimate(flops=1, bytes_accessed=1, transcendentals=0),
    )(*parts)


def unpack(place, lines, spots):
    count, unit = lines[0].shape
    sizes = {}
    for rows, out, column in spots:
        sizes[out] = max(sizes.get(out, 0), column + 4 * rows * unit)

    def kernel(where, *refs):
        outs = refs[4:]
        parts = [ref[...].astype(F32) for ref in refs[:4]]
        for ref in outs:
            ref[...] = jnp.zeros_like(ref)
        for owner in range(4):
            mine = jnp.zeros((count, unit), F32)
            for spot, part in enumerate(parts):
                mine = jnp.where((where[0] ^ spot) == owner, part, mine)
            row = 0
            for rows, out, column in spots:
                for at in range(rows):
                    start = column + (owner * rows + at) * unit
                    outs[out][:, start : start + unit] = mine[row : row + 1]
                    row += 1

    return pl.pallas_call(
        kernel,
        in_specs=[pl.BlockSpec(memory_space=pltpu.SMEM)]
        + [pl.BlockSpec(memory_space=pltpu.VMEM)] * 4,
        out_specs=[pl.BlockSpec(memory_space=pltpu.VMEM)] * len(sizes),
        out_shape=[jax.ShapeDtypeStruct((1, sizes[at]), F32) for at in range(len(sizes))],
        cost_estimate=pl.CostEstimate(flops=1, bytes_accessed=6 * 2**20, transcendentals=0),
    )(place, *lines)


def query_body(at, where, blocked, whole, weights, outs, sums):
    gain, shift, bias = whole
    hat, _ = normed(blocked[0][0].astype(F32))
    low = (hat * gain[...] + shift[...]).astype(BF16)
    outs[0][0] = low
    width = low.shape[1]
    for part in range(3):
        cut = slice(part * width, (part + 1) * width)
        outs[1][0, :, cut] = (dot(low, weights[0][:, cut]) + bias[:, cut]).astype(BF16)


def attend_body(length, at, where, blocked, whole, weights, outs, sums):
    (packed,) = blocked
    rows = packed.shape[1]
    width = packed.shape[2] // 3
    lanes = 2 * width // HEADS
    factor = (width // HEADS) ** (-0.5)
    low_lane = lax.broadcasted_iota(jnp.int32, (rows, lanes), 1) < lanes // 2
    key_there = lax.broadcasted_iota(jnp.int32, (rows, rows), 1) < length
    for pair in range(HEADS // 2):
        start = pair * lanes
        query = packed[0, :, start : start + lanes] * jnp.asarray(factor, BF16)
        keys = packed[0, :, width + start : width + start + lanes]
        values = packed[0, :, 2 * width + start : 2 * width + start + lanes]
        both = []
        for side in range(2):
            mine = low_lane if side == 0 else jnp.logical_not(low_lane)
            scores = dot_nt(jnp.where(mine, query, jnp.zeros_like(query)), keys)
            scores = jnp.where(key_there, scores, -1e30)
            expo = jnp.exp(scores - jnp.max(scores, -1, keepdims=True))
            probs = expo * (1.0 / jnp.sum(expo, -1, keepdims=True))
            both.append(dot(probs.astype(BF16), values))
        outs[0][0, :, start : start + lanes] = jnp.where(low_lane, both[0], both[1]).astype(BF16)


def up_body(at, where, blocked, whole, weights, outs, sums):
    attended, images = blocked
    bias_out, gain, shift, bias_up = whole
    w_out, w_up = weights
    middle = images[0].astype(F32) + dot(attended[0], w_out[...]) + bias_out[...]
    outs[2][0] = middle
    hat, _ = normed(middle)
    low = (hat * gain[...] + shift[...]).astype(BF16)
    outs[3][0] = low
    inner = w_up.shape[1]
    width = low.shape[1]
    for start in range(0, inner, width):
        cut = slice(start, start + width)
        pre = dot(low, w_up[:, cut]) + bias_up[:, cut]
        square = pre * pre
        bend = jnp.tanh(pre * (GELU_A + (GELU_A * GELU_B) * square))
        half = 0.5 + 0.5 * bend
        outs[0][0, :, cut] = (pre * half).astype(BF16)
        slope = GELU_A + (3.0 * GELU_A * GELU_B) * square
        outs[1][0, :, cut] = (half + (0.5 * pre) * ((1.0 - bend * bend) * slope)).astype(BF16)


def pre_body(at, where, blocked, whole, weights, outs, sums):
    cotangent, slope = blocked
    grad_low = cotangent[0]
    width = grad_low.shape[1]
    for start in range(0, slope.shape[2], width):
        cut = slice(start, start + width)
        grad_pre = dot_nt(grad_low, weights[0][cut, :]) * slope[0, :, cut].astype(F32)
        low = grad_pre.astype(BF16)
        outs[0][0, :, cut] = low
        sums[0][:, cut] += column_sum(low)
    sums[1][...] += column_sum(grad_low)


def back_body(at, where, blocked, whole, weights, outs, sums):
    cotangent, grad_pre, middle = blocked
    (gain,) = whole
    w_up, w_out = weights
    grad_two = dot_nt(grad_pre[0], w_up[...])
    hat, scale = normed(middle[0])
    sums[0][...] += column_sum(grad_two * hat)
    sums[1][...] += column_sum(grad_two)
    grad_middle = cotangent[0].astype(F32) + norm_back(grad_two, gain[...], hat, scale)
    outs[0][0] = grad_middle
    low = grad_middle.astype(BF16)
    outs[1][0] = low
    sums[2][...] += column_sum(low)
    outs[2][0] = dot_nt(low, w_out[...]).astype(BF16)


def attend_back_body(length, pairs, at, where, blocked, whole, weights, outs, sums):
    packed, grads = blocked
    rows, width = grads.shape[1:]
    part = outs[0].shape[2] // 3
    lanes = 2 * width // HEADS
    factor = (width // HEADS) ** (-0.5)
    low_lane = lax.broadcasted_iota(jnp.int32, (rows, lanes), 1) < lanes // 2
    key_there = lax.broadcasted_iota(jnp.int32, (rows, rows), 0) < length
    for pair in pairs:
        start = pair * lanes
        first = (pair - pairs[0]) * lanes
        cuts = [slice(at * width + start, at * width + start + lanes) for at in range(3)]
        query, keys, values = (packed[0, :, cut] for cut in cuts)
        grad = grads[0, :, start : start + lanes]
        scaled = query * jnp.asarray(factor, BF16)
        results = []
        for side in range(2):
            mine = low_lane if side == 0 else jnp.logical_not(low_lane)
            scores = dot_nt(jnp.where(mine, keys, jnp.zeros_like(keys)), scaled)
            scores = jnp.where(key_there, scores, -1e30)
            expo = jnp.exp(scores - jnp.max(scores, 0, keepdims=True))
            probs = expo * (1.0 / jnp.sum(expo, 0, keepdims=True))
            grad_probs = dot_nt(jnp.where(mine, values, jnp.zeros_like(values)), grad)
            inner = jnp.sum(probs * grad_probs, 0, keepdims=True)
            grad_scores = (probs * (grad_probs - inner) * factor).astype(BF16)
            results.append(
                (
                    dot_tn(grad_scores, keys),
                    dot(grad_scores, query),
                    dot(probs.astype(BF16), grad),
                )
            )
        for kind in range(3):
            low = jnp.where(low_lane, results[0][kind], results[1][kind]).astype(BF16)
            cut = slice(kind * part + first, kind * part + first + lanes)
            outs[0][0, :, cut] = low
            sums[0][:, cut] += column_sum(low)


def input_body(length, at, where, blocked, whole, weights, outs, sums):
    *packed, images, grad_middle = blocked
    width = images.shape[2]
    grad_one = None
    start = 0
    for array in packed:
        part = array.shape[2] // 3
        for kind in range(3):
            weight = weights[0][:, kind * width + start : kind * width + start + part]
            term = dot_nt(array[0, :, kind * part : (kind + 1) * part], weight)
            grad_one = term if grad_one is None else grad_one + term
        start += part
    hat, scale = normed(images[0].astype(F32))
    sums[0][...] += column_sum(grad_one * hat)
    sums[1][...] += column_sum(grad_one)
    result = grad_middle[0] + norm_back(grad_one, whole[0][...], hat, scale)
    outs[0][0] = result[:length]


def down_body(length, at, where, blocked, whole, weights, outs, sums):
    hidden, middle = blocked
    result = middle[0] + dot(hidden[0], weights[0][...]) + whole[0][...]
    live = jnp.where(at < where[1], 1.0, 0.0).astype(F32)
    outs[0][0] = (result * live)[:length].astype(BF16)


def on_device(
    sizes,
    images,
    counts,
    ln1_gain,
    ln1_shift,
    w_qkv,
    b_query,
    b_value,
    w_out,
    b_out,
    ln2_gain,
    ln2_shift,
    w_up,
    b_up,
    w_down,
    b_down,
    cotangent,
):
    slots, length, width = images.shape
    inner = w_up.shape[1]
    rows = -(-length // 16) * 16
    vectors = (ln1_gain, ln1_shift, b_query, b_value, b_out, ln2_gain, ln2_shift, b_down, b_up)
    g_qkv = Gather(w_qkv, sizes, 1)
    g_out = Gather(w_out, sizes, 0)
    g_up = Gather(w_up, sizes, 2)
    g_down = Gather(w_down, sizes, 0)
    if g_qkv.split:
        g_qkv.out, vectors = fence(g_qkv.out, vectors)
    g_qkv.far()
    g_qkv.near()
    place = jnp.stack(
        [
            lax.axis_index("group"),
            counts[0],
            lax.axis_index("replica") & 1,
            (lax.axis_index("replica") >> 1) & 1,
        ]
    ).astype(jnp.int32)
    widths = [vector.shape[0] for vector in vectors]
    unit = min(widths)
    at = jnp.arange(sum(widths) // unit)[:, None]
    line = jnp.zeros((sum(widths) // unit, unit), BF16)
    row = 0
    for vector in vectors:
        if vector.shape[0] == unit:
            line = jnp.where(at == row, vector[None, :], line)
        else:
            count = vector.shape[0] // unit
            fill = ((row, line.shape[0] - row - count), (0, 0))
            line = line + jnp.pad(vector.reshape(count, unit), fill)
        row += vector.shape[0] // unit
    if sizes[0] == 4:
        far_line = swap(line, "group", 4, 2)
        near_line = swap(line, "group", 4, 1)
        far_near = swap(far_line, "group", 4, 1)
        spots = []
        for at, size in enumerate(widths):
            out, column = (2, 2 * width) if at == 3 else (at - (at > 3), 0)
            spots.append((size // unit, out, column))
        small = unpack(place, (line, near_line, far_line, far_near), spots)
    else:
        gathered = lax.all_gather(line.reshape(-1), "group", axis=0, tiled=False)
        small = []
        start = 0
        for size in widths:
            small.append(gathered[:, start : start + size].reshape(1, -1).astype(F32))
            start += size
        small[2:4] = [jnp.concatenate([small[2], jnp.zeros_like(small[2]), small[3]], 1)]
    images, cotangent = prepare(place, images, cotangent, rows)
    tokens = slots * rows

    def outer(left, right):
        left = left.reshape(tokens, -1)
        right = right.reshape(tokens, -1)
        return dot_tn(left, right).astype(BF16)

    def chain(pairs, halvings, step):
        if sizes[0] > 1 and is_power(sizes[0]) and is_power(sizes[1]):
            return Reduce(outer_halves(place, pairs, sizes[0], step), sizes, halvings)
        return Reduce(jnp.concatenate([outer(*pair) for pair in pairs], 1), sizes, halvings)

    def hand_over(gather, name, carry):
        if gather.hops:
            part, carry = fence(getattr(gather, name), carry)
            setattr(gather, name, part)
        return carry

    if g_qkv.split:
        g_qkv.first, far_line, g_out.out, g_up.out = fence(
            g_qkv.first, far_line, g_out.out, g_up.out
        )
    g_qkv.across()
    g_up.far()
    if g_qkv.split:
        g_qkv.second, small, images, cotangent = fence(g_qkv.second, small, images, cotangent)
    g_qkv.last()
    g_out.far()
    gain_one, shift_one, bias_cat, bias_out, gain_two, shift_two, bias_down, bias_up = small
    images = hand_over(g_up, "first", images)
    g_up.across()
    low_one, packed = per_image(
        query_body, place, [images], [gain_one, shift_one, bias_cat], [g_qkv],
        [(rows, width, BF16), (rows, 3 * width, BF16)], [],
    )
    packed = hand_over(g_out, "first", packed)
    g_out.shard, g_up.shard, g_down.shard, g_down.out, packed = fence(
        g_out.shard, g_up.shard, g_down.shard, g_down.out, packed
    )
    g_out.across()
    g_down.far()
    g_out.near()
    g_up.near()
    g_down.near()
    (attended,) = per_image(
        functools.partial(attend_body, length), place, [packed], [], [],
        [(rows, width, BF16)], [],
    )
    if g_up.split:
        attended = hand_over(g_up, "second", attended)
    g_up.last()
    hidden, slope, middle, low_two = per_image(
        up_body, place, [attended, images], [bias_out, gain_two, shift_two, bias_up],
        [g_out, g_up],
        [(rows, inner, BF16), (rows, inner, BF16), (rows, width, F32), (rows, width, BF16)],
        [],
    )
    hidden = hand_over(g_down, "first", hidden)
    g_down.across()
    down, slope = fence(outer(hidden, cotangent), slope)
    down = Reduce(down, sizes, 2, True)
    grad_pre, grad_bup, grad_bdown = per_image(
        pre_body, place, [cotangent, slope], [], [g_down],
        [(rows, inner, BF16)], [inner, width],
    )
    up = chain([(low_two, grad_pre)], 2, inner // 4)
    grad_pre = turn([], [up], grad_pre)
    grad_middle, grad_branch, grad_att, grad_gain_two, grad_shift_two, grad_bout = per_image(
        back_body, place, [cotangent, grad_pre, middle], [gain_two], [g_up, g_out],
        [(rows, width, F32), (rows, width, BF16), (rows, width, BF16)],
        [width, width, width],
    )
    grad_att = turn([up], [up, down], grad_att)
    half = HEADS // 4
    part = width // 2
    grad_one, sums_one = per_image(
        functools.partial(attend_back_body, length, range(half)), place, [packed, grad_att],
        [], [], [(rows, 3 * part, BF16)], [3 * part],
    )
    one = chain([(low_one, grad_one), (attended, grad_branch)], 1, part)
    grad_att = turn([up, down], [up, down], grad_att, [one])
    grad_two, sums_two = per_image(
        functools.partial(attend_back_body, length, range(half, 2 * half)), place,
        [packed, grad_att], [], [], [(rows, 3 * part, BF16)], [3 * part],
    )
    two = chain([(low_one, grad_two)], 1, part)
    grad_middle = turn([one, up, down], [one, up, down], grad_middle, [two])
    input_grad, grad_gain_one, grad_shift_one = per_image(
        functools.partial(input_body, length), place, [grad_one, grad_two, images, grad_middle],
        [gain_one], [g_qkv], [(length, width, F32)], [width, width],
    )
    parts = (
        grad_gain_one,
        grad_shift_one,
        sums_one[:, :part],
        sums_two[:, :part],
        sums_one[:, 2 * part :],
        sums_two[:, 2 * part :],
        grad_bout,
        grad_gain_two,
        grad_shift_two,
        grad_bdown,
        grad_bup,
    )
    little = Share(pack(parts), sizes)
    chains = [two, up, one, down, little]
    hidden = turn(chains[:-1], chains, hidden)
    outputs = None
    for span in ((0, slots // 2), (slots // 2, slots)):
        (outputs,) = per_image(
            functools.partial(down_body, length), place, [hidden, middle], [bias_down], [g_down],
            [(length, width, BF16)], [], span, outputs,
        )
        outputs = turn(chains, chains, outputs)
    for item in chains:
        item.drain()
    little = little.field.reshape(-1)
    sums = []
    start = 0
    for size in widths:
        mine = lax.axis_index("group") * size
        sums.append(lax.dynamic_slice(little, (start + mine,), (size,)))
        start += size * sizes[0]
    one, two = one.result(), two.result()
    grad_qkv = jnp.concatenate(
        [side[:, kind * part : (kind + 1) * part] for kind in range(3) for side in (one, two)], 1
    )
    big = [down.result(), up.result(), one[:, 3 * part :], grad_qkv]
    return (
        outputs,
        input_grad,
        sums[0],
        sums[1],
        big[3],
        sums[2],
        sums[3],
        big[2],
        sums[4],
        sums[5],
        sums[6],
        big[1],
        sums[8],
        big[0],
        sums[7],
    )


def solution(mesh):
    sizes = (mesh.shape["group"], mesh.shape["replica"])
    line = P("group")
    grid = P("group", None)
    field = P(("replica", "group"), None, None)
    return jax.shard_map(
        functools.partial(on_device, sizes),
        mesh=mesh,
        in_specs=(
            field, P(("replica", "group")), line, line, grid, line, line, grid, line, line, line,
            grid, line, grid, line, field,
        ),
        out_specs=(
            field, field, line, line, grid, line, line, grid, line, line, line, grid, line, grid,
            line,
        ),
        check_vma=False,
    )
```

```python
import functools

import jax
import jax.numpy as jnp
from jax import lax
from jax.experimental import pallas as pl
from jax.experimental.pallas import tpu as pltpu
from jax.sharding import PartitionSpec as P

HEADS = 12
GROUP = 3
F32 = jnp.float32
BF16 = jnp.bfloat16
GELU_A = 0.7978845608028654
GELU_B = 0.044715


def swap(field, axis, size, bit):
    return lax.ppermute(field, axis, [(at, at ^ bit) for at in range(size)])


def is_power(size):
    return size & (size - 1) == 0


def pick(field, at, axis):
    return lax.dynamic_index_in_dim(field, at, axis, keepdims=False)


def fence(*groups):
    return lax.optimization_barrier(groups)


class Gather:
    def __init__(self, shard, sizes, partner):
        self.groups, self.replicas = sizes
        self.shard = shard
        self.rows = shard.shape[0]
        self.hops = self.groups == 4 and self.rows % 32 == 0
        self.split = self.hops and partner and self.replicas % (2 * partner) == 0
        self.partner = partner
        if not self.hops:
            self.whole = lax.all_gather(shard, "group", axis=0, tiled=True)
        self.out = shard
        if self.split:
            half = (lax.axis_index("replica") // partner) & 1
            self.out = pick(shard.reshape(2, self.rows // 2, -1), half, 0)

    def near(self):
        if self.hops:
            self.beside = swap(self.shard, "group", 4, 1)

    def far(self):
        if self.hops:
            self.first = swap(self.out, "group", 4, 2)

    def across(self):
        if self.split:
            self.second = swap(self.first, "replica", self.replicas, self.partner)
        if self.hops:
            self.far_first = swap(self.first, "group", 4, 1)

    def last(self):
        if self.split:
            self.far_second = swap(self.second, "group", 4, 1)

    def pieces(self):
        if not self.hops:
            return (self.whole,)
        if not self.split:
            return (self.shard, self.beside, self.first, self.far_first)
        return (self.shard, self.beside, self.first, self.second, self.far_first, self.far_second)


def place_pieces(rows, pieces, me, half):
    if pieces == 1:
        return [0]
    if pieces == 4:
        return [(me ^ spot) * rows for spot in range(4)]
    part = rows // 2
    return [
        me * rows,
        (me ^ 1) * rows,
        (me ^ 2) * rows + half * part,
        (me ^ 2) * rows + (1 - half) * part,
        (me ^ 3) * rows + half * part,
        (me ^ 3) * rows + (1 - half) * part,
    ]


def add_low(left, right, kind):
    return (left.astype(F32) + right.astype(F32)).astype(kind)


class Share:
    def __init__(self, field, sizes):
        self.field = field
        self.flying = False
        self.hops = []
        if not (is_power(sizes[0]) and is_power(sizes[1])):
            self.field = lax.psum(field, ("replica", "group"))
            return
        for axis, size in zip(("group", "replica"), sizes):
            bit = 1
            while bit < size:
                self.hops.append((axis, size, bit))
                bit *= 2

    def outgoing(self):
        return self.field

    def launch(self, out):
        self.field = out
        self.came = swap(out, *self.hops.pop(0))
        self.flying = True

    def land(self, came):
        self.field = self.field + came
        self.flying = False

    def drain(self):
        while self.flying or self.hops:
            if not self.flying:
                self.launch(self.outgoing())
            self.land(self.came)


class Reduce:
    def __init__(self, grad, sizes, halvings, scatter=False):
        self.sizes = sizes
        self.ready = None
        self.kind = BF16
        groups, replicas = sizes
        self.hops = []
        self.flying = False
        if not (is_power(groups) and is_power(replicas)):
            shard = lax.psum_scatter(grad, "group", scatter_dimension=0, tiled=True)
            self.terms = [lax.psum(shard.astype(F32), "replica")]
            return
        if scatter:
            self.terms = [lax.psum_scatter(grad, "group", scatter_dimension=0, tiled=True)]
        else:
            self.ready = grad
            bit = 1
            while bit < groups:
                self.hops.append(("group", bit, "split"))
                bit *= 2
        bit = 1
        back = []
        while bit < replicas:
            if len(back) < halvings:
                self.hops.append(("replica", bit, "halve"))
                back.append(("replica", bit, "back"))
            else:
                self.hops.append(("replica", bit, "whole"))
            bit *= 2
        self.hops += reversed(back)

    def total(self, parts=None, kind=None):
        parts = self.terms if parts is None else parts
        if len(parts) == 1:
            return parts[0].astype(kind or self.kind)
        return sum(part.astype(F32) for part in parts).astype(kind or self.kind)

    def outgoing(self):
        if self.ready:
            out, keep = self.ready
            self.ready, self.keep = None, [keep]
            return out
        axis, bit, kind = self.hops[0]
        side = (lax.axis_index(axis) // bit) & 1
        if kind == "split":
            shape = self.terms[0].shape
            pairs = [term.reshape((shape[0] // 2, 2) + shape[1:]) for term in self.terms]
            self.keep = [pick(term, side, 1) for term in pairs]
            if shape[0] == 2:
                self.keep = [term[0] for term in self.keep]
            return self.total([pick(term, 1 - side, 1) for term in pairs])
        if kind == "halve":
            shape = self.terms[0].shape
            pairs = [term.reshape((2, shape[0] // 2) + shape[1:]) for term in self.terms]
            self.keep = [pick(term, side, 0) for term in pairs]
            return self.total([pick(term, 1 - side, 0) for term in pairs])
        return self.total()

    def launch(self, out):
        axis, bit, kind = self.hops.pop(0)
        size = self.sizes[0] if axis == "group" else self.sizes[1]
        self.came = swap(out, axis, size, bit)
        side = (lax.axis_index(axis) // bit) & 1
        if kind in ("split", "halve"):
            self.held = self.total(self.keep)
            if kind == "split" and out.shape[0] == 1 and self.held.ndim == out.ndim:
                self.held = self.held[0]
        else:
            self.held = out
        self.kind_of_hop, self.side = kind, side
        self.flying = True

    def land(self, came):
        self.flying = False
        if self.kind_of_hop == "back":
            held = self.held
            self.terms = [
                jnp.where(
                    self.side == 0,
                    jnp.concatenate([held, came]),
                    jnp.concatenate([came, held]),
                )
            ]
            return
        if self.kind_of_hop == "split" and self.held.ndim < came.ndim:
            came = came[0]
        self.terms = [self.held, came]

    def drain(self):
        while self.flying or self.hops:
            if not self.flying:
                self.launch(self.outgoing())
            self.land(self.came)

    def result(self):
        return self.total(kind=F32)


def turn(landing, launching, carry, quick=()):
    landing = [chain for chain in landing if chain.flying]
    came, carry = fence([chain.came for chain in landing], carry)
    for chain, part in zip(landing, came):
        chain.land(part)
    for chain in quick:
        out, carry = fence(chain.outgoing(), carry)
        chain.launch(out)
    launching = [chain for chain in launching if chain.hops]
    outs, carry = fence([chain.outgoing() for chain in launching], carry)
    for chain, out in zip(launching, outs):
        chain.launch(out)
    for chain in quick:
        came, outs, carry = fence(chain.came, outs, carry)
        chain.land(came)
        out, carry = fence(chain.outgoing(), carry)
        chain.launch(out)
    return carry


def dot(left, right):
    return lax.dot_general(left, right, (((1,), (0,)), ((), ())), preferred_element_type=F32)


def dot_nt(left, right):
    return lax.dot_general(left, right, (((1,), (1,)), ((), ())), preferred_element_type=F32)


def dot_tn(left, right):
    return lax.dot_general(left, right, (((0,), (0,)), ((), ())), preferred_element_type=F32)


def per_image(body, place, blocked, whole, weights, outs, sums, span=None, into=None):
    slots = blocked[0].shape[0]
    first, last = span or (0, slots)
    halves = [1 + (gather.partner or 1) for gather in weights]
    weights = [gather.pieces() for gather in weights]
    counts = [len(pieces) for pieces in weights]
    rows_of = [pieces[0].shape[0] for pieces in weights]
    total = [rows * (4 if len(pieces) > 1 else 1) for rows, pieces in zip(rows_of, weights)]

    def kernel(*refs):
        refs = list(refs)

        def take(count):
            taken = refs[:count]
            del refs[:count]
            return taken

        (where,) = take(1)
        blocked_refs = take(len(blocked))
        whole_refs = take(len(whole))
        piece_refs = [take(count) for count in counts]
        take(0 if into is None else 1)
        out_refs = take(len(outs))
        sum_refs = take(len(sums))
        weight_refs = take(len(weights))
        at = pl.program_id(0)

        @pl.when(at == 0)
        def _():
            copies = []
            for index, pieces in enumerate(piece_refs):
                starts = place_pieces(rows_of[index], len(pieces), where[0], where[halves[index]])
                for spot, (piece, start) in enumerate(zip(pieces, starts)):
                    target = weight_refs[index].at[pl.ds(pl.multiple_of(start, 16), piece.shape[0])]
                    copies.append(pltpu.make_async_copy(piece, target, refs[0].at[index, spot]))
            for copy in copies:
                copy.start()
            for ref in sum_refs:
                ref[...] = jnp.zeros_like(ref)
            for copy in copies:
                copy.wait()

        body(at + first, where, blocked_refs, whole_refs, weight_refs, out_refs, sum_refs)

    in_specs = [pl.BlockSpec(memory_space=pltpu.SMEM)]
    for array in blocked:
        in_specs.append(pl.BlockSpec((1,) + array.shape[1:], lambda i: (i + first, 0, 0)))
    for array in whole:
        in_specs.append(pl.BlockSpec(array.shape, lambda i: (0, 0)))
    pieces = [piece for parts in weights for piece in parts]
    extra = [] if into is None else [into]
    in_specs += [pl.BlockSpec(memory_space=pl.ANY)] * (len(pieces) + len(extra))
    out_specs = [
        pl.BlockSpec((1, rows, columns), lambda i: (i + first, 0, 0)) for rows, columns, _ in outs
    ]
    out_specs += [pl.BlockSpec((1, columns), lambda i: (0, 0)) for columns in sums]
    shapes = [jax.ShapeDtypeStruct((slots, rows, columns), kind) for rows, columns, kind in outs]
    shapes += [jax.ShapeDtypeStruct((1, columns), F32) for columns in sums]
    scratch = [
        pltpu.VMEM((rows, parts[0].shape[1]), BF16) for rows, parts in zip(total, weights)
    ]
    if weights:
        scratch.append(pltpu.SemaphoreType.DMA((len(weights), 6)))
    return pl.pallas_call(
        kernel,
        grid=(last - first,),
        in_specs=in_specs,
        out_specs=out_specs,
        input_output_aliases={len(in_specs) - 1: 0} if extra else {},
        out_shape=shapes,
        scratch_shapes=scratch,
        compiler_params=pltpu.CompilerParams(
            dimension_semantics=("arbitrary",), vmem_limit_bytes=58 * 2**20
        ),
        cost_estimate=pl.CostEstimate(flops=2000000000, bytes_accessed=1, transcendentals=0),
    )(place, *blocked, *whole, *pieces, *extra)


def normed(field):
    centred = field - jnp.mean(field, -1, keepdims=True)
    scale = lax.rsqrt(jnp.mean(centred * centred, -1, keepdims=True) + 1e-06)
    return centred * scale, scale


def norm_back(grad, gain, hat, scale):
    inner = grad * gain
    mean = jnp.mean(inner, -1, keepdims=True)
    along = jnp.mean(inner * hat, -1, keepdims=True)
    return scale * (inner - mean - hat * along)


def column_sum(field):
    return jnp.sum(field.astype(F32), 0, keepdims=True)


def outer_halves(place, pairs, groups, step):
    slots, rows, width = pairs[0][0].shape
    tokens = slots * rows
    share = width // groups
    columns = sum(right.shape[2] for _, right in pairs)
    bounds = [0]
    for _, right in pairs:
        bounds.append(bounds[-1] + right.shape[2] // step)

    def kernel(where, *refs):
        lefts, rights = refs[: len(pairs)], refs[len(pairs) : 2 * len(pairs)]
        send_ref, keep_ref, total = refs[2 * len(pairs) :]
        at = pl.program_id(0)
        for left, right, first, last in zip(lefts, rights, bounds, bounds[1:]):

            @pl.when((at >= first) & (at < last))
            def _(left=left, right=right):
                total[...] = dot_tn(left[...], right[...]).astype(BF16)

        side = where[0] & 1
        for spot in range(groups // 2):
            for ref, mine in ((send_ref, 1 - side), (keep_ref, side)):
                start = pl.multiple_of((2 * spot + mine) * share, 16)
                ref[spot] = total[pl.ds(start, share), :]

    def column_map(first, last):
        return lambda i: (0, jnp.clip(i - first, 0, last - first - 1))

    shape = jax.ShapeDtypeStruct((groups // 2, share, columns), BF16)
    return pl.pallas_call(
        kernel,
        grid=(bounds[-1],),
        in_specs=[pl.BlockSpec(memory_space=pltpu.SMEM)]
        + [pl.BlockSpec((tokens, width), lambda i: (0, 0))] * len(pairs)
        + [
            pl.BlockSpec((tokens, step), column_map(first, last))
            for first, last in zip(bounds, bounds[1:])
        ],
        out_specs=[pl.BlockSpec((groups // 2, share, step), lambda i: (0, 0, i))] * 2,
        out_shape=[shape, shape],
        scratch_shapes=[pltpu.VMEM((width, step), BF16)],
        compiler_params=pltpu.CompilerParams(
            dimension_semantics=("arbitrary",), vmem_limit_bytes=58 * 2**20
        ),
        cost_estimate=pl.CostEstimate(flops=1, bytes_accessed=1, transcendentals=0),
    )(
        place,
        *[left.reshape(tokens, width) for left, _ in pairs],
        *[right.reshape(tokens, -1) for _, right in pairs],
    )


def prepare(place, images, cotangent, rows):
    slots, length, width = images.shape

    def kernel(where, images_ref, cotangent_ref, images_out, cotangent_out):
        live = jnp.where(pl.program_id(0) < where[1], 1.0, 0.0).astype(BF16)
        empty = jnp.zeros((rows - length // 16 * 16, width), BF16)
        for ref, scale, out in (
            (images_ref, None, images_out),
            (cotangent_ref, live, cotangent_out),
        ):
            out[0, length // 16 * 16 :, :] = empty
            value = ref[0] if scale is None else ref[0] * scale
            out[0, :length, :] = value

    shape = jax.ShapeDtypeStruct((slots, rows, width), BF16)
    block = pl.BlockSpec((1, length, width), lambda i: (i, 0, 0))
    padded = pl.BlockSpec((1, rows, width), lambda i: (i, 0, 0))
    return pl.pallas_call(
        kernel,
        grid=(slots,),
        in_specs=[pl.BlockSpec(memory_space=pltpu.SMEM), block, block],
        out_specs=[padded, padded],
        out_shape=[shape, shape],
        compiler_params=pltpu.CompilerParams(dimension_semantics=("arbitrary",)),
        cost_estimate=pl.CostEstimate(flops=1, bytes_accessed=16 * 2**20, transcendentals=0),
    )(place, images, cotangent)


def pack(parts):
    total = sum(part.shape[1] for part in parts) // 128

    def kernel(*refs):
        at = 0
        for ref in refs[:-1]:
            for start in range(0, ref.shape[1], 128):
                refs[-1][at : at + 1, :] = ref[:, start : start + 128]
                at += 1

    return pl.pallas_call(
        kernel,
        in_specs=[pl.BlockSpec(memory_space=pltpu.VMEM)] * len(parts),
        out_specs=pl.BlockSpec(memory_space=pltpu.VMEM),
        out_shape=jax.ShapeDtypeStruct((total, 128), F32),
        cost_estimate=pl.CostEstimate(flops=1, bytes_accessed=1, transcendentals=0),
    )(*parts)


def unpack(place, lines, spots):
    count, unit = lines[0].shape
    sizes = {}
    for rows, out, column in spots:
        sizes[out] = max(sizes.get(out, 0), column + 4 * rows * unit)

    def kernel(where, *refs):
        outs = refs[4:]
        parts = [ref[...].astype(F32) for ref in refs[:4]]
        for ref in outs:
            ref[...] = jnp.zeros_like(ref)
        for owner in range(4):
            mine = jnp.zeros((count, unit), F32)
            for spot, part in enumerate(parts):
                mine = jnp.where((where[0] ^ spot) == owner, part, mine)
            row = 0
            for rows, out, column in spots:
                for at in range(rows):
                    start = column + (owner * rows + at) * unit
                    outs[out][:, start : start + unit] = mine[row : row + 1]
                    row += 1

    return pl.pallas_call(
        kernel,
        in_specs=[pl.BlockSpec(memory_space=pltpu.SMEM)]
        + [pl.BlockSpec(memory_space=pltpu.VMEM)] * 4,
        out_specs=[pl.BlockSpec(memory_space=pltpu.VMEM)] * len(sizes),
        out_shape=[jax.ShapeDtypeStruct((1, sizes[at]), F32) for at in range(len(sizes))],
        cost_estimate=pl.CostEstimate(flops=1, bytes_accessed=6 * 2**20, transcendentals=0),
    )(place, *lines)


def query_body(at, where, blocked, whole, weights, outs, sums):
    gain, shift, bias = whole
    hat, _ = normed(blocked[0][0].astype(F32))
    low = (hat * gain[...] + shift[...]).astype(BF16)
    outs[0][0] = low
    width = low.shape[1]
    for part in range(3):
        cut = slice(part * width, (part + 1) * width)
        outs[1][0, :, cut] = (dot(low, weights[0][:, cut]) + bias[:, cut]).astype(BF16)


def attend_body(length, at, where, blocked, whole, weights, outs, sums):
    (packed,) = blocked
    rows = packed.shape[1]
    width = packed.shape[2] // 3
    lanes = 2 * width // HEADS
    factor = (width // HEADS) ** (-0.5)
    low_lane = lax.broadcasted_iota(jnp.int32, (rows, lanes), 1) < lanes // 2
    key_there = lax.broadcasted_iota(jnp.int32, (rows, rows), 1) < length
    for group in range(0, HEADS // 2, GROUP):
        first = []
        for pair in range(group, group + GROUP):
            start = pair * lanes
            query = packed[0, :, start : start + lanes] * jnp.asarray(factor, BF16)
            keys = packed[0, :, width + start : width + start + lanes]
            values = packed[0, :, 2 * width + start : 2 * width + start + lanes]
            for side in range(2):
                mine = low_lane if side == 0 else jnp.logical_not(low_lane)
                first.append((dot_nt(jnp.where(mine, query, jnp.zeros_like(query)), keys), values))
        second = []
        for scores, values in first:
            scores = jnp.where(key_there, scores, -1e30)
            expo = jnp.exp(scores - jnp.max(scores, -1, keepdims=True))
            probs = expo * (1.0 / jnp.sum(expo, -1, keepdims=True))
            second.append((probs.astype(BF16), values))
        third = [dot(probs, values) for probs, values in second]
        for spot in range(GROUP):
            start = (group + spot) * lanes
            both = jnp.where(low_lane, third[2 * spot], third[2 * spot + 1])
            outs[0][0, :, start : start + lanes] = both.astype(BF16)


def up_body(at, where, blocked, whole, weights, outs, sums):
    attended, images = blocked
    bias_out, gain, shift, bias_up = whole
    w_out, w_up = weights
    middle = images[0].astype(F32) + dot(attended[0], w_out[...]) + bias_out[...]
    outs[2][0] = middle
    hat, _ = normed(middle)
    low = (hat * gain[...] + shift[...]).astype(BF16)
    outs[3][0] = low
    inner = w_up.shape[1]
    width = low.shape[1]
    for start in range(0, inner, width):
        cut = slice(start, start + width)
        pre = dot(low, w_up[:, cut]) + bias_up[:, cut]
        square = pre * pre
        bend = jnp.tanh(pre * (GELU_A + (GELU_A * GELU_B) * square))
        half = 0.5 + 0.5 * bend
        outs[0][0, :, cut] = (pre * half).astype(BF16)
        slope = GELU_A + (3.0 * GELU_A * GELU_B) * square
        outs[1][0, :, cut] = (half + (0.5 * pre) * ((1.0 - bend * bend) * slope)).astype(BF16)


def pre_body(at, where, blocked, whole, weights, outs, sums):
    cotangent, slope = blocked
    grad_low = cotangent[0]
    width = grad_low.shape[1]
    for start in range(0, slope.shape[2], width):
        cut = slice(start, start + width)
        grad_pre = dot_nt(grad_low, weights[0][cut, :]) * slope[0, :, cut].astype(F32)
        low = grad_pre.astype(BF16)
        outs[0][0, :, cut] = low
        sums[0][:, cut] += column_sum(low)
    sums[1][...] += column_sum(grad_low)


def back_body(at, where, blocked, whole, weights, outs, sums):
    cotangent, grad_pre, middle = blocked
    (gain,) = whole
    w_up, w_out = weights
    grad_two = dot_nt(grad_pre[0], w_up[...])
    hat, scale = normed(middle[0])
    sums[0][...] += column_sum(grad_two * hat)
    sums[1][...] += column_sum(grad_two)
    grad_middle = cotangent[0].astype(F32) + norm_back(grad_two, gain[...], hat, scale)
    outs[0][0] = grad_middle
    low = grad_middle.astype(BF16)
    outs[1][0] = low
    sums[2][...] += column_sum(low)
    outs[2][0] = dot_nt(low, w_out[...]).astype(BF16)


def attend_back_body(length, pairs, at, where, blocked, whole, weights, outs, sums):
    packed, grads = blocked
    rows, width = grads.shape[1:]
    part = outs[0].shape[2] // 3
    lanes = 2 * width // HEADS
    factor = (width // HEADS) ** (-0.5)
    low_lane = lax.broadcasted_iota(jnp.int32, (rows, lanes), 1) < lanes // 2
    full = length // 8 * 8
    there = lax.broadcasted_iota(jnp.int32, (rows - full, rows), 0) < length - full
    first = []
    for pair in pairs:
        start = pair * lanes
        cuts = [slice(at * width + start, at * width + start + lanes) for at in range(3)]
        query, keys, values = (packed[0, :, cut] for cut in cuts)
        grad = grads[0, :, start : start + lanes]
        scaled = query * jnp.asarray(factor, BF16)
        for side in range(2):
            mine = low_lane if side == 0 else jnp.logical_not(low_lane)
            scores = dot_nt(jnp.where(mine, keys, jnp.zeros_like(keys)), scaled)
            grad_probs = dot_nt(jnp.where(mine, values, jnp.zeros_like(values)), grad)
            first.append((query, keys, grad, scores, grad_probs))
    second = []
    for query, keys, grad, scores, grad_probs in first:
        scores = jnp.concatenate([scores[:full], jnp.where(there, scores[full:], -1e30)], 0)
        expo = jnp.exp(scores - jnp.max(scores, 0, keepdims=True))
        probs = expo * (1.0 / jnp.sum(expo, 0, keepdims=True))
        both = probs * grad_probs
        inner = jnp.sum(both, 0, keepdims=True)
        grad_scores = (both - probs * inner).astype(BF16)
        second.append((query, keys, grad, probs.astype(BF16), grad_scores))
    third = []
    for query, keys, grad, probs, grad_scores in second:
        third.append(
            (
                dot_tn(grad_scores, keys) * factor,
                dot(grad_scores, query) * factor,
                dot(probs, grad),
            )
        )
    for spot in range(len(pairs)):
        for kind in range(3):
            low = jnp.where(low_lane, third[2 * spot][kind], third[2 * spot + 1][kind])
            low = low.astype(BF16)
            cut = slice(kind * part + spot * lanes, kind * part + (spot + 1) * lanes)
            outs[0][0, :, cut] = low
            sums[0][:, cut] += column_sum(low)


def input_body(length, at, where, blocked, whole, weights, outs, sums):
    *packed, images, grad_middle = blocked
    width = images.shape[2]
    grad_one = None
    start = 0
    for array in packed:
        part = array.shape[2] // 3
        for kind in range(3):
            weight = weights[0][:, kind * width + start : kind * width + start + part]
            term = dot_nt(array[0, :, kind * part : (kind + 1) * part], weight)
            grad_one = term if grad_one is None else grad_one + term
        start += part
    hat, scale = normed(images[0].astype(F32))
    sums[0][...] += column_sum(grad_one * hat)
    sums[1][...] += column_sum(grad_one)
    result = grad_middle[0] + norm_back(grad_one, whole[0][...], hat, scale)
    outs[0][0] = result[:length]


def down_body(length, at, where, blocked, whole, weights, outs, sums):
    hidden, middle = blocked
    result = middle[0] + dot(hidden[0], weights[0][...]) + whole[0][...]
    live = jnp.where(at < where[1], 1.0, 0.0).astype(F32)
    outs[0][0] = (result * live)[:length].astype(BF16)


def on_device(
    sizes,
    images,
    counts,
    ln1_gain,
    ln1_shift,
    w_qkv,
    b_query,
    b_value,
    w_out,
    b_out,
    ln2_gain,
    ln2_shift,
    w_up,
    b_up,
    w_down,
    b_down,
    cotangent,
):
    slots, length, width = images.shape
    inner = w_up.shape[1]
    rows = -(-length // 16) * 16
    vectors = (ln1_gain, ln1_shift, b_query, b_value, b_out, ln2_gain, ln2_shift, b_down, b_up)
    g_qkv = Gather(w_qkv, sizes, 1)
    g_out = Gather(w_out, sizes, 0)
    g_up = Gather(w_up, sizes, 2)
    g_down = Gather(w_down, sizes, 0)
    if g_qkv.split:
        g_qkv.out, vectors = fence(g_qkv.out, vectors)
    g_qkv.far()
    g_qkv.near()
    place = jnp.stack(
        [
            lax.axis_index("group"),
            counts[0],
            lax.axis_index("replica") & 1,
            (lax.axis_index("replica") >> 1) & 1,
        ]
    ).astype(jnp.int32)
    widths = [vector.shape[0] for vector in vectors]
    unit = min(widths)
    at = jnp.arange(sum(widths) // unit)[:, None]
    line = jnp.zeros((sum(widths) // unit, unit), BF16)
    row = 0
    for vector in vectors:
        if vector.shape[0] == unit:
            line = jnp.where(at == row, vector[None, :], line)
        else:
            count = vector.shape[0] // unit
            fill = ((row, line.shape[0] - row - count), (0, 0))
            line = line + jnp.pad(vector.reshape(count, unit), fill)
        row += vector.shape[0] // unit
    if sizes[0] == 4:
        far_line = swap(line, "group", 4, 2)
        near_line = swap(line, "group", 4, 1)
        far_near = swap(far_line, "group", 4, 1)
        spots = []
        for at, size in enumerate(widths):
            out, column = (2, 2 * width) if at == 3 else (at - (at > 3), 0)
            spots.append((size // unit, out, column))
        small = unpack(place, (line, near_line, far_line, far_near), spots)
    else:
        gathered = lax.all_gather(line.reshape(-1), "group", axis=0, tiled=False)
        small = []
        start = 0
        for size in widths:
            small.append(gathered[:, start : start + size].reshape(1, -1).astype(F32))
            start += size
        small[2:4] = [jnp.concatenate([small[2], jnp.zeros_like(small[2]), small[3]], 1)]
    images, cotangent = prepare(place, images, cotangent, rows)
    tokens = slots * rows

    def outer(left, right):
        left = left.reshape(tokens, -1)
        right = right.reshape(tokens, -1)
        return dot_tn(left, right).astype(BF16)

    def chain(pairs, halvings, step):
        if sizes[0] > 1 and is_power(sizes[0]) and is_power(sizes[1]):
            return Reduce(outer_halves(place, pairs, sizes[0], step), sizes, halvings)
        return Reduce(jnp.concatenate([outer(*pair) for pair in pairs], 1), sizes, halvings)

    def hand_over(gather, name, carry):
        if gather.hops:
            part, carry = fence(getattr(gather, name), carry)
            setattr(gather, name, part)
        return carry

    if g_qkv.split:
        g_qkv.first, far_line, g_out.out, g_up.out = fence(
            g_qkv.first, far_line, g_out.out, g_up.out
        )
    g_qkv.across()
    g_up.far()
    if g_qkv.split:
        g_qkv.second, small, images, cotangent = fence(g_qkv.second, small, images, cotangent)
    g_qkv.last()
    g_out.far()
    gain_one, shift_one, bias_cat, bias_out, gain_two, shift_two, bias_down, bias_up = small
    images = hand_over(g_up, "first", images)
    g_up.across()
    low_one, packed = per_image(
        query_body, place, [images], [gain_one, shift_one, bias_cat], [g_qkv],
        [(rows, width, BF16), (rows, 3 * width, BF16)], [],
    )
    packed = hand_over(g_out, "first", packed)
    g_out.shard, g_up.shard, g_down.shard, g_down.out, packed = fence(
        g_out.shard, g_up.shard, g_down.shard, g_down.out, packed
    )
    g_out.across()
    g_down.far()
    g_out.near()
    g_up.near()
    g_down.near()
    (attended,) = per_image(
        functools.partial(attend_body, length), place, [packed], [], [],
        [(rows, width, BF16)], [],
    )
    if g_up.split:
        attended = hand_over(g_up, "second", attended)
    g_up.last()
    hidden, slope, middle, low_two = per_image(
        up_body, place, [attended, images], [bias_out, gain_two, shift_two, bias_up],
        [g_out, g_up],
        [(rows, inner, BF16), (rows, inner, BF16), (rows, width, F32), (rows, width, BF16)],
        [],
    )
    hidden = hand_over(g_down, "first", hidden)
    g_down.across()
    down, slope = fence(outer(hidden, cotangent), slope)
    down = Reduce(down, sizes, 2, True)
    grad_pre, grad_bup, grad_bdown = per_image(
        pre_body, place, [cotangent, slope], [], [g_down],
        [(rows, inner, BF16)], [inner, width],
    )
    up = chain([(low_two, grad_pre)], 2, inner // 4)
    grad_pre = turn([], [up], grad_pre)
    grad_middle, grad_branch, grad_att, grad_gain_two, grad_shift_two, grad_bout = per_image(
        back_body, place, [cotangent, grad_pre, middle], [gain_two], [g_up, g_out],
        [(rows, width, F32), (rows, width, BF16), (rows, width, BF16)],
        [width, width, width],
    )
    grad_att = turn([up], [up, down], grad_att)
    half = HEADS // 4
    part = width // 2
    grad_one, sums_one = per_image(
        functools.partial(attend_back_body, length, range(half)), place, [packed, grad_att],
        [], [], [(rows, 3 * part, BF16)], [3 * part],
    )
    grad_one = turn([down], [down], grad_one)
    one = chain([(low_one, grad_one), (attended, grad_branch)], 2, part)
    grad_att = turn([up, down], [up, down], grad_att, [one])
    grad_two, sums_two = per_image(
        functools.partial(attend_back_body, length, range(half, 2 * half)), place,
        [packed, grad_att], [], [], [(rows, 3 * part, BF16)], [3 * part],
    )
    two = chain([(low_one, grad_two)], 1, part)
    grad_middle = turn([one, up, down], [one, up, down], grad_middle, [two])
    input_grad, grad_gain_one, grad_shift_one = per_image(
        functools.partial(input_body, length), place, [grad_one, grad_two, images, grad_middle],
        [gain_one], [g_qkv], [(length, width, F32)], [width, width],
    )
    parts = (
        grad_gain_one,
        grad_shift_one,
        sums_one[:, :part],
        sums_two[:, :part],
        sums_one[:, 2 * part :],
        sums_two[:, 2 * part :],
        grad_bout,
        grad_gain_two,
        grad_shift_two,
        grad_bdown,
        grad_bup,
    )
    little = Share(pack(parts), sizes)
    hidden = turn([two], [two], hidden)
    hidden = turn([up, one, down], [up, one, down], hidden, [little])
    outputs = None
    for span in ((0, slots // 2), (slots // 2, slots)):
        (outputs,) = per_image(
            functools.partial(down_body, length), place, [hidden, middle], [bias_down], [g_down],
            [(length, width, BF16)], [], span, outputs,
        )
        if span[0] == 0:
            outputs = turn([two, up, one, little], [two, up, one, little], outputs)
    outputs = turn([two], [two], outputs)
    outputs = turn([one, up, little, down], [one, up, little], outputs)
    outputs = turn([two], [two], outputs)
    outputs = turn([one, little], [one, little], outputs)
    for item in (two, one, up, little, down):
        item.drain()
    little = little.field.reshape(-1)
    sums = []
    start = 0
    for size in widths:
        mine = lax.axis_index("group") * size
        sums.append(lax.dynamic_slice(little, (start + mine,), (size,)))
        start += size * sizes[0]
    one, two = one.result(), two.result()
    grad_qkv = jnp.concatenate(
        [side[:, kind * part : (kind + 1) * part] for kind in range(3) for side in (one, two)], 1
    )
    big = [down.result(), up.result(), one[:, 3 * part :], grad_qkv]
    return (
        outputs,
        input_grad,
        sums[0],
        sums[1],
        big[3],
        sums[2],
        sums[3],
        big[2],
        sums[4],
        sums[5],
        sums[6],
        big[1],
        sums[8],
        big[0],
        sums[7],
    )


def solution(mesh):
    sizes = (mesh.shape["group"], mesh.shape["replica"])
    line = P("group")
    grid = P("group", None)
    field = P(("replica", "group"), None, None)
    return jax.shard_map(
        functools.partial(on_device, sizes),
        mesh=mesh,
        in_specs=(
            field, P(("replica", "group")), line, line, grid, line, line, grid, line, line, line,
            grid, line, grid, line, field,
        ),
        out_specs=(
            field, field, line, line, grid, line, line, grid, line, line, line, grid, line, grid,
            line,
        ),
        check_vma=False,
    )
```

```python
import functools

import jax
import jax.numpy as jnp
from jax import lax
from jax.experimental import pallas as pl
from jax.experimental.pallas import tpu as pltpu
from jax.sharding import PartitionSpec as P

HEADS = 12
GROUP = 3
F32 = jnp.float32
BF16 = jnp.bfloat16
GELU_A = 0.7978845608028654
GELU_B = 0.044715


def swap(field, axis, size, bit):
    return lax.ppermute(field, axis, [(at, at ^ bit) for at in range(size)])


def is_power(size):
    return size & (size - 1) == 0


def pick(field, at, axis):
    return lax.dynamic_index_in_dim(field, at, axis, keepdims=False)


def fence(*groups):
    return lax.optimization_barrier(groups)


class Gather:
    def __init__(self, shard, sizes, partner):
        self.groups, self.replicas = sizes
        self.shard = shard
        self.rows = shard.shape[0]
        self.hops = self.groups == 4 and self.rows % 32 == 0
        self.split = self.hops and partner and self.replicas % (2 * partner) == 0
        self.partner = partner
        if not self.hops:
            self.whole = lax.all_gather(shard, "group", axis=0, tiled=True)
        self.out = shard
        if self.split:
            half = (lax.axis_index("replica") // partner) & 1
            self.out = pick(shard.reshape(2, self.rows // 2, -1), half, 0)

    def near(self):
        if self.hops:
            self.beside = swap(self.shard, "group", 4, 1)

    def far(self):
        if self.hops:
            self.first = swap(self.out, "group", 4, 2)

    def across(self):
        if self.split:
            self.second = swap(self.first, "replica", self.replicas, self.partner)
        if self.hops:
            self.far_first = swap(self.first, "group", 4, 1)

    def last(self):
        if self.split:
            self.far_second = swap(self.second, "group", 4, 1)

    def pieces(self):
        if not self.hops:
            return (self.whole,)
        if not self.split:
            return (self.shard, self.beside, self.first, self.far_first)
        return (self.shard, self.beside, self.first, self.second, self.far_first, self.far_second)


def place_pieces(rows, pieces, me, half):
    if pieces == 1:
        return [0]
    if pieces == 4:
        return [(me ^ spot) * rows for spot in range(4)]
    part = rows // 2
    return [
        me * rows,
        (me ^ 1) * rows,
        (me ^ 2) * rows + half * part,
        (me ^ 2) * rows + (1 - half) * part,
        (me ^ 3) * rows + half * part,
        (me ^ 3) * rows + (1 - half) * part,
    ]


def add_low(left, right, kind):
    return (left.astype(F32) + right.astype(F32)).astype(kind)


class Share:
    def __init__(self, field, sizes):
        self.field = field
        self.flying = False
        self.hops = []
        if not (is_power(sizes[0]) and is_power(sizes[1])):
            self.field = lax.psum(field, ("replica", "group"))
            return
        for axis, size in zip(("group", "replica"), sizes):
            bit = 1
            while bit < size:
                self.hops.append((axis, size, bit))
                bit *= 2

    def outgoing(self):
        return self.field

    def launch(self, out):
        self.field = out
        self.came = swap(out, *self.hops.pop(0))
        self.flying = True

    def land(self, came):
        self.field = self.field + came
        self.flying = False

    def drain(self):
        while self.flying or self.hops:
            if not self.flying:
                self.launch(self.outgoing())
            self.land(self.came)


class Reduce:
    def __init__(self, grad, sizes, halvings, scatter=False):
        self.sizes = sizes
        self.ready = None
        self.kind = BF16
        groups, replicas = sizes
        self.hops = []
        self.flying = False
        if not (is_power(groups) and is_power(replicas)):
            shard = lax.psum_scatter(grad, "group", scatter_dimension=0, tiled=True)
            self.terms = [lax.psum(shard.astype(F32), "replica")]
            return
        if scatter:
            self.terms = [lax.psum_scatter(grad, "group", scatter_dimension=0, tiled=True)]
        else:
            self.ready = grad
            bit = 1
            while bit < groups:
                self.hops.append(("group", bit, "split"))
                bit *= 2
        bit = 1
        back = []
        while bit < replicas:
            if len(back) < halvings:
                self.hops.append(("replica", bit, "halve"))
                back.append(("replica", bit, "back"))
            else:
                self.hops.append(("replica", bit, "whole"))
            bit *= 2
        self.hops += reversed(back)

    def total(self, parts=None, kind=None):
        parts = self.terms if parts is None else parts
        if len(parts) == 1:
            return parts[0].astype(kind or self.kind)
        return sum(part.astype(F32) for part in parts).astype(kind or self.kind)

    def outgoing(self):
        if self.ready:
            out, keep = self.ready
            self.ready, self.keep = None, [keep]
            return out
        axis, bit, kind = self.hops[0]
        side = (lax.axis_index(axis) // bit) & 1
        if kind == "split":
            shape = self.terms[0].shape
            pairs = [term.reshape((shape[0] // 2, 2) + shape[1:]) for term in self.terms]
            self.keep = [pick(term, side, 1) for term in pairs]
            if shape[0] == 2:
                self.keep = [term[0] for term in self.keep]
            return self.total([pick(term, 1 - side, 1) for term in pairs])
        if kind == "halve":
            shape = self.terms[0].shape
            pairs = [term.reshape((2, shape[0] // 2) + shape[1:]) for term in self.terms]
            self.keep = [pick(term, side, 0) for term in pairs]
            return self.total([pick(term, 1 - side, 0) for term in pairs])
        return self.total()

    def launch(self, out):
        axis, bit, kind = self.hops.pop(0)
        size = self.sizes[0] if axis == "group" else self.sizes[1]
        self.came = swap(out, axis, size, bit)
        side = (lax.axis_index(axis) // bit) & 1
        if kind in ("split", "halve"):
            self.held = self.total(self.keep)
            if kind == "split" and out.shape[0] == 1 and self.held.ndim == out.ndim:
                self.held = self.held[0]
        else:
            self.held = out
        self.kind_of_hop, self.side = kind, side
        self.flying = True

    def land(self, came):
        self.flying = False
        if self.kind_of_hop == "back":
            held = self.held
            self.terms = [
                jnp.where(
                    self.side == 0,
                    jnp.concatenate([held, came]),
                    jnp.concatenate([came, held]),
                )
            ]
            return
        if self.kind_of_hop == "split" and self.held.ndim < came.ndim:
            came = came[0]
        self.terms = [self.held, came]

    def drain(self):
        while self.flying or self.hops:
            if not self.flying:
                self.launch(self.outgoing())
            self.land(self.came)

    def result(self):
        return self.total(kind=F32)


def turn(landing, launching, carry, quick=()):
    landing = [chain for chain in landing if chain.flying]
    came, carry = fence([chain.came for chain in landing], carry)
    for chain, part in zip(landing, came):
        chain.land(part)
    for chain in quick:
        out, carry = fence(chain.outgoing(), carry)
        chain.launch(out)
    launching = [chain for chain in launching if chain.hops]
    outs, carry = fence([chain.outgoing() for chain in launching], carry)
    for chain, out in zip(launching, outs):
        chain.launch(out)
    for chain in quick:
        came, outs, carry = fence(chain.came, outs, carry)
        chain.land(came)
        out, carry = fence(chain.outgoing(), carry)
        chain.launch(out)
    return carry


def dot(left, right):
    return lax.dot_general(left, right, (((1,), (0,)), ((), ())), preferred_element_type=F32)


def dot_nt(left, right):
    return lax.dot_general(left, right, (((1,), (1,)), ((), ())), preferred_element_type=F32)


def dot_tn(left, right):
    return lax.dot_general(left, right, (((0,), (0,)), ((), ())), preferred_element_type=F32)


def per_image(body, place, blocked, whole, weights, outs, sums, span=None, into=None):
    slots = blocked[0].shape[0]
    first, last = span or (0, slots)
    halves = [1 + (gather.partner or 1) for gather in weights]
    weights = [gather.pieces() for gather in weights]
    counts = [len(pieces) for pieces in weights]
    rows_of = [pieces[0].shape[0] for pieces in weights]
    total = [rows * (4 if len(pieces) > 1 else 1) for rows, pieces in zip(rows_of, weights)]

    def kernel(*refs):
        refs = list(refs)

        def take(count):
            taken = refs[:count]
            del refs[:count]
            return taken

        (where,) = take(1)
        blocked_refs = take(len(blocked))
        whole_refs = take(len(whole))
        piece_refs = [take(count) for count in counts]
        take(0 if into is None else 1)
        out_refs = take(len(outs))
        sum_refs = take(len(sums))
        weight_refs = take(len(weights))
        at = pl.program_id(0)

        @pl.when(at == 0)
        def _():
            copies = []
            for index, pieces in enumerate(piece_refs):
                starts = place_pieces(rows_of[index], len(pieces), where[0], where[halves[index]])
                for spot, (piece, start) in enumerate(zip(pieces, starts)):
                    target = weight_refs[index].at[pl.ds(pl.multiple_of(start, 16), piece.shape[0])]
                    copies.append(pltpu.make_async_copy(piece, target, refs[0].at[index, spot]))
            for copy in copies:
                copy.start()
            for ref in sum_refs:
                ref[...] = jnp.zeros_like(ref)
            for copy in copies:
                copy.wait()

        body(at + first, where, blocked_refs, whole_refs, weight_refs, out_refs, sum_refs)

    in_specs = [pl.BlockSpec(memory_space=pltpu.SMEM)]
    for array in blocked:
        in_specs.append(pl.BlockSpec((1,) + array.shape[1:], lambda i: (i + first, 0, 0)))
    for array in whole:
        in_specs.append(pl.BlockSpec(array.shape, lambda i: (0, 0)))
    pieces = [piece for parts in weights for piece in parts]
    extra = [] if into is None else [into]
    in_specs += [pl.BlockSpec(memory_space=pl.ANY)] * (len(pieces) + len(extra))
    out_specs = [
        pl.BlockSpec((1, rows, columns), lambda i: (i + first, 0, 0)) for rows, columns, _ in outs
    ]
    out_specs += [pl.BlockSpec((1, columns), lambda i: (0, 0)) for columns in sums]
    shapes = [jax.ShapeDtypeStruct((slots, rows, columns), kind) for rows, columns, kind in outs]
    shapes += [jax.ShapeDtypeStruct((1, columns), F32) for columns in sums]
    scratch = [
        pltpu.VMEM((rows, parts[0].shape[1]), BF16) for rows, parts in zip(total, weights)
    ]
    if weights:
        scratch.append(pltpu.SemaphoreType.DMA((len(weights), 6)))
    return pl.pallas_call(
        kernel,
        grid=(last - first,),
        in_specs=in_specs,
        out_specs=out_specs,
        input_output_aliases={len(in_specs) - 1: 0} if extra else {},
        out_shape=shapes,
        scratch_shapes=scratch,
        compiler_params=pltpu.CompilerParams(
            dimension_semantics=("arbitrary",), vmem_limit_bytes=58 * 2**20
        ),
        cost_estimate=pl.CostEstimate(flops=2000000000, bytes_accessed=1, transcendentals=0),
    )(place, *blocked, *whole, *pieces, *extra)


def normed(field):
    centred = field - jnp.mean(field, -1, keepdims=True)
    scale = lax.rsqrt(jnp.mean(centred * centred, -1, keepdims=True) + 1e-06)
    return centred * scale, scale


def norm_back(grad, gain, hat, scale):
    inner = grad * gain
    mean = jnp.mean(inner, -1, keepdims=True)
    along = jnp.mean(inner * hat, -1, keepdims=True)
    return scale * (inner - mean - hat * along)


def column_sum(field):
    return jnp.sum(field.astype(F32), 0, keepdims=True)


def outer_halves(place, pairs, groups, step):
    slots, rows, width = pairs[0][0].shape
    tokens = slots * rows
    share = width // groups
    columns = sum(right.shape[2] for _, right in pairs)
    bounds = [0]
    for _, right in pairs:
        bounds.append(bounds[-1] + right.shape[2] // step)

    def kernel(where, *refs):
        lefts, rights = refs[: len(pairs)], refs[len(pairs) : 2 * len(pairs)]
        send_ref, keep_ref, total = refs[2 * len(pairs) :]
        at = pl.program_id(0)
        for left, right, first, last in zip(lefts, rights, bounds, bounds[1:]):

            @pl.when((at >= first) & (at < last))
            def _(left=left, right=right):
                total[...] = dot_tn(left[...], right[...]).astype(BF16)

        side = where[0] & 1
        for spot in range(groups // 2):
            for ref, mine in ((send_ref, 1 - side), (keep_ref, side)):
                start = pl.multiple_of((2 * spot + mine) * share, 16)
                ref[spot] = total[pl.ds(start, share), :]

    def column_map(first, last):
        return lambda i: (0, jnp.clip(i - first, 0, last - first - 1))

    shape = jax.ShapeDtypeStruct((groups // 2, share, columns), BF16)
    return pl.pallas_call(
        kernel,
        grid=(bounds[-1],),
        in_specs=[pl.BlockSpec(memory_space=pltpu.SMEM)]
        + [pl.BlockSpec((tokens, width), lambda i: (0, 0))] * len(pairs)
        + [
            pl.BlockSpec((tokens, step), column_map(first, last))
            for first, last in zip(bounds, bounds[1:])
        ],
        out_specs=[pl.BlockSpec((groups // 2, share, step), lambda i: (0, 0, i))] * 2,
        out_shape=[shape, shape],
        scratch_shapes=[pltpu.VMEM((width, step), BF16)],
        compiler_params=pltpu.CompilerParams(
            dimension_semantics=("arbitrary",), vmem_limit_bytes=58 * 2**20
        ),
        cost_estimate=pl.CostEstimate(flops=1, bytes_accessed=1, transcendentals=0),
    )(
        place,
        *[left.reshape(tokens, width) for left, _ in pairs],
        *[right.reshape(tokens, -1) for _, right in pairs],
    )


def prepare(place, images, cotangent, rows):
    slots, length, width = images.shape

    def kernel(where, images_ref, cotangent_ref, images_out, cotangent_out):
        live = jnp.where(pl.program_id(0) < where[1], 1.0, 0.0).astype(BF16)
        empty = jnp.zeros((rows - length // 16 * 16, width), BF16)
        for ref, scale, out in (
            (images_ref, None, images_out),
            (cotangent_ref, live, cotangent_out),
        ):
            out[0, length // 16 * 16 :, :] = empty
            value = ref[0] if scale is None else ref[0] * scale
            out[0, :length, :] = value

    shape = jax.ShapeDtypeStruct((slots, rows, width), BF16)
    block = pl.BlockSpec((1, length, width), lambda i: (i, 0, 0))
    padded = pl.BlockSpec((1, rows, width), lambda i: (i, 0, 0))
    return pl.pallas_call(
        kernel,
        grid=(slots,),
        in_specs=[pl.BlockSpec(memory_space=pltpu.SMEM), block, block],
        out_specs=[padded, padded],
        out_shape=[shape, shape],
        compiler_params=pltpu.CompilerParams(dimension_semantics=("arbitrary",)),
        cost_estimate=pl.CostEstimate(flops=1, bytes_accessed=16 * 2**20, transcendentals=0),
    )(place, images, cotangent)


def pack(parts):
    total = sum(part.shape[1] for part in parts) // 128

    def kernel(*refs):
        at = 0
        for ref in refs[:-1]:
            for start in range(0, ref.shape[1], 128):
                refs[-1][at : at + 1, :] = ref[:, start : start + 128]
                at += 1

    return pl.pallas_call(
        kernel,
        in_specs=[pl.BlockSpec(memory_space=pltpu.VMEM)] * len(parts),
        out_specs=pl.BlockSpec(memory_space=pltpu.VMEM),
        out_shape=jax.ShapeDtypeStruct((total, 128), F32),
        cost_estimate=pl.CostEstimate(flops=1, bytes_accessed=1, transcendentals=0),
    )(*parts)


def unpack(place, lines, spots):
    count, unit = lines[0].shape
    sizes = {}
    for rows, out, column in spots:
        sizes[out] = max(sizes.get(out, 0), column + 4 * rows * unit)

    def kernel(where, *refs):
        outs = refs[4:]
        parts = [ref[...].astype(F32) for ref in refs[:4]]
        for ref in outs:
            ref[...] = jnp.zeros_like(ref)
        for owner in range(4):
            mine = jnp.zeros((count, unit), F32)
            for spot, part in enumerate(parts):
                mine = jnp.where((where[0] ^ spot) == owner, part, mine)
            row = 0
            for rows, out, column in spots:
                for at in range(rows):
                    start = column + (owner * rows + at) * unit
                    outs[out][:, start : start + unit] = mine[row : row + 1]
                    row += 1

    return pl.pallas_call(
        kernel,
        in_specs=[pl.BlockSpec(memory_space=pltpu.SMEM)]
        + [pl.BlockSpec(memory_space=pltpu.VMEM)] * 4,
        out_specs=[pl.BlockSpec(memory_space=pltpu.VMEM)] * len(sizes),
        out_shape=[jax.ShapeDtypeStruct((1, sizes[at]), F32) for at in range(len(sizes))],
        cost_estimate=pl.CostEstimate(flops=1, bytes_accessed=6 * 2**20, transcendentals=0),
    )(place, *lines)


def query_body(at, where, blocked, whole, weights, outs, sums):
    gain, shift, bias = whole
    hat, _ = normed(blocked[0][0].astype(F32))
    low = (hat * gain[...] + shift[...]).astype(BF16)
    outs[0][0] = low
    width = low.shape[1]
    for part in range(3):
        cut = slice(part * width, (part + 1) * width)
        outs[1][0, :, cut] = (dot(low, weights[0][:, cut]) + bias[:, cut]).astype(BF16)


def attend_body(length, at, where, blocked, whole, weights, outs, sums):
    (packed,) = blocked
    rows = packed.shape[1]
    width = packed.shape[2] // 3
    lanes = 2 * width // HEADS
    factor = (width // HEADS) ** (-0.5)
    low_lane = lax.broadcasted_iota(jnp.int32, (rows, lanes), 1) < lanes // 2
    key_there = lax.broadcasted_iota(jnp.int32, (rows, rows), 1) < length
    for group in range(0, HEADS // 2, GROUP):
        first = []
        for pair in range(group, group + GROUP):
            start = pair * lanes
            query = packed[0, :, start : start + lanes] * jnp.asarray(factor, BF16)
            keys = packed[0, :, width + start : width + start + lanes]
            values = packed[0, :, 2 * width + start : 2 * width + start + lanes]
            for side in range(2):
                mine = low_lane if side == 0 else jnp.logical_not(low_lane)
                first.append((dot_nt(jnp.where(mine, query, jnp.zeros_like(query)), keys), values))
        second = []
        for scores, values in first:
            scores = jnp.where(key_there, scores, -1e30)
            expo = jnp.exp(scores - jnp.max(scores, -1, keepdims=True))
            probs = expo * (1.0 / jnp.sum(expo, -1, keepdims=True))
            second.append((probs.astype(BF16), values))
        third = [dot(probs, values) for probs, values in second]
        for spot in range(GROUP):
            start = (group + spot) * lanes
            both = jnp.where(low_lane, third[2 * spot], third[2 * spot + 1])
            outs[0][0, :, start : start + lanes] = both.astype(BF16)


def up_body(at, where, blocked, whole, weights, outs, sums):
    attended, images = blocked
    bias_out, gain, shift, bias_up = whole
    w_out, w_up = weights
    middle = images[0].astype(F32) + dot(attended[0], w_out[...]) + bias_out[...]
    outs[2][0] = middle
    hat, _ = normed(middle)
    low = (hat * gain[...] + shift[...]).astype(BF16)
    outs[3][0] = low
    inner = w_up.shape[1]
    width = low.shape[1]
    for start in range(0, inner, width):
        cut = slice(start, start + width)
        pre = dot(low, w_up[:, cut]) + bias_up[:, cut]
        square = pre * pre
        bend = jnp.tanh(pre * (GELU_A + (GELU_A * GELU_B) * square))
        half = 0.5 + 0.5 * bend
        outs[0][0, :, cut] = (pre * half).astype(BF16)
        slope = GELU_A + (3.0 * GELU_A * GELU_B) * square
        outs[1][0, :, cut] = (half + (0.5 * pre) * ((1.0 - bend * bend) * slope)).astype(BF16)


def pre_body(at, where, blocked, whole, weights, outs, sums):
    cotangent, slope = blocked
    grad_low = cotangent[0]
    width = grad_low.shape[1]
    for start in range(0, slope.shape[2], width):
        cut = slice(start, start + width)
        grad_pre = dot_nt(grad_low, weights[0][cut, :]) * slope[0, :, cut].astype(F32)
        low = grad_pre.astype(BF16)
        outs[0][0, :, cut] = low
        sums[0][:, cut] += column_sum(low)
    sums[1][...] += column_sum(grad_low)


def back_body(at, where, blocked, whole, weights, outs, sums):
    cotangent, grad_pre, middle = blocked
    (gain,) = whole
    w_up, w_out = weights
    grad_two = dot_nt(grad_pre[0], w_up[...])
    hat, scale = normed(middle[0])
    sums[0][...] += column_sum(grad_two * hat)
    sums[1][...] += column_sum(grad_two)
    grad_middle = cotangent[0].astype(F32) + norm_back(grad_two, gain[...], hat, scale)
    outs[0][0] = grad_middle
    low = grad_middle.astype(BF16)
    outs[1][0] = low
    sums[2][...] += column_sum(low)
    outs[2][0] = dot_nt(low, w_out[...]).astype(BF16)


def attend_back_body(length, pairs, at, where, blocked, whole, weights, outs, sums):
    packed, grads = blocked
    rows, width = grads.shape[1:]
    part = outs[0].shape[2] // 3
    lanes = 2 * width // HEADS
    factor = (width // HEADS) ** (-0.5)
    low_lane = lax.broadcasted_iota(jnp.int32, (rows, lanes), 1) < lanes // 2
    full = length // 8 * 8
    there = lax.broadcasted_iota(jnp.int32, (rows - full, rows), 0) < length - full
    first = []
    for pair in pairs:
        start = pair * lanes
        cuts = [slice(at * width + start, at * width + start + lanes) for at in range(3)]
        query, keys, values = (packed[0, :, cut] for cut in cuts)
        grad = grads[0, :, start : start + lanes]
        scaled = query * jnp.asarray(factor, BF16)
        for side in range(2):
            mine = low_lane if side == 0 else jnp.logical_not(low_lane)
            scores = dot_nt(jnp.where(mine, keys, jnp.zeros_like(keys)), scaled)
            grad_probs = dot_nt(jnp.where(mine, values, jnp.zeros_like(values)), grad)
            first.append((query, keys, grad, scores, grad_probs))
    second = []
    for query, keys, grad, scores, grad_probs in first:
        scores = jnp.concatenate([scores[:full], jnp.where(there, scores[full:], -1e30)], 0)
        expo = jnp.exp(scores - jnp.max(scores, 0, keepdims=True))
        probs = expo * (1.0 / jnp.sum(expo, 0, keepdims=True))
        both = probs * grad_probs
        inner = jnp.sum(both, 0, keepdims=True)
        grad_scores = (both - probs * inner).astype(BF16)
        second.append((query, keys, grad, probs.astype(BF16), grad_scores))
    third = []
    for query, keys, grad, probs, grad_scores in second:
        third.append(
            (
                dot_tn(grad_scores, keys) * factor,
                dot(grad_scores, query) * factor,
                dot(probs, grad),
            )
        )
    for spot in range(len(pairs)):
        for kind in range(3):
            low = jnp.where(low_lane, third[2 * spot][kind], third[2 * spot + 1][kind])
            low = low.astype(BF16)
            cut = slice(kind * part + spot * lanes, kind * part + (spot + 1) * lanes)
            outs[0][0, :, cut] = low
            sums[0][:, cut] += column_sum(low)


def input_body(length, at, where, blocked, whole, weights, outs, sums):
    *packed, images, grad_middle = blocked
    width = images.shape[2]
    grad_one = None
    start = 0
    for array in packed:
        part = array.shape[2] // 3
        for kind in range(3):
            weight = weights[0][:, kind * width + start : kind * width + start + part]
            term = dot_nt(array[0, :, kind * part : (kind + 1) * part], weight)
            grad_one = term if grad_one is None else grad_one + term
        start += part
    hat, scale = normed(images[0].astype(F32))
    sums[0][...] += column_sum(grad_one * hat)
    sums[1][...] += column_sum(grad_one)
    result = grad_middle[0] + norm_back(grad_one, whole[0][...], hat, scale)
    outs[0][0] = result[:length]


def down_body(length, at, where, blocked, whole, weights, outs, sums):
    hidden, middle = blocked
    result = middle[0] + dot(hidden[0], weights[0][...]) + whole[0][...]
    live = jnp.where(at < where[1], 1.0, 0.0).astype(F32)
    outs[0][0] = (result * live)[:length].astype(BF16)


def on_device(
    sizes,
    images,
    counts,
    ln1_gain,
    ln1_shift,
    w_qkv,
    b_query,
    b_value,
    w_out,
    b_out,
    ln2_gain,
    ln2_shift,
    w_up,
    b_up,
    w_down,
    b_down,
    cotangent,
):
    slots, length, width = images.shape
    inner = w_up.shape[1]
    rows = -(-length // 16) * 16
    vectors = (ln1_gain, ln1_shift, b_query, b_value, b_out, ln2_gain, ln2_shift, b_down, b_up)
    g_qkv = Gather(w_qkv, sizes, 1)
    g_out = Gather(w_out, sizes, 0)
    g_up = Gather(w_up, sizes, 2)
    g_down = Gather(w_down, sizes, 0)
    if g_qkv.split:
        g_qkv.out, vectors = fence(g_qkv.out, vectors)
    g_qkv.far()
    g_qkv.near()
    place = jnp.stack(
        [
            lax.axis_index("group"),
            counts[0],
            lax.axis_index("replica") & 1,
            (lax.axis_index("replica") >> 1) & 1,
        ]
    ).astype(jnp.int32)
    widths = [vector.shape[0] for vector in vectors]
    unit = min(widths)
    at = jnp.arange(sum(widths) // unit)[:, None]
    line = jnp.zeros((sum(widths) // unit, unit), BF16)
    row = 0
    for vector in vectors:
        if vector.shape[0] == unit:
            line = jnp.where(at == row, vector[None, :], line)
        else:
            count = vector.shape[0] // unit
            fill = ((row, line.shape[0] - row - count), (0, 0))
            line = line + jnp.pad(vector.reshape(count, unit), fill)
        row += vector.shape[0] // unit
    if sizes[0] == 4:
        far_line = swap(line, "group", 4, 2)
        near_line = swap(line, "group", 4, 1)
        far_near = swap(far_line, "group", 4, 1)
        spots = []
        for at, size in enumerate(widths):
            out, column = (2, 2 * width) if at == 3 else (at - (at > 3), 0)
            spots.append((size // unit, out, column))
        small = unpack(place, (line, near_line, far_line, far_near), spots)
    else:
        gathered = lax.all_gather(line.reshape(-1), "group", axis=0, tiled=False)
        small = []
        start = 0
        for size in widths:
            small.append(gathered[:, start : start + size].reshape(1, -1).astype(F32))
            start += size
        small[2:4] = [jnp.concatenate([small[2], jnp.zeros_like(small[2]), small[3]], 1)]
    images, cotangent = prepare(place, images, cotangent, rows)
    tokens = slots * rows

    def outer(left, right):
        left = left.reshape(tokens, -1)
        right = right.reshape(tokens, -1)
        return dot_tn(left, right).astype(BF16)

    def chain(pairs, halvings, step):
        if sizes[0] > 1 and is_power(sizes[0]) and is_power(sizes[1]):
            return Reduce(outer_halves(place, pairs, sizes[0], step), sizes, halvings)
        return Reduce(jnp.concatenate([outer(*pair) for pair in pairs], 1), sizes, halvings)

    def hand_over(gather, name, carry):
        if gather.hops:
            part, carry = fence(getattr(gather, name), carry)
            setattr(gather, name, part)
        return carry

    if g_qkv.split:
        g_qkv.first, far_line, g_out.out, g_up.out = fence(
            g_qkv.first, far_line, g_out.out, g_up.out
        )
    g_qkv.across()
    g_up.far()
    if g_qkv.split:
        g_qkv.second, small, images, cotangent = fence(g_qkv.second, small, images, cotangent)
    g_qkv.last()
    g_out.far()
    gain_one, shift_one, bias_cat, bias_out, gain_two, shift_two, bias_down, bias_up = small
    images = hand_over(g_up, "first", images)
    g_up.across()
    low_one, packed = per_image(
        query_body, place, [images], [gain_one, shift_one, bias_cat], [g_qkv],
        [(rows, width, BF16), (rows, 3 * width, BF16)], [],
    )
    packed = hand_over(g_out, "first", packed)
    g_out.shard, g_up.shard, g_down.shard, g_down.out, packed = fence(
        g_out.shard, g_up.shard, g_down.shard, g_down.out, packed
    )
    g_out.across()
    g_down.far()
    g_out.near()
    g_up.near()
    g_down.near()
    (attended,) = per_image(
        functools.partial(attend_body, length), place, [packed], [], [],
        [(rows, width, BF16)], [],
    )
    if g_up.split:
        attended = hand_over(g_up, "second", attended)
    g_up.last()
    hidden, slope, middle, low_two = per_image(
        up_body, place, [attended, images], [bias_out, gain_two, shift_two, bias_up],
        [g_out, g_up],
        [(rows, inner, BF16), (rows, inner, BF16), (rows, width, F32), (rows, width, BF16)],
        [],
    )
    hidden = hand_over(g_down, "first", hidden)
    g_down.across()
    down, slope = fence(outer(hidden, cotangent), slope)
    down = Reduce(down, sizes, 2, True)
    grad_pre, grad_bup, grad_bdown = per_image(
        pre_body, place, [cotangent, slope], [], [g_down],
        [(rows, inner, BF16)], [inner, width],
    )
    up = chain([(low_two, grad_pre)], 2, inner // 4)
    grad_pre = turn([], [], grad_pre, [up])
    grad_middle, grad_branch, grad_att, grad_gain_two, grad_shift_two, grad_bout = per_image(
        back_body, place, [cotangent, grad_pre, middle], [gain_two], [g_up, g_out],
        [(rows, width, F32), (rows, width, BF16), (rows, width, BF16)],
        [width, width, width],
    )
    grad_att = turn([], [down], grad_att)
    half = HEADS // 4
    part = width // 2
    grad_one, sums_one = per_image(
        functools.partial(attend_back_body, length, range(half)), place, [packed, grad_att],
        [], [], [(rows, 3 * part, BF16)], [3 * part],
    )
    grad_one = turn([up, down], [up, down], grad_one)
    one = chain([(low_one, grad_one), (attended, grad_branch)], 2, part)
    grad_att = turn([up, down], [up, down], grad_att, [one])
    grad_two, sums_two = per_image(
        functools.partial(attend_back_body, length, range(half, 2 * half)), place,
        [packed, grad_att], [], [], [(rows, 3 * part, BF16)], [3 * part],
    )
    two = chain([(low_one, grad_two)], 1, part)
    grad_middle = turn([one, up, down], [one, up, down], grad_middle, [two])
    input_grad, grad_gain_one, grad_shift_one = per_image(
        functools.partial(input_body, length), place, [grad_one, grad_two, images, grad_middle],
        [gain_one], [g_qkv], [(length, width, F32)], [width, width],
    )
    parts = (
        grad_gain_one,
        grad_shift_one,
        sums_one[:, :part],
        sums_two[:, :part],
        sums_one[:, 2 * part :],
        sums_two[:, 2 * part :],
        grad_bout,
        grad_gain_two,
        grad_shift_two,
        grad_bdown,
        grad_bup,
    )
    little = Share(pack(parts), sizes)
    hidden = turn([two], [two], hidden)
    hidden = turn([up, one, down], [up, one, down], hidden, [little])
    outputs = None
    for span in ((0, slots // 2), (slots // 2, slots)):
        (outputs,) = per_image(
            functools.partial(down_body, length), place, [hidden, middle], [bias_down], [g_down],
            [(length, width, BF16)], [], span, outputs,
        )
        if span[0] == 0:
            outputs = turn([two, up, one, little], [two, up, one, little], outputs)
    outputs = turn([two], [two], outputs)
    outputs = turn([one, little], [one, little], outputs)
    outputs = turn([two], [two], outputs)
    outputs = turn([one, little], [one, little], outputs)
    for item in (two, one, up, little, down):
        item.drain()
    little = little.field.reshape(-1)
    sums = []
    start = 0
    for size in widths:
        mine = lax.axis_index("group") * size
        sums.append(lax.dynamic_slice(little, (start + mine,), (size,)))
        start += size * sizes[0]
    one, two = one.result(), two.result()
    grad_qkv = jnp.concatenate(
        [side[:, kind * part : (kind + 1) * part] for kind in range(3) for side in (one, two)], 1
    )
    big = [down.result(), up.result(), one[:, 3 * part :], grad_qkv]
    return (
        outputs,
        input_grad,
        sums[0],
        sums[1],
        big[3],
        sums[2],
        sums[3],
        big[2],
        sums[4],
        sums[5],
        sums[6],
        big[1],
        sums[8],
        big[0],
        sums[7],
    )


def solution(mesh):
    sizes = (mesh.shape["group"], mesh.shape["replica"])
    line = P("group")
    grid = P("group", None)
    field = P(("replica", "group"), None, None)
    return jax.shard_map(
        functools.partial(on_device, sizes),
        mesh=mesh,
        in_specs=(
            field, P(("replica", "group")), line, line, grid, line, line, grid, line, line, line,
            grid, line, grid, line, field,
        ),
        out_specs=(
            field, field, line, line, grid, line, line, grid, line, line, line, grid, line, grid,
            line,
        ),
        check_vma=False,
    )
```

```python
import functools

import jax
import jax.numpy as jnp
from jax import lax
from jax.experimental import pallas as pl
from jax.experimental.pallas import tpu as pltpu
from jax.sharding import PartitionSpec as P

HEADS = 12
GROUP = 6
F32 = jnp.float32
BF16 = jnp.bfloat16
GELU_A = 0.7978845608028654
GELU_B = 0.044715


def swap(field, axis, size, bit):
    return lax.ppermute(field, axis, [(at, at ^ bit) for at in range(size)])


def is_power(size):
    return size & (size - 1) == 0


def pick(field, at, axis):
    return lax.dynamic_index_in_dim(field, at, axis, keepdims=False)


def fence(*groups):
    return lax.optimization_barrier(groups)


class Gather:
    def __init__(self, shard, sizes, partner):
        self.groups, self.replicas = sizes
        self.shard = shard
        self.rows = shard.shape[0]
        self.hops = self.groups == 4 and self.rows % 32 == 0
        self.split = self.hops and partner and self.replicas % (2 * partner) == 0
        self.partner = partner
        if not self.hops:
            self.whole = lax.all_gather(shard, "group", axis=0, tiled=True)
        self.out = shard
        if self.split:
            half = (lax.axis_index("replica") // partner) & 1
            self.out = pick(shard.reshape(2, self.rows // 2, -1), half, 0)

    def near(self):
        if self.hops:
            self.beside = swap(self.shard, "group", 4, 1)

    def far(self):
        if self.hops:
            self.first = swap(self.out, "group", 4, 2)

    def across(self):
        if self.split:
            self.second = swap(self.first, "replica", self.replicas, self.partner)
        if self.hops:
            self.far_first = swap(self.first, "group", 4, 1)

    def last(self):
        if self.split:
            self.far_second = swap(self.second, "group", 4, 1)

    def pieces(self):
        if not self.hops:
            return (self.whole,)
        if not self.split:
            return (self.shard, self.beside, self.first, self.far_first)
        return (self.shard, self.beside, self.first, self.second, self.far_first, self.far_second)


def place_pieces(rows, pieces, me, half):
    if pieces == 1:
        return [0]
    if pieces == 4:
        return [(me ^ spot) * rows for spot in range(4)]
    part = rows // 2
    return [
        me * rows,
        (me ^ 1) * rows,
        (me ^ 2) * rows + half * part,
        (me ^ 2) * rows + (1 - half) * part,
        (me ^ 3) * rows + half * part,
        (me ^ 3) * rows + (1 - half) * part,
    ]


def add_low(left, right, kind):
    return (left.astype(F32) + right.astype(F32)).astype(kind)


class Share:
    def __init__(self, field, sizes):
        self.field = field
        self.flying = False
        self.hops = []
        if not (is_power(sizes[0]) and is_power(sizes[1])):
            self.field = lax.psum(field, ("replica", "group"))
            return
        for axis, size in zip(("group", "replica"), sizes):
            bit = 1
            while bit < size:
                self.hops.append((axis, size, bit))
                bit *= 2

    def outgoing(self):
        return self.field

    def launch(self, out):
        self.field = out
        self.came = swap(out, *self.hops.pop(0))
        self.flying = True

    def land(self, came):
        self.field = self.field + came
        self.flying = False

    def drain(self):
        while self.flying or self.hops:
            if not self.flying:
                self.launch(self.outgoing())
            self.land(self.came)


class Reduce:
    def __init__(self, grad, sizes, halvings, scatter=False):
        self.sizes = sizes
        self.ready = None
        self.kind = BF16
        groups, replicas = sizes
        self.hops = []
        self.flying = False
        if not (is_power(groups) and is_power(replicas)):
            shard = lax.psum_scatter(grad, "group", scatter_dimension=0, tiled=True)
            self.terms = [lax.psum(shard.astype(F32), "replica")]
            return
        if scatter:
            self.terms = [lax.psum_scatter(grad, "group", scatter_dimension=0, tiled=True)]
        else:
            self.ready = grad
            bit = 1
            while bit < groups:
                self.hops.append(("group", bit, "split"))
                bit *= 2
        bit = 1
        back = []
        while bit < replicas:
            if len(back) < halvings:
                self.hops.append(("replica", bit, "halve"))
                back.append(("replica", bit, "back"))
            else:
                self.hops.append(("replica", bit, "whole"))
            bit *= 2
        self.hops += reversed(back)

    def total(self, parts=None, kind=None):
        parts = self.terms if parts is None else parts
        if len(parts) == 1:
            return parts[0].astype(kind or self.kind)
        return sum(part.astype(F32) for part in parts).astype(kind or self.kind)

    def outgoing(self):
        if self.ready:
            out, keep = self.ready
            self.ready, self.keep = None, [keep]
            return out
        axis, bit, kind = self.hops[0]
        side = (lax.axis_index(axis) // bit) & 1
        if kind == "split":
            shape = self.terms[0].shape
            pairs = [term.reshape((shape[0] // 2, 2) + shape[1:]) for term in self.terms]
            self.keep = [pick(term, side, 1) for term in pairs]
            if shape[0] == 2:
                self.keep = [term[0] for term in self.keep]
            return self.total([pick(term, 1 - side, 1) for term in pairs])
        if kind == "halve":
            shape = self.terms[0].shape
            pairs = [term.reshape((2, shape[0] // 2) + shape[1:]) for term in self.terms]
            self.keep = [pick(term, side, 0) for term in pairs]
            return self.total([pick(term, 1 - side, 0) for term in pairs])
        return self.total()

    def launch(self, out):
        axis, bit, kind = self.hops.pop(0)
        size = self.sizes[0] if axis == "group" else self.sizes[1]
        self.came = swap(out, axis, size, bit)
        side = (lax.axis_index(axis) // bit) & 1
        if kind in ("split", "halve"):
            self.held = self.total(self.keep)
            if kind == "split" and out.shape[0] == 1 and self.held.ndim == out.ndim:
                self.held = self.held[0]
        else:
            self.held = out
        self.kind_of_hop, self.side = kind, side
        self.flying = True

    def land(self, came):
        self.flying = False
        if self.kind_of_hop == "back":
            held = self.held
            self.terms = [
                jnp.where(
                    self.side == 0,
                    jnp.concatenate([held, came]),
                    jnp.concatenate([came, held]),
                )
            ]
            return
        if self.kind_of_hop == "split" and self.held.ndim < came.ndim:
            came = came[0]
        self.terms = [self.held, came]

    def drain(self):
        while self.flying or self.hops:
            if not self.flying:
                self.launch(self.outgoing())
            self.land(self.came)

    def result(self):
        return self.total(kind=F32)


def turn(landing, launching, carry, quick=()):
    landing = [chain for chain in landing if chain.flying]
    came, carry = fence([chain.came for chain in landing], carry)
    for chain, part in zip(landing, came):
        chain.land(part)
    for chain in quick:
        out, carry = fence(chain.outgoing(), carry)
        chain.launch(out)
    launching = [chain for chain in launching if chain.hops]
    outs, carry = fence([chain.outgoing() for chain in launching], carry)
    for chain, out in zip(launching, outs):
        chain.launch(out)
    for chain in quick:
        came, outs, carry = fence(chain.came, outs, carry)
        chain.land(came)
        out, carry = fence(chain.outgoing(), carry)
        chain.launch(out)
    return carry


def dot(left, right):
    return lax.dot_general(left, right, (((1,), (0,)), ((), ())), preferred_element_type=F32)


def dot_nt(left, right):
    return lax.dot_general(left, right, (((1,), (1,)), ((), ())), preferred_element_type=F32)


def dot_tn(left, right):
    return lax.dot_general(left, right, (((0,), (0,)), ((), ())), preferred_element_type=F32)


def per_image(body, place, blocked, whole, weights, outs, sums, span=None, into=None):
    slots = blocked[0].shape[0]
    first, last = span or (0, slots)
    halves = [1 + (gather.partner or 1) for gather in weights]
    weights = [gather.pieces() for gather in weights]
    counts = [len(pieces) for pieces in weights]
    rows_of = [pieces[0].shape[0] for pieces in weights]
    total = [rows * (4 if len(pieces) > 1 else 1) for rows, pieces in zip(rows_of, weights)]

    def kernel(*refs):
        refs = list(refs)

        def take(count):
            taken = refs[:count]
            del refs[:count]
            return taken

        (where,) = take(1)
        blocked_refs = take(len(blocked))
        whole_refs = take(len(whole))
        piece_refs = [take(count) for count in counts]
        take(0 if into is None else 1)
        out_refs = take(len(outs))
        sum_refs = take(len(sums))
        weight_refs = take(len(weights))
        at = pl.program_id(0)

        @pl.when(at == 0)
        def _():
            copies = []
            for index, pieces in enumerate(piece_refs):
                starts = place_pieces(rows_of[index], len(pieces), where[0], where[halves[index]])
                for spot, (piece, start) in enumerate(zip(pieces, starts)):
                    target = weight_refs[index].at[pl.ds(pl.multiple_of(start, 16), piece.shape[0])]
                    copies.append(pltpu.make_async_copy(piece, target, refs[0].at[index, spot]))
            for copy in copies:
                copy.start()
            for ref in sum_refs:
                ref[...] = jnp.zeros_like(ref)
            for copy in copies:
                copy.wait()

        body(at + first, where, blocked_refs, whole_refs, weight_refs, out_refs, sum_refs)

    in_specs = [pl.BlockSpec(memory_space=pltpu.SMEM)]
    for array in blocked:
        in_specs.append(pl.BlockSpec((1,) + array.shape[1:], lambda i: (i + first, 0, 0)))
    for array in whole:
        in_specs.append(pl.BlockSpec(array.shape, lambda i: (0, 0)))
    pieces = [piece for parts in weights for piece in parts]
    extra = [] if into is None else [into]
    in_specs += [pl.BlockSpec(memory_space=pl.ANY)] * (len(pieces) + len(extra))
    out_specs = [
        pl.BlockSpec((1, rows, columns), lambda i: (i + first, 0, 0)) for rows, columns, _ in outs
    ]
    out_specs += [pl.BlockSpec((1, columns), lambda i: (0, 0)) for columns in sums]
    shapes = [jax.ShapeDtypeStruct((slots, rows, columns), kind) for rows, columns, kind in outs]
    shapes += [jax.ShapeDtypeStruct((1, columns), F32) for columns in sums]
    scratch = [
        pltpu.VMEM((rows, parts[0].shape[1]), BF16) for rows, parts in zip(total, weights)
    ]
    if weights:
        scratch.append(pltpu.SemaphoreType.DMA((len(weights), 6)))
    return pl.pallas_call(
        kernel,
        grid=(last - first,),
        in_specs=in_specs,
        out_specs=out_specs,
        input_output_aliases={len(in_specs) - 1: 0} if extra else {},
        out_shape=shapes,
        scratch_shapes=scratch,
        compiler_params=pltpu.CompilerParams(
            dimension_semantics=("arbitrary",), vmem_limit_bytes=58 * 2**20
        ),
        cost_estimate=pl.CostEstimate(flops=2000000000, bytes_accessed=1, transcendentals=0),
    )(place, *blocked, *whole, *pieces, *extra)


def normed(field):
    centred = field - jnp.mean(field, -1, keepdims=True)
    scale = lax.rsqrt(jnp.mean(centred * centred, -1, keepdims=True) + 1e-06)
    return centred * scale, scale


def norm_back(grad, gain, hat, scale):
    inner = grad * gain
    mean = jnp.mean(inner, -1, keepdims=True)
    along = jnp.mean(inner * hat, -1, keepdims=True)
    return scale * (inner - mean - hat * along)


def column_sum(field):
    return jnp.sum(field.astype(F32), 0, keepdims=True)


def outer_halves(place, pairs, groups, step):
    slots, rows, width = pairs[0][0].shape
    tokens = slots * rows
    share = width // groups
    columns = sum(right.shape[2] for _, right in pairs)
    bounds = [0]
    for _, right in pairs:
        bounds.append(bounds[-1] + right.shape[2] // step)

    def kernel(where, *refs):
        lefts, rights = refs[: len(pairs)], refs[len(pairs) : 2 * len(pairs)]
        send_ref, keep_ref, total = refs[2 * len(pairs) :]
        at = pl.program_id(0)
        for left, right, first, last in zip(lefts, rights, bounds, bounds[1:]):

            @pl.when((at >= first) & (at < last))
            def _(left=left, right=right):
                total[...] = dot_tn(left[...], right[...]).astype(BF16)

        side = where[0] & 1
        for spot in range(groups // 2):
            for ref, mine in ((send_ref, 1 - side), (keep_ref, side)):
                start = pl.multiple_of((2 * spot + mine) * share, 16)
                ref[spot] = total[pl.ds(start, share), :]

    def column_map(first, last):
        return lambda i: (0, jnp.clip(i - first, 0, last - first - 1))

    shape = jax.ShapeDtypeStruct((groups // 2, share, columns), BF16)
    return pl.pallas_call(
        kernel,
        grid=(bounds[-1],),
        in_specs=[pl.BlockSpec(memory_space=pltpu.SMEM)]
        + [pl.BlockSpec((tokens, width), lambda i: (0, 0))] * len(pairs)
        + [
            pl.BlockSpec((tokens, step), column_map(first, last))
            for first, last in zip(bounds, bounds[1:])
        ],
        out_specs=[pl.BlockSpec((groups // 2, share, step), lambda i: (0, 0, i))] * 2,
        out_shape=[shape, shape],
        scratch_shapes=[pltpu.VMEM((width, step), BF16)],
        compiler_params=pltpu.CompilerParams(
            dimension_semantics=("arbitrary",), vmem_limit_bytes=58 * 2**20
        ),
        cost_estimate=pl.CostEstimate(flops=1, bytes_accessed=1, transcendentals=0),
    )(
        place,
        *[left.reshape(tokens, width) for left, _ in pairs],
        *[right.reshape(tokens, -1) for _, right in pairs],
    )


def prepare(place, images, cotangent, rows):
    slots, length, width = images.shape

    def kernel(where, images_ref, cotangent_ref, images_out, cotangent_out):
        live = jnp.where(pl.program_id(0) < where[1], 1.0, 0.0).astype(BF16)
        empty = jnp.zeros((rows - length // 16 * 16, width), BF16)
        for ref, scale, out in (
            (images_ref, None, images_out),
            (cotangent_ref, live, cotangent_out),
        ):
            out[0, length // 16 * 16 :, :] = empty
            value = ref[0] if scale is None else ref[0] * scale
            out[0, :length, :] = value

    shape = jax.ShapeDtypeStruct((slots, rows, width), BF16)
    block = pl.BlockSpec((1, length, width), lambda i: (i, 0, 0))
    padded = pl.BlockSpec((1, rows, width), lambda i: (i, 0, 0))
    return pl.pallas_call(
        kernel,
        grid=(slots,),
        in_specs=[pl.BlockSpec(memory_space=pltpu.SMEM), block, block],
        out_specs=[padded, padded],
        out_shape=[shape, shape],
        compiler_params=pltpu.CompilerParams(dimension_semantics=("arbitrary",)),
        cost_estimate=pl.CostEstimate(flops=1, bytes_accessed=16 * 2**20, transcendentals=0),
    )(place, images, cotangent)


def pack(parts):
    total = sum(part.shape[1] for part in parts) // 128

    def kernel(*refs):
        at = 0
        for ref in refs[:-1]:
            for start in range(0, ref.shape[1], 128):
                refs[-1][at : at + 1, :] = ref[:, start : start + 128]
                at += 1

    return pl.pallas_call(
        kernel,
        in_specs=[pl.BlockSpec(memory_space=pltpu.VMEM)] * len(parts),
        out_specs=pl.BlockSpec(memory_space=pltpu.VMEM),
        out_shape=jax.ShapeDtypeStruct((total, 128), F32),
        cost_estimate=pl.CostEstimate(flops=1, bytes_accessed=1, transcendentals=0),
    )(*parts)


def unpack(place, lines, spots):
    count, unit = lines[0].shape
    sizes = {}
    for rows, out, column in spots:
        sizes[out] = max(sizes.get(out, 0), column + 4 * rows * unit)

    def kernel(where, *refs):
        outs = refs[4:]
        parts = [ref[...].astype(F32) for ref in refs[:4]]
        for ref in outs:
            ref[...] = jnp.zeros_like(ref)
        for owner in range(4):
            mine = jnp.zeros((count, unit), F32)
            for spot, part in enumerate(parts):
                mine = jnp.where((where[0] ^ spot) == owner, part, mine)
            row = 0
            for rows, out, column in spots:
                for at in range(rows):
                    start = column + (owner * rows + at) * unit
                    outs[out][:, start : start + unit] = mine[row : row + 1]
                    row += 1

    return pl.pallas_call(
        kernel,
        in_specs=[pl.BlockSpec(memory_space=pltpu.SMEM)]
        + [pl.BlockSpec(memory_space=pltpu.VMEM)] * 4,
        out_specs=[pl.BlockSpec(memory_space=pltpu.VMEM)] * len(sizes),
        out_shape=[jax.ShapeDtypeStruct((1, sizes[at]), F32) for at in range(len(sizes))],
        cost_estimate=pl.CostEstimate(flops=1, bytes_accessed=6 * 2**20, transcendentals=0),
    )(place, *lines)


def query_body(at, where, blocked, whole, weights, outs, sums):
    gain, shift, bias = whole
    hat, _ = normed(blocked[0][0].astype(F32))
    low = (hat * gain[...] + shift[...]).astype(BF16)
    outs[0][0] = low
    width = low.shape[1]
    for part in range(3):
        cut = slice(part * width, (part + 1) * width)
        outs[1][0, :, cut] = (dot(low, weights[0][:, cut]) + bias[:, cut]).astype(BF16)


def attend_body(length, at, where, blocked, whole, weights, outs, sums):
    (packed,) = blocked
    rows = packed.shape[1]
    width = packed.shape[2] // 3
    lanes = 2 * width // HEADS
    factor = (width // HEADS) ** (-0.5)
    low_lane = lax.broadcasted_iota(jnp.int32, (rows, lanes), 1) < lanes // 2
    key_there = lax.broadcasted_iota(jnp.int32, (rows, rows), 1) < length
    for group in range(0, HEADS // 2, GROUP):
        first = []
        for pair in range(group, group + GROUP):
            start = pair * lanes
            query = packed[0, :, start : start + lanes] * jnp.asarray(factor, BF16)
            keys = packed[0, :, width + start : width + start + lanes]
            values = packed[0, :, 2 * width + start : 2 * width + start + lanes]
            for side in range(2):
                mine = low_lane if side == 0 else jnp.logical_not(low_lane)
                first.append((dot_nt(jnp.where(mine, query, jnp.zeros_like(query)), keys), values))
        second = []
        for scores, values in first:
            scores = jnp.where(key_there, scores, -1e30)
            expo = jnp.exp(scores - jnp.max(scores, -1, keepdims=True))
            probs = expo * (1.0 / jnp.sum(expo, -1, keepdims=True))
            second.append((probs.astype(BF16), values))
        third = [dot(probs, values) for probs, values in second]
        for spot in range(GROUP):
            start = (group + spot) * lanes
            both = jnp.where(low_lane, third[2 * spot], third[2 * spot + 1])
            outs[0][0, :, start : start + lanes] = both.astype(BF16)


def up_body(at, where, blocked, whole, weights, outs, sums):
    attended, images = blocked
    bias_out, gain, shift, bias_up = whole
    w_out, w_up = weights
    middle = images[0].astype(F32) + dot(attended[0], w_out[...]) + bias_out[...]
    outs[2][0] = middle
    hat, _ = normed(middle)
    low = (hat * gain[...] + shift[...]).astype(BF16)
    outs[3][0] = low
    inner = w_up.shape[1]
    width = low.shape[1]
    for start in range(0, inner, width):
        cut = slice(start, start + width)
        pre = dot(low, w_up[:, cut]) + bias_up[:, cut]
        square = pre * pre
        bend = jnp.tanh(pre * (GELU_A + (GELU_A * GELU_B) * square))
        half = 0.5 + 0.5 * bend
        outs[0][0, :, cut] = (pre * half).astype(BF16)
        slope = GELU_A + (3.0 * GELU_A * GELU_B) * square
        outs[1][0, :, cut] = (half + (0.5 * pre) * ((1.0 - bend * bend) * slope)).astype(BF16)


def pre_body(at, where, blocked, whole, weights, outs, sums):
    cotangent, slope = blocked
    grad_low = cotangent[0]
    width = grad_low.shape[1]
    for start in range(0, slope.shape[2], width):
        cut = slice(start, start + width)
        grad_pre = dot_nt(grad_low, weights[0][cut, :]) * slope[0, :, cut].astype(F32)
        low = grad_pre.astype(BF16)
        outs[0][0, :, cut] = low
        sums[0][:, cut] += column_sum(low)
    sums[1][...] += column_sum(grad_low)


def back_body(at, where, blocked, whole, weights, outs, sums):
    cotangent, grad_pre, middle = blocked
    (gain,) = whole
    w_up, w_out = weights
    grad_two = dot_nt(grad_pre[0], w_up[...])
    hat, scale = normed(middle[0])
    sums[0][...] += column_sum(grad_two * hat)
    sums[1][...] += column_sum(grad_two)
    grad_middle = cotangent[0].astype(F32) + norm_back(grad_two, gain[...], hat, scale)
    outs[0][0] = grad_middle
    low = grad_middle.astype(BF16)
    outs[1][0] = low
    sums[2][...] += column_sum(low)
    outs[2][0] = dot_nt(low, w_out[...]).astype(BF16)


def attend_back_body(length, pairs, at, where, blocked, whole, weights, outs, sums):
    packed, grads = blocked
    rows, width = grads.shape[1:]
    part = outs[0].shape[2] // 3
    lanes = 2 * width // HEADS
    factor = (width // HEADS) ** (-0.5)
    low_lane = lax.broadcasted_iota(jnp.int32, (rows, lanes), 1) < lanes // 2
    full = length // 8 * 8
    there = lax.broadcasted_iota(jnp.int32, (rows - full, rows), 0) < length - full
    first = []
    for pair in pairs:
        start = pair * lanes
        cuts = [slice(at * width + start, at * width + start + lanes) for at in range(3)]
        query, keys, values = (packed[0, :, cut] for cut in cuts)
        grad = grads[0, :, start : start + lanes]
        scaled = query * jnp.asarray(factor, BF16)
        for side in range(2):
            mine = low_lane if side == 0 else jnp.logical_not(low_lane)
            scores = dot_nt(jnp.where(mine, keys, jnp.zeros_like(keys)), scaled)
            grad_probs = dot_nt(jnp.where(mine, values, jnp.zeros_like(values)), grad)
            first.append((query, keys, grad, scores, grad_probs))
    second = []
    for query, keys, grad, scores, grad_probs in first:
        scores = jnp.concatenate([scores[:full], jnp.where(there, scores[full:], -1e30)], 0)
        expo = jnp.exp(scores - jnp.max(scores, 0, keepdims=True))
        probs = expo * (1.0 / jnp.sum(expo, 0, keepdims=True))
        both = probs * grad_probs
        inner = jnp.sum(both, 0, keepdims=True)
        grad_scores = (both - probs * inner).astype(BF16)
        second.append((query, keys, grad, probs.astype(BF16), grad_scores))
    third = []
    for query, keys, grad, probs, grad_scores in second:
        third.append(
            (
                dot_tn(grad_scores, keys) * factor,
                dot(grad_scores, query) * factor,
                dot(probs, grad),
            )
        )
    for spot in range(len(pairs)):
        for kind in range(3):
            low = jnp.where(low_lane, third[2 * spot][kind], third[2 * spot + 1][kind])
            low = low.astype(BF16)
            cut = slice(kind * part + spot * lanes, kind * part + (spot + 1) * lanes)
            outs[0][0, :, cut] = low
            sums[0][:, cut] += column_sum(low)


def input_body(length, at, where, blocked, whole, weights, outs, sums):
    *packed, images, grad_middle = blocked
    width = images.shape[2]
    grad_one = None
    start = 0
    for array in packed:
        part = array.shape[2] // 3
        for kind in range(3):
            weight = weights[0][:, kind * width + start : kind * width + start + part]
            term = dot_nt(array[0, :, kind * part : (kind + 1) * part], weight)
            grad_one = term if grad_one is None else grad_one + term
        start += part
    hat, scale = normed(images[0].astype(F32))
    sums[0][...] += column_sum(grad_one * hat)
    sums[1][...] += column_sum(grad_one)
    result = grad_middle[0] + norm_back(grad_one, whole[0][...], hat, scale)
    outs[0][0] = result[:length]


def down_body(length, at, where, blocked, whole, weights, outs, sums):
    hidden, middle = blocked
    result = middle[0] + dot(hidden[0], weights[0][...]) + whole[0][...]
    live = jnp.where(at < where[1], 1.0, 0.0).astype(F32)
    outs[0][0] = (result * live)[:length].astype(BF16)


def on_device(
    sizes,
    images,
    counts,
    ln1_gain,
    ln1_shift,
    w_qkv,
    b_query,
    b_value,
    w_out,
    b_out,
    ln2_gain,
    ln2_shift,
    w_up,
    b_up,
    w_down,
    b_down,
    cotangent,
):
    slots, length, width = images.shape
    inner = w_up.shape[1]
    rows = -(-length // 16) * 16
    vectors = (ln1_gain, ln1_shift, b_query, b_value, b_out, ln2_gain, ln2_shift, b_down, b_up)
    g_qkv = Gather(w_qkv, sizes, 1)
    g_out = Gather(w_out, sizes, 0)
    g_up = Gather(w_up, sizes, 2)
    g_down = Gather(w_down, sizes, 0)
    if g_qkv.split:
        g_qkv.out, vectors = fence(g_qkv.out, vectors)
    g_qkv.far()
    g_qkv.near()
    place = jnp.stack(
        [
            lax.axis_index("group"),
            counts[0],
            lax.axis_index("replica") & 1,
            (lax.axis_index("replica") >> 1) & 1,
        ]
    ).astype(jnp.int32)
    widths = [vector.shape[0] for vector in vectors]
    unit = min(widths)
    at = jnp.arange(sum(widths) // unit)[:, None]
    line = jnp.zeros((sum(widths) // unit, unit), BF16)
    row = 0
    for vector in vectors:
        if vector.shape[0] == unit:
            line = jnp.where(at == row, vector[None, :], line)
        else:
            count = vector.shape[0] // unit
            fill = ((row, line.shape[0] - row - count), (0, 0))
            line = line + jnp.pad(vector.reshape(count, unit), fill)
        row += vector.shape[0] // unit
    if sizes[0] == 4:
        far_line = swap(line, "group", 4, 2)
        near_line = swap(line, "group", 4, 1)
        far_near = swap(far_line, "group", 4, 1)
        spots = []
        for at, size in enumerate(widths):
            out, column = (2, 2 * width) if at == 3 else (at - (at > 3), 0)
            spots.append((size // unit, out, column))
        small = unpack(place, (line, near_line, far_line, far_near), spots)
    else:
        gathered = lax.all_gather(line.reshape(-1), "group", axis=0, tiled=False)
        small = []
        start = 0
        for size in widths:
            small.append(gathered[:, start : start + size].reshape(1, -1).astype(F32))
            start += size
        small[2:4] = [jnp.concatenate([small[2], jnp.zeros_like(small[2]), small[3]], 1)]
    images, cotangent = prepare(place, images, cotangent, rows)
    tokens = slots * rows

    def outer(left, right):
        left = left.reshape(tokens, -1)
        right = right.reshape(tokens, -1)
        return dot_tn(left, right).astype(BF16)

    def chain(pairs, halvings, step):
        if sizes[0] > 1 and is_power(sizes[0]) and is_power(sizes[1]):
            return Reduce(outer_halves(place, pairs, sizes[0], step), sizes, halvings)
        return Reduce(jnp.concatenate([outer(*pair) for pair in pairs], 1), sizes, halvings)

    def hand_over(gather, name, carry):
        if gather.hops:
            part, carry = fence(getattr(gather, name), carry)
            setattr(gather, name, part)
        return carry

    if g_qkv.split:
        g_qkv.first, far_line, g_out.out, g_up.out = fence(
            g_qkv.first, far_line, g_out.out, g_up.out
        )
    g_qkv.across()
    g_up.far()
    if g_qkv.split:
        g_qkv.second, small, images, cotangent = fence(g_qkv.second, small, images, cotangent)
    g_qkv.last()
    g_out.far()
    gain_one, shift_one, bias_cat, bias_out, gain_two, shift_two, bias_down, bias_up = small
    images = hand_over(g_up, "first", images)
    g_up.across()
    low_one, packed = per_image(
        query_body, place, [images], [gain_one, shift_one, bias_cat], [g_qkv],
        [(rows, width, BF16), (rows, 3 * width, BF16)], [],
    )
    packed = hand_over(g_out, "first", packed)
    g_out.shard, g_up.shard, g_down.shard, g_down.out, packed = fence(
        g_out.shard, g_up.shard, g_down.shard, g_down.out, packed
    )
    g_out.across()
    g_down.far()
    g_out.near()
    g_up.near()
    g_down.near()
    (attended,) = per_image(
        functools.partial(attend_body, length), place, [packed], [], [],
        [(rows, width, BF16)], [],
    )
    if g_up.split:
        attended = hand_over(g_up, "second", attended)
    g_up.last()
    hidden, slope, middle, low_two = per_image(
        up_body, place, [attended, images], [bias_out, gain_two, shift_two, bias_up],
        [g_out, g_up],
        [(rows, inner, BF16), (rows, inner, BF16), (rows, width, F32), (rows, width, BF16)],
        [],
    )
    hidden = hand_over(g_down, "first", hidden)
    g_down.across()
    down, slope = fence(outer(hidden, cotangent), slope)
    down = Reduce(down, sizes, 2, True)
    grad_pre, grad_bup, grad_bdown = per_image(
        pre_body, place, [cotangent, slope], [], [g_down],
        [(rows, inner, BF16)], [inner, width],
    )
    up = chain([(low_two, grad_pre)], 2, inner // 4)
    grad_pre = turn([], [], grad_pre, [up])
    grad_middle, grad_branch, grad_att, grad_gain_two, grad_shift_two, grad_bout = per_image(
        back_body, place, [cotangent, grad_pre, middle], [gain_two], [g_up, g_out],
        [(rows, width, F32), (rows, width, BF16), (rows, width, BF16)],
        [width, width, width],
    )
    grad_att = turn([], [down], grad_att)
    half = HEADS // 4
    part = width // 2
    grad_one, sums_one = per_image(
        functools.partial(attend_back_body, length, range(half)), place, [packed, grad_att],
        [], [], [(rows, 3 * part, BF16)], [3 * part],
    )
    grad_one = turn([up, down], [up, down], grad_one)
    one = chain([(low_one, grad_one), (attended, grad_branch)], 2, part)
    grad_att = turn([up, down], [up, down], grad_att, [one])
    grad_two, sums_two = per_image(
        functools.partial(attend_back_body, length, range(half, 2 * half)), place,
        [packed, grad_att], [], [], [(rows, 3 * part, BF16)], [3 * part],
    )
    two = chain([(low_one, grad_two)], 1, part)
    grad_middle = turn([one, up, down], [one, up, down], grad_middle, [two])
    input_grad, grad_gain_one, grad_shift_one = per_image(
        functools.partial(input_body, length), place, [grad_one, grad_two, images, grad_middle],
        [gain_one], [g_qkv], [(length, width, F32)], [width, width],
    )
    parts = (
        grad_gain_one,
        grad_shift_one,
        sums_one[:, :part],
        sums_two[:, :part],
        sums_one[:, 2 * part :],
        sums_two[:, 2 * part :],
        grad_bout,
        grad_gain_two,
        grad_shift_two,
        grad_bdown,
        grad_bup,
    )
    little = Share(pack(parts), sizes)
    hidden = turn([two], [two], hidden)
    hidden = turn([up, one, down], [up, one, down], hidden, [little])
    outputs = None
    for span in ((0, slots // 2), (slots // 2, slots)):
        (outputs,) = per_image(
            functools.partial(down_body, length), place, [hidden, middle], [bias_down], [g_down],
            [(length, width, BF16)], [], span, outputs,
        )
        if span[0] == 0:
            outputs = turn([two, up, one, little], [two, up, one, little], outputs)
    outputs = turn([two], [two], outputs)
    outputs = turn([one, little], [one, little], outputs)
    outputs = turn([two], [two], outputs)
    outputs = turn([one, little], [one, little], outputs)
    for item in (two, one, up, little, down):
        item.drain()
    little = little.field.reshape(-1)
    sums = []
    start = 0
    for size in widths:
        mine = lax.axis_index("group") * size
        sums.append(lax.dynamic_slice(little, (start + mine,), (size,)))
        start += size * sizes[0]
    one, two = one.result(), two.result()
    grad_qkv = jnp.concatenate(
        [side[:, kind * part : (kind + 1) * part] for kind in range(3) for side in (one, two)], 1
    )
    big = [down.result(), up.result(), one[:, 3 * part :], grad_qkv]
    return (
        outputs,
        input_grad,
        sums[0],
        sums[1],
        big[3],
        sums[2],
        sums[3],
        big[2],
        sums[4],
        sums[5],
        sums[6],
        big[1],
        sums[8],
        big[0],
        sums[7],
    )


def solution(mesh):
    sizes = (mesh.shape["group"], mesh.shape["replica"])
    line = P("group")
    grid = P("group", None)
    field = P(("replica", "group"), None, None)
    return jax.shard_map(
        functools.partial(on_device, sizes),
        mesh=mesh,
        in_specs=(
            field, P(("replica", "group")), line, line, grid, line, line, grid, line, line, line,
            grid, line, grid, line, field,
        ),
        out_specs=(
            field, field, line, line, grid, line, line, grid, line, line, line, grid, line, grid,
            line,
        ),
        check_vma=False,
    )
```
